32 devices in a mesh: dp: 4 (over y, x), shard: 8 (over z, core).
Axes of the slice: x: 2, y: 2, z: 4, core: 2. Of those that a mesh axis runs over, the one named last changes fastest.
Arguments:
- grads: bfloat16 [4, 8, 1024, 1024], P('dp', 'shard'), may hold values from -6 to 6
- left_roots: bfloat16 [8, 1024, 1024], P('shard'), as said below
- right_roots: bfloat16 [8, 1024, 1024], P('shard'), as said below
- rows_valid: int32 [8], P('shard'), may hold values from 256 to 1024, as said below
- cols_valid: int32 [8], P('shard'), may hold values from 256 to 1024, as said below
Outputs:
- update: bfloat16 [8, 1024, 1024], P('shard', 'dp')
The draws below stay inside these ranges and needn't reach their ends.
Inputs may be any that keep to these rules, and one draw needn't show every extreme that they name: `left_roots`: each entry is symmetric, with a diagonal between 0.5 and 2. `right_roots`: each entry is symmetric, with a diagonal between 0.5 and 2. A multiple of 256; no block has both rows_valid and cols_valid below 1024. A multiple of 256; no block has both rows_valid and cols_valid below 1024.
All inputs are finite; a program needn't handle non-finite values.
Results may differ from the reference program's by a relative error of at most 0.024.
Values may be sent and summed in bfloat16 or wider, within the bound.
No kernel may reach another device: no remote copies, remote signals or barrier semaphores. Data moves between devices by JAX's collectives and lax.ppermute only.
A program may use at most 64 MiB of HBM per device.

```python
import jax
import jax.numpy as jnp
from jax import lax

B = 1024
NB = 8
N_DP = 4


def symmetric_root(key):
    first, second = jax.random.split(key)
    diag_vals = jnp.exp(jax.random.uniform(first, (NB, B), jnp.float32, jnp.log(0.5), jnp.log(2.0)))
    noise = jax.random.normal(second, (NB, B, B), jnp.float32) * (0.7 / jnp.sqrt(float(B)))
    sym = (noise + jnp.swapaxes(noise, 1, 2)) * 0.7071067811865476
    identity = jnp.eye(B, dtype=jnp.float32)
    return (sym * (1.0 - identity) + diag_vals[:, :, None] * identity).astype(jnp.bfloat16)


def edge_kinds(key):
    kind_key, amount_key = jax.random.split(key)
    kinds = jax.random.randint(kind_key, (NB,), 0, 4).astype(jnp.int32)
    place = jnp.arange(NB, dtype=jnp.int32)
    kinds = jnp.where(place == 0, 0, kinds)
    kinds = jnp.where(place == 1, 1, kinds)
    kinds = jnp.where(place == 2, 2, kinds)
    quarters = jax.random.randint(amount_key, (NB,), 1, 4).astype(jnp.int32)
    quarters = jnp.where(place == 0, 1, quarters)
    quarters = jnp.where(place == 2, 1, quarters)
    amounts = (quarters * (B // 4)).astype(jnp.int32)
    return (kinds.astype(jnp.int32), amounts)


def draw_left_roots(key, part):
    key = jax.random.fold_in(key, 11)
    return symmetric_root(key)


def draw_right_roots(key, part):
    key = jax.random.fold_in(key, 23)
    return symmetric_root(key)


def draw_rows_valid(key, part):
    kinds, amounts = edge_kinds(key)
    return jnp.where(kinds == 0, amounts, B).astype(jnp.int32)


def draw_cols_valid(key, part):
    kinds, amounts = edge_kinds(key)
    partial_cols = (kinds == 1) | (kinds == 2)
    return jnp.where(partial_cols, amounts, B).astype(jnp.int32)


def spiked(values, stream_key, source, target, blocks, factor):
    def block_of(position):
        return (jnp.arange(values.shape[position]) // (values.shape[position] // blocks)).reshape((-1,) + (1,) * (values.ndim - 1 - position))

    one_side = jax.random.permutation(stream_key, blocks)[block_of(target)]
    other_side = (block_of(target) + blocks // 2) % blocks
    return jnp.where((block_of(source) == one_side) | (block_of(source) == other_side), factor * values, values)


def block_scale(rng, dims, cuts, least, largest):
    loudness = 1.0
    for position, shards_of in cuts:
        draws = jax.random.uniform(jax.random.fold_in(jax.random.fold_in(rng, 6), position), (shards_of,), jnp.float32, least / len(cuts), largest / len(cuts))
        loudness = loudness * jnp.repeat(jnp.exp(draws), dims[position] // shards_of).reshape((-1,) + (1,) * (len(dims) - 1 - position))
    return loudness


def heavy_noise(stream_key, dims, scale, bound, shards, heavy, held_as=jnp.bfloat16):
    result = scale * jax.random.normal(stream_key, dims, jnp.float32)
    if shards:
        result = result * block_scale(stream_key, dims, shards, -0.22, 0.18)
    return jnp.clip(spiked(result, jax.random.fold_in(stream_key, 3), *heavy), -bound, bound).astype(held_as)


def setup_inputs(seed: int = 0) -> dict:
    keys = jax.random.split(jax.random.key(seed), 6)
    grads = heavy_noise(keys[0], (N_DP, NB, B, B), 1.0, 6.0, ((0, 4), (1, 8)), (0, 2, 4, 2.0))
    left_roots = draw_left_roots(jax.random.fold_in(keys[5], 71), 0)
    right_roots = draw_right_roots(jax.random.fold_in(keys[5], 71), 0)
    rows_valid = draw_rows_valid(jax.random.fold_in(keys[5], 71), 0)
    cols_valid = draw_cols_valid(jax.random.fold_in(keys[5], 71), 0)
    return {"grads": grads, "left_roots": left_roots, "right_roots": right_roots, "rows_valid": rows_valid, "cols_valid": cols_valid}


def precondition(items):
    masked, left, right = items
    half = jnp.dot(masked, right, preferred_element_type=jnp.float32).astype(jnp.bfloat16)
    left_groups = left.reshape(B, N_DP, B // N_DP).astype(jnp.float32)
    half_groups = half.reshape(N_DP, B // N_DP, B).astype(jnp.float32)
    terms = jnp.einsum("iks,ksj->kij", left_groups, half_groups).astype(jnp.bfloat16)
    return jnp.sum(terms.astype(jnp.float32), axis=0)


def reference(grads, left_roots, right_roots, rows_valid, cols_valid):
    grad = jnp.sum(grads.astype(jnp.float32), axis=0)
    rows = jnp.arange(B, dtype=jnp.int32)
    mask = (rows[None, :, None] < rows_valid[:, None, None]) & (rows[None, None, :] < cols_valid[:, None, None])
    masked = jnp.where(mask, grad, 0.0).astype(jnp.bfloat16)
    offset = NB // 2
    left = jnp.roll(left_roots, offset, axis=0)
    right = jnp.roll(right_roots, offset, axis=0)
    summed = lax.map(precondition, (masked, left, right))
    return jnp.where(mask, summed, 0.0).astype(jnp.bfloat16)
```

```python
import functools

import jax
import jax.numpy as jnp
from jax import lax
from jax.experimental import pallas as pl
from jax.experimental.pallas import tpu as pltpu
from jax.sharding import PartitionSpec as P

TILE = 256
VMEM = 56 * 1024 * 1024


def shifted(value, axis, steps):
    count = lax.axis_size(axis)
    pairs = [(source, (source + steps) % count) for source in range(count)]
    return lax.ppermute(value, axis, pairs)


def swapped(value, axis, flip):
    count = lax.axis_size(axis)
    return lax.ppermute(value, axis, [(source, source ^ flip) for source in range(count)])


def pack_kernel(strip, me_ref, left_ref, right_ref, corner_ref, packed_ref, diag_ref):
    step = pl.program_id(0)
    rows = packed_ref.shape[0]
    width = packed_ref.shape[1]
    start = me_ref[0] * strip + step * rows
    row = lax.broadcasted_iota(jnp.int32, (rows, width), 0) + start
    column = lax.broadcasted_iota(jnp.int32, (rows, width), 1)
    packed_ref[...] = jnp.where(row <= column, left_ref[0], right_ref[0])
    tile = corner_ref.shape[1]
    on_diag = lax.broadcasted_iota(jnp.int32, (tile, tile), 0) == lax.broadcasted_iota(jnp.int32, (tile, tile), 1)
    line = jnp.sum(jnp.where(on_diag, corner_ref[0].astype(jnp.float32), 0.0), axis=0, keepdims=True)
    per = tile // 128
    for part in range(per):
        diag_ref[pl.ds(step * per + part, 1), :] = line[:, part * 128 : (part + 1) * 128]


def pack(me, left, right, strip):
    width = left.shape[-1]
    steps = width // TILE
    rows = strip // steps
    return pl.pallas_call(
        functools.partial(pack_kernel, strip),
        grid_spec=pltpu.PrefetchScalarGridSpec(
            num_scalar_prefetch=1,
            grid=(steps,),
            in_specs=[
                pl.BlockSpec((1, rows, width), lambda i, me: (0, me[0] * steps + i, 0)),
                pl.BlockSpec((1, rows, width), lambda i, me: (0, me[0] * steps + i, 0)),
                pl.BlockSpec((1, TILE, TILE), lambda i, me: (0, i, i)),
            ],
            out_specs=[
                pl.BlockSpec((rows, width), lambda i, me: (i, 0)),
                pl.BlockSpec((width // 128, 128), lambda i, me: (0, 0)),
            ],
        ),
        out_shape=[
            jax.ShapeDtypeStruct((strip, width), jnp.bfloat16),
            jax.ShapeDtypeStruct((width // 128, 128), jnp.float32),
        ],
        compiler_params=pltpu.CompilerParams(vmem_limit_bytes=VMEM),
        name="pack_roots",
    )(me, left, right, right)


def product_kernel(groups, me_ref, rows_ref, cols_ref, grad_ref, diag_ref, *refs):
    pieces, outs, (packed, left, right, half) = refs[:groups], refs[groups : 2 * groups], refs[2 * groups :]
    width = packed.shape[0]
    strip = width // groups
    tiles = width // TILE
    me = me_ref[0]
    for flip in range(groups):
        start = pl.multiple_of(jnp.bitwise_xor(me, flip) * strip, strip)
        packed[pl.ds(start, strip), :] = pieces[flip][...]

    row = lax.broadcasted_iota(jnp.int32, (TILE, TILE), 0)
    column = lax.broadcasted_iota(jnp.int32, (TILE, TILE), 1)
    for i in range(tiles):
        at_i = pl.ds(i * TILE, TILE)
        corner = packed[at_i, at_i].astype(jnp.float32)
        turned = corner.T
        line = jnp.concatenate(
            [diag_ref[pl.ds(i * (TILE // 128) + part, 1), :] for part in range(TILE // 128)], axis=1
        )
        left[at_i, at_i] = jnp.where(row <= column, corner, turned).astype(jnp.bfloat16)
        right[at_i, at_i] = jnp.where(
            row == column, jnp.broadcast_to(line, (TILE, TILE)), jnp.where(row > column, corner, turned)
        ).astype(jnp.bfloat16)
        for j in range(i):
            at_j = pl.ds(j * TILE, TILE)
            low, high = packed[at_i, at_j], packed[at_j, at_i]
            right[at_i, at_j] = low
            right[at_j, at_i] = low.T
            left[at_j, at_i] = high
            left[at_i, at_j] = high.T

    rows_valid, cols_valid = rows_ref[0], cols_ref[0]

    def mask_rows(i, carry):
        at = pl.ds(pl.multiple_of(i * TILE, TILE), TILE)
        rows = lax.broadcasted_iota(jnp.int32, (TILE, width), 0) + i * TILE
        columns = lax.broadcasted_iota(jnp.int32, (TILE, width), 1)
        keep = (rows < rows_valid) & (columns < cols_valid)
        value = jnp.where(keep, grad_ref[0, 0, at, :].astype(jnp.float32), 0.0).astype(jnp.bfloat16)
        half[at, :] = jnp.dot(value, right[...], preferred_element_type=jnp.float32).astype(jnp.bfloat16)
        return carry

    lax.fori_loop(0, tiles, mask_rows, 0)
    for flip in reversed(range(groups)):
        start = pl.multiple_of(jnp.bitwise_xor(me, flip) * strip, strip)
        outs[flip][...] = jnp.dot(
            left[pl.ds(start, strip), :], half[...], preferred_element_type=jnp.float32
        ).astype(jnp.bfloat16)


def product(me, rows_valid, cols_valid, grads, diag, pieces):
    groups = len(pieces)
    width = grads.shape[-1]
    strip = width // groups
    smem = pl.BlockSpec(memory_space=pltpu.SMEM)
    vmem = pl.BlockSpec(memory_space=pltpu.VMEM)
    return pl.pallas_call(
        functools.partial(product_kernel, groups),
        in_specs=[smem, smem, smem] + [vmem] * (2 + groups),
        out_specs=[vmem] * groups,
        out_shape=[jax.ShapeDtypeStruct((strip, width), jnp.bfloat16)] * groups,
        scratch_shapes=[pltpu.VMEM((width, width), jnp.bfloat16)] * 4,
        compiler_params=pltpu.CompilerParams(vmem_limit_bytes=VMEM),
        name="left_grad_right",
    )(me, rows_valid, cols_valid, grads, diag, *pieces)


def on_device(grads, left_roots, right_roots, rows_valid, cols_valid):
    width = grads.shape[3]
    groups = lax.axis_size("dp")
    strip = width // groups
    me = lax.axis_index("dp")
    me_arr = me.astype(jnp.int32).reshape(1)
    offset = lax.axis_size("shard") // 2

    packed, diag = pack(me_arr, left_roots, right_roots, strip)
    packed, diag = shifted((packed, diag), "shard", offset)
    pieces = [packed] + [swapped(packed, "dp", flip) for flip in range(1, groups)]
    terms = product(me_arr, rows_valid, cols_valid, grads, diag, pieces)
    got = [terms[0]] + [swapped(terms[flip], "dp", flip) for flip in range(1, groups)]

    row_ids = me * strip + jnp.arange(strip, dtype=jnp.int32)
    col_ids = jnp.arange(width, dtype=jnp.int32)
    mask = (row_ids[:, None] < rows_valid[0]) & (col_ids[None, :] < cols_valid[0])
    total = functools.reduce(lambda a, b: a + b, [term.astype(jnp.float32) for term in got])
    return jnp.where(mask, total, 0.0).astype(jnp.bfloat16)[None]


def solution(mesh):
    placed = (
        P("dp", "shard", None, None),
        P("shard", None, None),
        P("shard", None, None),
        P("shard"),
        P("shard"),
    )
    return jax.shard_map(
        on_device, mesh=mesh, in_specs=placed, out_specs=P("shard", "dp", None), check_vma=False
    )
```

```python
import functools

import jax
import jax.numpy as jnp
from jax import lax
from jax.experimental import pallas as pl
from jax.experimental.pallas import tpu as pltpu
from jax.sharding import PartitionSpec as P

TILE = 256
VMEM = 24 * 1024 * 1024
PACK_VMEM = 60 * 1024 * 1024
SMEM_SPEC = pl.BlockSpec(memory_space=pltpu.SMEM)
VMEM_SPEC = pl.BlockSpec(memory_space=pltpu.VMEM)
BF16 = jnp.bfloat16
F32 = jnp.float32


def shifted(value, axis, steps):
    count = lax.axis_size(axis)
    pairs = [(source, (source + steps) % count) for source in range(count)]
    return lax.ppermute(value, axis, pairs)


def swapped(value, flip):
    count = lax.axis_size("dp")
    return lax.ppermute(value, "dp", [(source, source ^ flip) for source in range(count)])


def after(value, *earlier):
    return lax.optimization_barrier((value, *earlier))[0]


def gathered(value, turn):
    count = lax.axis_size("dp")
    if count != 4:
        return [value] + [swapped(value, flip) for flip in range(1, count)]
    near = [swapped(value, 1), swapped(value, 2)]
    return [value, *near, swapped(near[turn], 2 - turn)]


def layout(tiles):
    above = [(i, j) for i in range(tiles) for j in range(i + 1, tiles)]
    cut = len(above) // 2
    below = [(i, j) for j in range(tiles) for i in range(j + 1, tiles)]
    return {
        "left_a": above[:cut],
        "left_b": above[cut:],
        "corner": [(i, i) for i in range(tiles)],
        "right_a": below[:cut],
        "right_b": below[cut:],
    }


def block(index):
    return pl.ds(index * TILE, TILE)


def cost(flops, bytes_accessed):
    return pl.CostEstimate(flops=flops, bytes_accessed=bytes_accessed, transcendentals=0)


def pack_first_kernel(blocks, rows_of, tiles, me_ref, *refs):
    lefts, out = refs[: len(rows_of)], refs[-1]
    strip = out.shape[0] // len(blocks)
    for k, (i, j) in enumerate(blocks):
        out[pl.ds(k * strip, strip), :] = lefts[rows_of.index(i)][0, :, block(j)]


def strip_specs(rows_of, strip, width, groups):
    def index_map(i):
        return lambda step, me: (0, i * groups + me[0], 0)

    return [pl.BlockSpec((1, strip, width), index_map(i)) for i in rows_of]


def pack_first(me, left, groups, blocks):
    width = left.shape[-1]
    strip = TILE // groups
    rows_of = sorted({i for i, _ in blocks})
    return pl.pallas_call(
        functools.partial(pack_first_kernel, blocks, rows_of, width // TILE),
        grid_spec=pltpu.PrefetchScalarGridSpec(
            num_scalar_prefetch=1,
            grid=(1,),
            in_specs=strip_specs(rows_of, strip, width, groups),
            out_specs=pl.BlockSpec((len(blocks) * strip, TILE), lambda step, me: (0, 0)),
        ),
        out_shape=jax.ShapeDtypeStruct((len(blocks) * strip, TILE), BF16),
        compiler_params=pltpu.CompilerParams(vmem_limit_bytes=PACK_VMEM),
        name="pack_first",
    )(me, *[left] * len(rows_of))


def pack_rest_kernel(plan, tiles, me_ref, *refs):
    lefts, rights, outs = refs[:tiles], refs[tiles : 2 * tiles], refs[2 * tiles :]
    strip = lefts[0].shape[1]
    left_b, corner, right_a, right_b = outs
    for k, (i, j) in enumerate(plan["left_b"]):
        left_b[pl.ds(k * strip, strip), :] = lefts[i][0, :, block(j)]
    for out, name in ((right_a, "right_a"), (right_b, "right_b")):
        for k, (i, j) in enumerate(plan[name]):
            out[pl.ds(k * strip, strip), :] = rights[i][0, :, block(j)]
    row = lax.broadcasted_iota(jnp.int32, (strip, TILE), 0) + me_ref[0] * strip
    column = lax.broadcasted_iota(jnp.int32, (strip, TILE), 1)
    lines = []
    for i in range(tiles):
        mine = lefts[i][0, :, block(i)].astype(F32)
        other = rights[i][0, :, block(i)].astype(F32)
        corner[pl.ds(i * strip, strip), :] = jnp.where(row <= column, mine, other).astype(BF16)
        lines.append(jnp.sum(jnp.where(row == column, other, 0.0), axis=0, keepdims=True))
    extra = right_b.shape[0] - len(plan["right_b"]) * strip
    lines.append(jnp.zeros((extra - tiles, TILE), F32))
    right_b[pl.ds(len(plan["right_b"]) * strip, extra), :] = jnp.concatenate(lines, axis=0).astype(BF16)


def pack_rest(me, left, right, groups, plan):
    width = left.shape[-1]
    strip = TILE // groups
    tiles = width // TILE
    extra = -(-tiles // 16) * 16
    rows = [len(plan[name]) * strip for name in ("left_b", "corner", "right_a", "right_b")]
    rows[-1] += extra
    return pl.pallas_call(
        functools.partial(pack_rest_kernel, plan, tiles),
        grid_spec=pltpu.PrefetchScalarGridSpec(
            num_scalar_prefetch=1,
            grid=(1,),
            in_specs=strip_specs(range(tiles), strip, width, groups) * 2,
            out_specs=[pl.BlockSpec((count, TILE), lambda step, me: (0, 0)) for count in rows],
        ),
        out_shape=[jax.ShapeDtypeStruct((count, TILE), BF16) for count in rows],
        compiler_params=pltpu.CompilerParams(vmem_limit_bytes=PACK_VMEM),
        name="pack_rest",
    )(me, *[left] * tiles, *[right] * tiles)


def place(blocks, pieces, me, target, at=lambda i, j: (i * TILE, j * TILE)):
    strip = TILE // len(pieces)
    for k, (i, j) in enumerate(blocks):
        top, side = at(i, j)
        for flip, piece in enumerate(pieces):
            start = pl.multiple_of(top + jnp.bitwise_xor(me, flip) * strip, strip)
            target[pl.ds(start, strip), pl.ds(side, TILE)] = piece[pl.ds(k * strip, strip), :]


def whole_left_kernel(plan, groups, me_ref, *refs):
    left_a, left_b, corner = refs[:groups], refs[groups : 2 * groups], refs[2 * groups : 3 * groups]
    left, right_corner, mixed = refs[3 * groups :]
    me = me_ref[0]
    tiles = left.shape[0] // TILE
    place(plan["left_a"], left_a, me, left)
    place(plan["left_b"], left_b, me, left)
    place(plan["corner"], corner, me, mixed, lambda i, j: (i * TILE, 0))
    row = lax.broadcasted_iota(jnp.int32, (TILE, TILE), 0)
    column = lax.broadcasted_iota(jnp.int32, (TILE, TILE), 1)
    for i in range(tiles):
        value = mixed[block(i), :].astype(F32)
        turned = value.T
        left[block(i), block(i)] = jnp.where(row <= column, value, turned).astype(BF16)
        right_corner[block(i), :] = jnp.where(row > column, value, turned).astype(BF16)
        for j in range(i):
            left[block(i), block(j)] = left[block(j), block(i)].T


def whole_left(me, width, plan, left_a, left_b, corner):
    groups = len(left_a)
    return pl.pallas_call(
        functools.partial(whole_left_kernel, plan, groups),
        in_specs=[SMEM_SPEC] + [VMEM_SPEC] * (3 * groups),
        out_specs=[VMEM_SPEC] * 2,
        out_shape=[jax.ShapeDtypeStruct((width, width), BF16), jax.ShapeDtypeStruct((width, TILE), BF16)],
        scratch_shapes=[pltpu.VMEM((width, TILE), BF16)],
        compiler_params=pltpu.CompilerParams(vmem_limit_bytes=VMEM),
        cost_estimate=cost(width**2, 4 * width**2),
        name="whole_left",
    )(me, *left_a, *left_b, *corner)


def left_grad_kernel(rows_ref, cols_ref, left, grad_ref, out, grad):
    tiles = left.shape[0] // TILE
    rows_valid, cols_valid = rows_ref[0], cols_ref[0]
    for i in range(tiles):
        for j in range(tiles):
            keep = (i * TILE < rows_valid) & (j * TILE < cols_valid)

            @pl.when(keep)
            def _():
                grad[block(i), block(j)] = grad_ref[0, 0, block(i), block(j)]

            @pl.when(jnp.logical_not(keep))
            def _():
                grad[block(i), block(j)] = jnp.zeros((TILE, TILE), BF16)

    def step(i, carry):
        at = pl.ds(pl.multiple_of(i * TILE, TILE), TILE)
        out[at, :] = jnp.dot(left[at, :], grad[...], preferred_element_type=F32).astype(BF16)
        return carry

    lax.fori_loop(0, tiles, step, 0)


def left_grad(rows_valid, cols_valid, left, grads):
    width = grads.shape[-1]
    return pl.pallas_call(
        left_grad_kernel,
        in_specs=[SMEM_SPEC] * 2 + [VMEM_SPEC] * 2,
        out_specs=VMEM_SPEC,
        out_shape=jax.ShapeDtypeStruct((width, width), BF16),
        scratch_shapes=[pltpu.VMEM((width, width), BF16)],
        compiler_params=pltpu.CompilerParams(vmem_limit_bytes=VMEM),
        cost_estimate=cost(2 * width**3, 6 * width**2),
        name="left_grad",
    )(rows_valid, cols_valid, left, grads)


def far_kernel(plan, groups, me_ref, product_ref, corner_ref, *refs):
    right_a, right_b = refs[:groups], refs[groups : 2 * groups]
    far_first, far_second, right = refs[2 * groups :]
    me = me_ref[0]
    width = right.shape[0]
    tiles = width // TILE
    place(plan["right_a"], right_a, me, right)
    place(plan["right_b"], right_b, me, right)
    row = lax.broadcasted_iota(jnp.int32, (TILE, TILE), 0)
    column = lax.broadcasted_iota(jnp.int32, (TILE, TILE), 1)
    base = len(plan["right_b"]) * (TILE // groups)
    lines = functools.reduce(
        lambda a, b: a + b, [piece[pl.ds(base, piece.shape[0] - base), :].astype(F32) for piece in right_b]
    )
    for i in range(tiles):
        line = jnp.broadcast_to(lines[i : i + 1, :], (TILE, TILE))
        right[block(i), block(i)] = jnp.where(row == column, line, corner_ref[block(i), :].astype(F32)).astype(BF16)
        for j in range(i):
            right[block(j), block(i)] = right[block(i), block(j)].T
    strip = width // groups
    start = pl.multiple_of(jnp.bitwise_xor(me, groups - 1) * strip, strip)
    value = jnp.dot(product_ref[pl.ds(start, strip), :], right[...], preferred_element_type=F32).astype(BF16)
    far_first[...] = value[:, : width // 2]
    far_second[...] = value[:, width // 2 :]


def far(me, product, corner, plan, right_a, right_b):
    groups = len(right_a)
    width = product.shape[0]
    strip = width // groups
    part = jax.ShapeDtypeStruct((strip, width // 2), BF16)
    return pl.pallas_call(
        functools.partial(far_kernel, plan, groups),
        in_specs=[SMEM_SPEC] + [VMEM_SPEC] * (2 + 2 * groups),
        out_specs=[VMEM_SPEC] * 3,
        out_shape=[part, part, jax.ShapeDtypeStruct((width, width), BF16)],
        compiler_params=pltpu.CompilerParams(vmem_limit_bytes=VMEM),
        cost_estimate=cost(2 * strip * width**2, 8 * width**2),
        name="far_rows",
    )(me, product, corner, *right_a, *right_b)


def near_kernel(flips, me_ref, product_ref, right_ref, *outs):
    me = me_ref[0]
    strip = outs[0].shape[0]
    width = right_ref.shape[0]
    for (flip, first, last), out in zip(flips, outs):
        start = pl.multiple_of(jnp.bitwise_xor(me, flip) * strip, strip)
        out[...] = jnp.dot(
            product_ref[pl.ds(start, strip), :], right_ref[:, first:last], preferred_element_type=F32
        ).astype(out.dtype)


def near(me, product, right, groups, flips, name):
    width = product.shape[0]
    strip = width // groups
    return pl.pallas_call(
        functools.partial(near_kernel, flips),
        in_specs=[SMEM_SPEC] + [VMEM_SPEC] * 2,
        out_specs=[VMEM_SPEC] * len(flips),
        out_shape=[jax.ShapeDtypeStruct((strip, last - first), BF16) for _, first, last in flips],
        compiler_params=pltpu.CompilerParams(vmem_limit_bytes=VMEM),
        cost_estimate=cost(2 * strip * width * sum(last - first for _, first, last in flips), 4 * width**2),
        name=name,
    )(me, product, right)


def added(*terms):
    return functools.reduce(lambda a, b: a + b, [term.astype(F32) for term in terms])


def on_device(grads, left_roots, right_roots, rows_valid, cols_valid):
    width = grads.shape[3]
    groups = lax.axis_size("dp")
    strip = width // groups
    half = width // 2
    me = lax.axis_index("dp").astype(jnp.int32)
    me_arr = me.reshape(1)
    offset = lax.axis_size("shard") // 2
    plan = layout(width // TILE)

    messages = [pack_first(me_arr, left_roots, groups, plan["left_a"])]
    crossed = [shifted(messages[0], "shard", offset)]
    messages += pack_rest(me_arr, left_roots, right_roots, groups, plan)
    crossed.append(shifted(messages[1], "shard", offset))
    pieces = []
    for k in range(len(messages)):
        arrived = crossed[k]
        if k > 0:
            arrived = after(arrived, *pieces[-1][1:3], *[piece[3] for piece in pieces[-2:-1]])
        if k == 4:
            left, right_corner = whole_left(me_arr, width, plan, *pieces[:3])
            arrived = after(arrived, right_corner)
        if k + 2 < len(messages):
            crossed.append(shifted(after(messages[k + 2], crossed[k]), "shard", offset))
        pieces.append(gathered(arrived, k % 2))
    right_a, right_b = pieces[3:]
    product = left_grad(rows_valid, cols_valid, left, grads)
    far_first, far_second, right = far(me_arr, product, right_corner, plan, right_a, right_b)
    if groups == 4:
        far_first, far_second = swapped(far_first, 1), swapped(far_second, 2)
        near_first, near_second = near(
            me_arr, product, right, groups, [(1, 0, half), (2, half, width)], "near_rows"
        )
        via_first, via_second, own = near(
            me_arr, product, right, groups, [(2, 0, half), (1, half, width), (0, 0, width)], "own_rows"
        )
        near_first, near_second = swapped(near_first, 1), swapped(near_second, 2)
        via_first = swapped(added(via_first, far_first).astype(BF16), 2)
        via_second = swapped(added(via_second, far_second).astype(BF16), 1)
        total = jnp.concatenate(
            [added(own[:, :half], near_first, via_first), added(own[:, half:], near_second, via_second)], axis=1
        )
    else:
        last = groups - 1
        rest = near(me_arr, product, right, groups, [(flip, 0, width) for flip in range(last)], "near_rows")
        far_whole = swapped(jnp.concatenate([far_first, far_second], axis=1), last)
        total = added(rest[0], far_whole, *[swapped(rest[flip], flip) for flip in range(1, last)])

    row_ids = me * strip + jnp.arange(strip, dtype=jnp.int32)
    col_ids = jnp.arange(width, dtype=jnp.int32)
    mask = (row_ids[:, None] < rows_valid[0]) & (col_ids[None, :] < cols_valid[0])
    return jnp.where(mask, total, 0.0).astype(BF16)[None]


def solution(mesh):
    placed = (
        P("dp", "shard", None, None),
        P("shard", None, None),
        P("shard", None, None),
        P("shard"),
        P("shard"),
    )
    return jax.shard_map(
        on_device, mesh=mesh, in_specs=placed, out_specs=P("shard", "dp", None), check_vma=False
    )
```

```python
import functools

import jax
import jax.numpy as jnp
from jax import lax
from jax.experimental import pallas as pl
from jax.experimental.pallas import tpu as pltpu
from jax.sharding import PartitionSpec as P

TILE = 256
EXTRA = 16
VMEM = 24 * 1024 * 1024
PACK_VMEM = 60 * 1024 * 1024
SMEM_SPEC = pl.BlockSpec(memory_space=pltpu.SMEM)
VMEM_SPEC = pl.BlockSpec(memory_space=pltpu.VMEM)
BF16 = jnp.bfloat16
F32 = jnp.float32


def shifted(value, axis, steps):
    count = lax.axis_size(axis)
    pairs = [(source, (source + steps) % count) for source in range(count)]
    return lax.ppermute(value, axis, pairs)


def swapped(value, flip):
    count = lax.axis_size("dp")
    return lax.ppermute(value, "dp", [(source, source ^ flip) for source in range(count)])


def block(index):
    return pl.ds(index * TILE, TILE)


def cost(flops, bytes_accessed):
    return pl.CostEstimate(flops=flops, bytes_accessed=bytes_accessed, transcendentals=0)


def below(tiles):
    return [(i, j) for j in range(tiles) for i in range(j + 1, tiles)]


def pick_kernel(me_ref, *refs):
    count = len(refs) // 2
    for source, target in zip(refs[:count], refs[count:]):
        target[...] = source[0, 0]


def pick(me, grads, groups, wanted, name):
    width = grads.shape[-1]
    strip, half = width // groups, width // 2

    def index_map(flip, h):
        return lambda step, me: (0, 0, jnp.bitwise_xor(me[0], flip), h)

    return pl.pallas_call(
        pick_kernel,
        grid_spec=pltpu.PrefetchScalarGridSpec(
            num_scalar_prefetch=1,
            grid=(1,),
            in_specs=[pl.BlockSpec((1, 1, strip, half), index_map(flip, h)) for flip, h in wanted],
            out_specs=[pl.BlockSpec((strip, half), lambda step, me: (0, 0))] * len(wanted),
        ),
        out_shape=[jax.ShapeDtypeStruct((strip, half), BF16)] * len(wanted),
        compiler_params=pltpu.CompilerParams(vmem_limit_bytes=PACK_VMEM),
        name=name,
    )(me, *[grads] * len(wanted))


def fold_kernel(tiles, me_ref, *refs):
    rights, out = refs[:tiles], refs[-1]
    strip = rights[0].shape[1]
    places = [(pl.ds(k // tiles * strip, strip), block(k % tiles)) for k in range(tiles * tiles // 2)]
    blocks = below(tiles)
    for (i, j), at in zip(blocks, places):
        out[at] = rights[i][0, :, block(j)]
    row = lax.broadcasted_iota(jnp.int32, (strip, TILE), 0) + me_ref[0] * strip
    column = lax.broadcasted_iota(jnp.int32, (strip, TILE), 1)
    for pair, at in enumerate(places[len(blocks) :]):
        even, odd = 2 * pair, 2 * pair + 1
        out[at] = jnp.where(row >= column, rights[even][0, :, block(even)], rights[odd][0, :, block(odd)])


def fold(me, right, groups):
    width = right.shape[-1]
    strip = TILE // groups
    tiles = width // TILE

    def index_map(i):
        return lambda step, me: (0, i * groups + me[0], 0)

    return pl.pallas_call(
        functools.partial(fold_kernel, tiles),
        grid_spec=pltpu.PrefetchScalarGridSpec(
            num_scalar_prefetch=1,
            grid=(1,),
            in_specs=[pl.BlockSpec((1, strip, width), index_map(i)) for i in range(tiles)],
            out_specs=pl.BlockSpec((tiles // 2 * strip, width), lambda step, me: (0, 0)),
        ),
        out_shape=jax.ShapeDtypeStruct((tiles // 2 * strip, width), BF16),
        compiler_params=pltpu.CompilerParams(vmem_limit_bytes=PACK_VMEM),
        name="fold_right",
    )(me, *[right] * tiles)


def left_strip_kernel(tiles, me_ref, left_ref, *refs):
    corners, out = refs[:tiles], refs[-1]
    strip = left_ref.shape[1]
    out[pl.ds(0, strip), :] = left_ref[0]
    on_diag = lax.broadcasted_iota(jnp.int32, (TILE, TILE), 0) == lax.broadcasted_iota(jnp.int32, (TILE, TILE), 1)
    lines = [
        jnp.sum(jnp.where(on_diag, corner[0].astype(F32), 0.0), axis=0, keepdims=True) for corner in corners
    ]
    line = jnp.concatenate(lines, axis=1)
    out[pl.ds(strip, EXTRA), :] = jnp.broadcast_to(line, (EXTRA, line.shape[1])).astype(BF16)


def left_strip(me, left, right, groups):
    width = left.shape[-1]
    strip = width // groups
    tiles = width // TILE

    def corner_map(i):
        return lambda step, me: (0, i, i)

    return pl.pallas_call(
        functools.partial(left_strip_kernel, tiles),
        grid_spec=pltpu.PrefetchScalarGridSpec(
            num_scalar_prefetch=1,
            grid=(1,),
            in_specs=[pl.BlockSpec((1, strip, width), lambda step, me: (0, me[0], 0))]
            + [pl.BlockSpec((1, TILE, TILE), corner_map(i)) for i in range(tiles)],
            out_specs=pl.BlockSpec((strip + EXTRA, width), lambda step, me: (0, 0)),
        ),
        out_shape=jax.ShapeDtypeStruct((strip + EXTRA, width), BF16),
        compiler_params=pltpu.CompilerParams(vmem_limit_bytes=PACK_VMEM),
        name="left_strip",
    )(me, left, *[right] * tiles)


def payload_kernel(h, groups, me_ref, rows_ref, cols_ref, folded_ref, own_ref, *refs):
    terms, out = refs[:-1], refs[-1]
    strip, half = own_ref.shape
    total = own_ref[...].astype(F32)
    for term in terms:
        total = total + term[...].astype(F32)
    column = lax.broadcasted_iota(jnp.int32, (strip, half), 1) + h * half
    row = lax.broadcasted_iota(jnp.int32, (strip, half), 0) + me_ref[0] * strip
    keep = (row < rows_ref[0]) & (column < cols_ref[0])
    out[pl.ds(0, strip), :] = jnp.where(keep, total, 0.0).astype(BF16)
    out[pl.ds(strip, out.shape[0] - strip), :] = folded_ref[:, pl.ds(h * half, half)]


def payload(me, rows_valid, cols_valid, folded, own, terms, h, groups):
    strip, half = own.shape
    return pl.pallas_call(
        functools.partial(payload_kernel, h, groups),
        in_specs=[SMEM_SPEC] * 3 + [VMEM_SPEC] * (2 + len(terms)),
        out_specs=VMEM_SPEC,
        out_shape=jax.ShapeDtypeStruct((strip + folded.shape[0], half), BF16),
        compiler_params=pltpu.CompilerParams(vmem_limit_bytes=VMEM),
        cost_estimate=cost(8 * strip * half, 8 * strip * half),
        name="payload",
    )(me, rows_valid, cols_valid, folded, own, *terms)


def update_kernel(groups, me_ref, rows_ref, cols_ref, left_ref, *refs):
    pieces, (out, masked, right, folded) = refs[: 2 * groups], refs[2 * groups :]
    me = me_ref[0]
    width = masked.shape[0]
    tiles = width // TILE
    strip, part, half = width // groups, TILE // groups, width // 2
    blocks = below(tiles)
    for flip in range(groups):
        other = jnp.bitwise_xor(me, flip)
        rows = pl.ds(pl.multiple_of(other * strip, strip), strip)
        for h in range(2):
            piece = pieces[2 * flip + h]
            masked[rows, pl.ds(h * half, half)] = piece[pl.ds(0, strip), :]
            for k in range(tiles * tiles // 2):
                side = k % tiles * TILE - h * half
                if side < 0 or side >= half:
                    continue
                value = piece[pl.ds(strip + k // tiles * part, part), pl.ds(side, TILE)]
                if k < len(blocks):
                    i, j = blocks[k]
                    right[pl.ds(pl.multiple_of(i * TILE + other * part, part), part), block(j)] = value
                else:
                    at = (k - len(blocks)) * TILE + other * part
                    folded[pl.ds(pl.multiple_of(at, part), part), :] = value
    row = lax.broadcasted_iota(jnp.int32, (TILE, TILE), 0)
    column = lax.broadcasted_iota(jnp.int32, (TILE, TILE), 1)
    for i in range(tiles):
        value = folded[block(i // 2), :].astype(F32)
        keep = row >= column if i % 2 == 0 else row < column
        value = jnp.where(keep, value, value.T)
        if i % 2:
            line = left_ref[pl.ds(strip, EXTRA), block(i)].astype(F32)[:1]
            value = jnp.where(row == column, jnp.broadcast_to(line, (TILE, TILE)), value)
        right[block(i), block(i)] = value.astype(BF16)
        for j in range(i):
            right[block(j), block(i)] = right[block(i), block(j)].T
    mixed = jnp.dot(left_ref[pl.ds(0, strip), :], masked[...], preferred_element_type=F32).astype(BF16)
    value = jnp.dot(mixed, right[...], preferred_element_type=F32)
    column = lax.broadcasted_iota(jnp.int32, (strip, width), 1)
    row = lax.broadcasted_iota(jnp.int32, (strip, width), 0) + me * strip
    out[0] = jnp.where((row < rows_ref[0]) & (column < cols_ref[0]), value, 0.0).astype(BF16)


def update(me, rows_valid, cols_valid, left, pieces, groups):
    width = left.shape[-1]
    strip = width // groups
    return pl.pallas_call(
        functools.partial(update_kernel, groups),
        in_specs=[SMEM_SPEC] * 3 + [VMEM_SPEC] * (1 + 2 * groups),
        out_specs=VMEM_SPEC,
        out_shape=jax.ShapeDtypeStruct((1, strip, width), BF16),
        scratch_shapes=[
            pltpu.VMEM((width, width), BF16),
            pltpu.VMEM((width, width), BF16),
            pltpu.VMEM((width // 2, TILE), BF16),
        ],
        compiler_params=pltpu.CompilerParams(vmem_limit_bytes=VMEM),
        cost_estimate=cost(4 * strip * width**2, 8 * width**2),
        name="update",
    )(me, rows_valid, cols_valid, left, *[half for piece in pieces for half in piece])


def added(*terms):
    return functools.reduce(lambda a, b: a + b, [term.astype(F32) for term in terms])


def on_device(grads, left_roots, right_roots, rows_valid, cols_valid):
    groups = lax.axis_size("dp")
    me = lax.axis_index("dp").astype(jnp.int32).reshape(1)
    offset = lax.axis_size("shard") // 2

    if groups == 4:
        far_0, far_1, near_0, near_1 = pick(me, grads, groups, [(3, 0), (3, 1), (1, 0), (2, 1)], "pick_sent")
        far_0, far_1 = swapped(far_0, 1), swapped(far_1, 2)
        folded = shifted(fold(me, right_roots, groups), "shard", offset)
        near_0, near_1 = swapped(near_0, 1), swapped(near_1, 2)
        left = shifted(left_strip(me, left_roots, right_roots, groups), "shard", offset)
        via_0, via_1, own_0, own_1 = pick(me, grads, groups, [(2, 0), (1, 1), (0, 0), (0, 1)], "pick_kept")
        via_0 = swapped(added(via_0, far_0).astype(BF16), 2)
        via_1 = swapped(added(via_1, far_1).astype(BF16), 1)
        mine_0 = payload(me, rows_valid, cols_valid, folded, own_0, [near_0, via_0], 0, groups)
        mine_1 = payload(me, rows_valid, cols_valid, folded, own_1, [near_1, via_1], 1, groups)
        up_0, side_1 = swapped(mine_0, 2), swapped(mine_1, 1)
        side_0, up_1 = swapped(mine_0, 1), swapped(mine_1, 2)
        pieces = [(mine_0, mine_1), (side_0, side_1), (up_0, up_1), (swapped(up_0, 1), swapped(side_1, 2))]
    else:
        folded = shifted(fold(me, right_roots, groups), "shard", offset)
        left = shifted(left_strip(me, left_roots, right_roots, groups), "shard", offset)
        mine = []
        for h in range(2):
            terms = pick(me, grads, groups, [(flip, h) for flip in range(groups)], "pick_all")
            got = [swapped(terms[flip], flip) for flip in range(1, groups)]
            mine.append(payload(me, rows_valid, cols_valid, folded, terms[0], got, h, groups))
        pieces = [mine] + [[swapped(part, flip) for part in mine] for flip in range(1, groups)]
    return update(me, rows_valid, cols_valid, left, pieces, groups)


def solution(mesh):
    placed = (
        P("dp", "shard", None, None),
        P("shard", None, None),
        P("shard", None, None),
        P("shard"),
        P("shard"),
    )
    return jax.shard_map(
        on_device, mesh=mesh, in_specs=placed, out_specs=P("shard", "dp", None), check_vma=False
    )
```

```python
import functools

import jax
import jax.numpy as jnp
from jax import lax
from jax.experimental import pallas as pl
from jax.experimental.pallas import tpu as pltpu
from jax.sharding import PartitionSpec as P

TILE = 256
EXTRA = 16
VMEM = 24 * 1024 * 1024
SMEM_SPEC = pl.BlockSpec(memory_space=pltpu.SMEM)
VMEM_SPEC = pl.BlockSpec(memory_space=pltpu.VMEM)
HBM_SPEC = pl.BlockSpec(memory_space=pltpu.HBM)
BF16 = jnp.bfloat16
F32 = jnp.float32


def shifted(value, axis, steps):
    count = lax.axis_size(axis)
    pairs = [(source, (source + steps) % count) for source in range(count)]
    return lax.ppermute(value, axis, pairs)


def swapped(value, flip):
    count = lax.axis_size("dp")
    return lax.ppermute(value, "dp", [(source, source ^ flip) for source in range(count)])


def after(value, *earlier):
    return lax.optimization_barrier((value, *earlier))[0]


def block(index):
    return pl.ds(index * TILE, TILE)


def strip_of(index, size):
    return pl.ds(pl.multiple_of(index * size, size), size)


def cost(flops, bytes_accessed):
    return pl.CostEstimate(flops=flops, bytes_accessed=bytes_accessed, transcendentals=0)


def below(tiles):
    return [(i, j) for j in range(tiles) for i in range(j + 1, tiles)]


def pick_copies(wanted, me, grad_ref, outs, sems):
    copies = []
    for parts, out in zip(wanted, outs):
        half, strip = out.shape[0] // len(parts), out.shape[1]
        for part, (flip, h) in enumerate(parts):
            source = grad_ref.at[0, 0, pl.ds(h * half, half), strip_of(jnp.bitwise_xor(me, flip), strip)]
            copies.append(
                pltpu.make_async_copy(source, out.at[pl.ds(part * half, half), :], sems.at[len(copies)])
            )
    return copies


def picked_shapes(wanted, width, groups):
    return [pltpu.VMEM((len(parts) * (width // 2), width // groups), BF16) for parts in wanted]


def pick_kernel(wanted, me_ref, grad_ref, *refs):
    copies = pick_copies(wanted, me_ref[0], grad_ref, refs[:-1], refs[-1])
    for copy in copies:
        copy.start()
    for copy in copies:
        copy.wait()


def pick(me, grads, groups, wanted):
    return pl.pallas_call(
        functools.partial(pick_kernel, wanted),
        in_specs=[SMEM_SPEC, HBM_SPEC],
        out_specs=[VMEM_SPEC] * len(wanted),
        out_shape=picked_shapes(wanted, grads.shape[-1], groups),
        scratch_shapes=[pltpu.SemaphoreType.DMA((sum(len(parts) for parts in wanted),))],
        compiler_params=pltpu.CompilerParams(vmem_limit_bytes=VMEM),
        name="pick_kept",
    )(me, grads)


def fold_copies(me, root_ref, strips, odd_corners, sems):
    tiles, strip, _ = strips.shape
    return [
        pltpu.make_async_copy(
            root_ref.at[0, pl.ds(pl.multiple_of(i * TILE + me * strip, strip), strip), :], strips.at[i], sems.at[i]
        )
        for i in range(tiles)
    ] + [
        pltpu.make_async_copy(
            root_ref.at[0, block(2 * pair + 1), block(2 * pair + 1)], odd_corners.at[pair], sems.at[tiles + pair]
        )
        for pair in range(tiles // 2)
    ]


def fold(me, strips, odd_corners, out):
    tiles, strip, _ = strips.shape
    blocks = below(tiles)
    for k, (i, j) in enumerate(blocks):
        out[pl.ds(k * strip, strip), :] = strips[i, :, block(j)]
    row = lax.broadcasted_iota(jnp.int32, (strip, TILE), 0) + me * strip
    column = lax.broadcasted_iota(jnp.int32, (strip, TILE), 1)
    on_diag = lax.broadcasted_iota(jnp.int32, (TILE, TILE), 0) == lax.broadcasted_iota(jnp.int32, (TILE, TILE), 1)
    lines = []
    for pair in range(tiles // 2):
        even, odd = 2 * pair, 2 * pair + 1
        out[pl.ds((len(blocks) + pair) * strip, strip), :] = jnp.where(
            row >= column, strips[even, :, block(even)], strips[odd, :, block(odd)]
        )
        corner = odd_corners[pair].astype(F32)
        lines.append(jnp.sum(jnp.where(on_diag, corner, 0.0), axis=0, keepdims=True))
    lines.append(jnp.zeros((EXTRA - len(lines), TILE), F32))
    out[pl.ds(tiles * tiles // 2 * strip, EXTRA), :] = jnp.concatenate(lines, axis=0).astype(BF16)


def messages_kernel(wanted, me_ref, grad_ref, left_ref, right_ref, *refs):
    outs, (left, right, strips, odd_corners, pick_sems, fold_sems) = refs[: len(wanted)], refs[len(wanted) :]
    me = me_ref[0]
    copies = pick_copies(wanted, me, grad_ref, outs, pick_sems)
    roots = [
        fold_copies(me, root, strips.at[index], odd_corners.at[index], fold_sems.at[index])
        for index, root in enumerate((left_ref, right_ref))
    ]
    for copy in roots[0] + roots[1] + copies:
        copy.start()
    for index, out in enumerate((left, right)):
        for copy in roots[index]:
            copy.wait()
        fold(me, strips.at[index], odd_corners.at[index], out)
    for copy in copies:
        copy.wait()


def messages(me, grads, left, right, groups, wanted):
    width = grads.shape[-1]
    strip, tiles = TILE // groups, width // TILE
    count = sum(len(parts) for parts in wanted)
    folded = pltpu.VMEM((tiles * tiles // 2 * strip + EXTRA, TILE), BF16)
    return pl.pallas_call(
        functools.partial(messages_kernel, wanted),
        in_specs=[SMEM_SPEC] + [HBM_SPEC] * 3,
        out_specs=[VMEM_SPEC] * (len(wanted) + 2),
        out_shape=picked_shapes(wanted, width, groups) + [folded] * 2,
        scratch_shapes=[
            pltpu.VMEM((2, tiles, strip, width), BF16),
            pltpu.VMEM((2, tiles // 2, TILE, TILE), BF16),
            pltpu.SemaphoreType.DMA((max(count, 1),)),
            pltpu.SemaphoreType.DMA((2, tiles + tiles // 2)),
        ],
        compiler_params=pltpu.CompilerParams(vmem_limit_bytes=VMEM),
        name="messages",
    )(me, grads, left, right)


def unfold(pieces, me, root, folded):
    tiles = root.shape[0] // TILE
    strip = TILE // len(pieces)
    blocks = below(tiles)
    for flip, piece in enumerate(pieces):
        other = jnp.bitwise_xor(me, flip)
        for k in range(tiles * tiles // 2):
            value = piece[pl.ds(k * strip, strip), :]
            if k < len(blocks):
                i, j = blocks[k]
                root[pl.ds(pl.multiple_of(i * TILE + other * strip, strip), strip), block(j)] = value
            else:
                at = (k - len(blocks)) * TILE + other * strip
                folded[pl.ds(pl.multiple_of(at, strip), strip), :] = value
    row = lax.broadcasted_iota(jnp.int32, (TILE, TILE), 0)
    column = lax.broadcasted_iota(jnp.int32, (TILE, TILE), 1)
    lines = pieces[0][pl.ds(tiles * tiles // 2 * strip, EXTRA), :].astype(F32)
    for i in range(tiles):
        value = folded[block(i // 2), :].astype(F32)
        value = jnp.where(row >= column if i % 2 == 0 else row < column, value, value.T)
        if i % 2:
            line = jnp.broadcast_to(lines[i // 2 : i // 2 + 1, :], (TILE, TILE))
            value = jnp.where(row == column, line, value)
        root[block(i), block(i)] = value.astype(BF16)
        for j in range(i):
            root[block(j), block(i)] = root[block(i), block(j)].T


def columns_kernel(groups, split, me_ref, rows_ref, cols_ref, *refs):
    count = sum(split)
    pieces, terms, outs = refs[:groups], refs[groups : groups + count], refs[groups + count : 2 * groups + count]
    left, folded, masked, mixed = refs[2 * groups + count :]
    me = me_ref[0]
    width, strip = masked.shape
    unfold(pieces, me, left, folded)
    part = width // len(split)
    column = lax.broadcasted_iota(jnp.int32, (part, strip), 1) + me * strip
    row = lax.broadcasted_iota(jnp.int32, (part, strip), 0)
    for index, number in enumerate(split):
        used, terms = terms[:number], terms[number:]
        total = functools.reduce(lambda a, b: a + b, [term[pl.ds(0, part), :].astype(F32) for term in used])
        keep = (row + index * part < rows_ref[0]) & (column < cols_ref[0])
        masked[pl.ds(index * part, part), :] = jnp.where(keep, total, 0.0).astype(BF16)
    mixed[...] = jnp.dot(left[...], masked[...], preferred_element_type=F32).astype(BF16)
    for flip, out in enumerate(outs):
        out[...] = mixed[strip_of(jnp.bitwise_xor(me, flip), strip), :]


def left_columns(me, rows_valid, cols_valid, pieces, terms, width):
    groups = len(pieces)
    strip = width // groups
    flat = [term for part in terms for term in part]
    return pl.pallas_call(
        functools.partial(columns_kernel, groups, [len(part) for part in terms]),
        in_specs=[SMEM_SPEC] * 3 + [VMEM_SPEC] * (groups + len(flat)),
        out_specs=[VMEM_SPEC] * groups,
        out_shape=[pltpu.VMEM((strip, strip), BF16)] * groups,
        scratch_shapes=[
            pltpu.VMEM((width, width), BF16),
            pltpu.VMEM((width // 2, TILE), BF16),
            pltpu.VMEM((width, strip), BF16),
            pltpu.VMEM((width, strip), BF16),
        ],
        compiler_params=pltpu.CompilerParams(vmem_limit_bytes=VMEM),
        cost_estimate=cost(2 * strip * width**2, 4 * width**2),
        name="left_columns",
    )(me, rows_valid, cols_valid, *pieces, *flat)


def rows_kernel(groups, me_ref, rows_ref, cols_ref, *refs):
    pieces, strips, (out, right, folded) = refs[:groups], refs[groups : 2 * groups], refs[2 * groups :]
    me = me_ref[0]
    width = right.shape[0]
    strip = width // groups
    unfold(pieces, me, right, folded)
    value = functools.reduce(
        lambda a, b: a + b,
        [
            jnp.dot(
                part[...], right[strip_of(jnp.bitwise_xor(me, flip), strip), :], preferred_element_type=F32
            )
            for flip, part in enumerate(strips)
        ],
    )
    column = lax.broadcasted_iota(jnp.int32, (strip, width), 1)
    row = lax.broadcasted_iota(jnp.int32, (strip, width), 0) + me * strip
    out[0] = jnp.where((row < rows_ref[0]) & (column < cols_ref[0]), value, 0.0).astype(BF16)


def update_rows(me, rows_valid, cols_valid, pieces, strips, width):
    groups = len(pieces)
    strip = width // groups
    return pl.pallas_call(
        functools.partial(rows_kernel, groups),
        in_specs=[SMEM_SPEC] * 3 + [VMEM_SPEC] * (2 * groups),
        out_specs=VMEM_SPEC,
        out_shape=jax.ShapeDtypeStruct((1, strip, width), BF16),
        scratch_shapes=[pltpu.VMEM((width, width), BF16), pltpu.VMEM((width // 2, TILE), BF16)],
        compiler_params=pltpu.CompilerParams(vmem_limit_bytes=VMEM),
        cost_estimate=cost(2 * strip * width**2, 4 * width**2),
        name="update_rows",
    )(me, rows_valid, cols_valid, *pieces, *strips)


def added(*terms):
    return functools.reduce(lambda a, b: a + b, [term.astype(F32) for term in terms])


def on_device(grads, left_roots, right_roots, rows_valid, cols_valid):
    groups = lax.axis_size("dp")
    me = lax.axis_index("dp").astype(jnp.int32).reshape(1)
    offset = lax.axis_size("shard") // 2
    width = grads.shape[-1]
    half, strip = width // 2, width // groups
    plain = grads
    grads, left_roots, right_roots = (
        pltpu.with_memory_space_constraint(array, pltpu.HBM) for array in (grads, left_roots, right_roots)
    )

    if groups == 4:
        sent_0, sent_1, left, right = messages(
            me, grads, left_roots, right_roots, groups, [[(1, 0), (3, 0)], [(2, 1), (3, 1)]]
        )
        sent_0, sent_1 = swapped(sent_0, 1), swapped(sent_1, 2)
        left, right = shifted((left, right), "shard", offset)
        kept = pick(me, grads, groups, [[(2, 0)], [(1, 1)], [(0, 0)], [(0, 1)]])
        via_0, via_1 = added(kept[0], sent_0[half:]).astype(BF16), added(kept[1], sent_1[half:]).astype(BF16)
        left = after(left, via_0, via_1)
        via_0, via_1 = swapped(via_0, 2), swapped(via_1, 1)
        lefts = [left, swapped(left, 1), swapped(left, 2)]
        lefts.append(swapped(lefts[1], 2))
        strips = left_columns(
            me, rows_valid, cols_valid, lefts, [[kept[2], sent_0, via_0], [kept[3], sent_1, via_1]], width
        )
        right = after(right, via_0, via_1)
        rights = [right, swapped(right, 1), swapped(right, 2)]
        rights.append(swapped(after(rights[2], strips[0]), 1))
    else:
        left, right = messages(me, grads, left_roots, right_roots, groups, [])
        left, right = shifted((left, right), "shard", offset)
        parts = [
            lax.dynamic_slice_in_dim(plain[0, 0], jnp.bitwise_xor(me[0], flip) * strip, strip, 1)
            for flip in range(groups)
        ]
        terms = [parts[:1] + [swapped(parts[flip], flip) for flip in range(1, groups)]]
        lefts = [left] + [swapped(left, flip) for flip in range(1, groups)]
        strips = left_columns(me, rows_valid, cols_valid, lefts, terms, width)
        rights = [right] + [swapped(right, flip) for flip in range(1, groups)]
    strips = [strips[0]] + [swapped(strips[flip], flip) for flip in range(1, groups)]
    return update_rows(me, rows_valid, cols_valid, rights, strips, width)


def solution(mesh):
    placed = (
        P("dp", "shard", None, None),
        P("shard", None, None),
        P("shard", None, None),
        P("shard"),
        P("shard"),
    )
    return jax.shard_map(
        on_device, mesh=mesh, in_specs=placed, out_specs=P("shard", "dp", None), check_vma=False
    )
```

```python
import functools

import jax
import jax.numpy as jnp
from jax import lax
from jax.experimental import pallas as pl
from jax.experimental.pallas import tpu as pltpu
from jax.sharding import PartitionSpec as P

TILE = 256
EXTRA = 16
VMEM = 24 * 1024 * 1024
SMEM_SPEC = pl.BlockSpec(memory_space=pltpu.SMEM)
VMEM_SPEC = pl.BlockSpec(memory_space=pltpu.VMEM)
HBM_SPEC = pl.BlockSpec(memory_space=pltpu.HBM)
BF16 = jnp.bfloat16
F32 = jnp.float32


def shifted(value, name):
    count = lax.axis_size("shard")
    with jax.named_scope(name):
        return lax.ppermute(value, "shard", [(source, (source + count // 2) % count) for source in range(count)])


def swapped(value, flip, name):
    count = lax.axis_size("dp")
    with jax.named_scope(name):
        return lax.ppermute(value, "dp", [(source, source ^ flip) for source in range(count)])


def after(value, *earlier):
    return lax.optimization_barrier((value, *earlier))[0]


def block(index):
    return pl.ds(index * TILE, TILE)


def strip_of(index, size):
    return pl.ds(pl.multiple_of(index * size, size), size)


def cost(flops, bytes_accessed):
    return pl.CostEstimate(flops=flops, bytes_accessed=bytes_accessed, transcendentals=0)


def below(tiles):
    return [(i, j) for j in range(tiles) for i in range(j + 1, tiles)]


def pick_copies(wanted, me, grad_ref, outs, sems):
    copies = []
    for parts, out in zip(wanted, outs):
        half, strip = out.shape[0] // len(parts), out.shape[1]
        for part, (flip, h) in enumerate(parts):
            source = grad_ref.at[0, 0, pl.ds(h * half, half), strip_of(jnp.bitwise_xor(me, flip), strip)]
            copies.append(
                pltpu.make_async_copy(source, out.at[pl.ds(part * half, half), :], sems.at[len(copies)])
            )
    return copies


def picked_shapes(wanted, width, groups):
    return [pltpu.VMEM((len(parts) * (width // 2), width // groups), BF16) for parts in wanted]


def pick_kernel(wanted, me_ref, grad_ref, *refs):
    copies = pick_copies(wanted, me_ref[0], grad_ref, refs[:-1], refs[-1])
    for copy in copies:
        copy.start()
    for copy in copies:
        copy.wait()


def pick(me, grads, groups, wanted):
    return pl.pallas_call(
        functools.partial(pick_kernel, wanted),
        in_specs=[SMEM_SPEC, HBM_SPEC],
        out_specs=[VMEM_SPEC] * len(wanted),
        out_shape=picked_shapes(wanted, grads.shape[-1], groups),
        scratch_shapes=[pltpu.SemaphoreType.DMA((sum(len(parts) for parts in wanted),))],
        compiler_params=pltpu.CompilerParams(vmem_limit_bytes=VMEM),
        name="pick_kept",
    )(me, grads)


def fold_copies(me, root_ref, strips, odd_corners, sems):
    tiles, strip, _ = strips.shape
    return [
        pltpu.make_async_copy(
            root_ref.at[0, pl.ds(pl.multiple_of(i * TILE + me * strip, strip), strip), :], strips.at[i], sems.at[i]
        )
        for i in range(tiles)
    ] + [
        pltpu.make_async_copy(
            root_ref.at[0, block(2 * pair + 1), block(2 * pair + 1)], odd_corners.at[pair], sems.at[tiles + pair]
        )
        for pair in range(tiles // 2)
    ]


def fold(me, strips, odd_corners, out):
    tiles, strip, _ = strips.shape
    blocks = below(tiles)
    for k, (i, j) in enumerate(blocks):
        out[pl.ds(k * strip, strip), :] = strips[i, :, block(j)]
    row = lax.broadcasted_iota(jnp.int32, (strip, TILE), 0) + me * strip
    column = lax.broadcasted_iota(jnp.int32, (strip, TILE), 1)
    on_diag = lax.broadcasted_iota(jnp.int32, (TILE, TILE), 0) == lax.broadcasted_iota(jnp.int32, (TILE, TILE), 1)
    lines = []
    for pair in range(tiles // 2):
        even, odd = 2 * pair, 2 * pair + 1
        out[pl.ds((len(blocks) + pair) * strip, strip), :] = jnp.where(
            row >= column, strips[even, :, block(even)], strips[odd, :, block(odd)]
        )
        corner = odd_corners[pair].astype(F32)
        lines.append(jnp.sum(jnp.where(on_diag, corner, 0.0), axis=0, keepdims=True))
    lines.append(jnp.zeros((EXTRA - len(lines), TILE), F32))
    out[pl.ds(tiles * tiles // 2 * strip, EXTRA), :] = jnp.concatenate(lines, axis=0).astype(BF16)


def messages_kernel(wanted, me_ref, grad_ref, left_ref, right_ref, *refs):
    outs, (left, right, strips, odd_corners, pick_sems, fold_sems) = refs[: len(wanted)], refs[len(wanted) :]
    me = me_ref[0]
    copies = pick_copies(wanted, me, grad_ref, outs, pick_sems)
    roots = [
        fold_copies(me, root, strips.at[index], odd_corners.at[index], fold_sems.at[index])
        for index, root in enumerate((left_ref, right_ref))
    ]
    for copy in roots[0] + roots[1] + copies:
        copy.start()
    for index, out in enumerate((left, right)):
        for copy in roots[index]:
            copy.wait()
        fold(me, strips.at[index], odd_corners.at[index], out)
    for copy in copies:
        copy.wait()


def messages(me, grads, left, right, groups, wanted):
    width = grads.shape[-1]
    strip, tiles = TILE // groups, width // TILE
    count = sum(len(parts) for parts in wanted)
    folded = pltpu.VMEM((tiles * tiles // 2 * strip + EXTRA, TILE), BF16)
    return pl.pallas_call(
        functools.partial(messages_kernel, wanted),
        in_specs=[SMEM_SPEC] + [HBM_SPEC] * 3,
        out_specs=[VMEM_SPEC] * (len(wanted) + 2),
        out_shape=picked_shapes(wanted, width, groups) + [folded] * 2,
        scratch_shapes=[
            pltpu.VMEM((2, tiles, strip, width), BF16),
            pltpu.VMEM((2, tiles // 2, TILE, TILE), BF16),
            pltpu.SemaphoreType.DMA((max(count, 1),)),
            pltpu.SemaphoreType.DMA((2, tiles + tiles // 2)),
        ],
        compiler_params=pltpu.CompilerParams(vmem_limit_bytes=VMEM),
        name="messages",
    )(me, grads, left, right)


def unfold(pieces, me, root, folded):
    tiles = root.shape[0] // TILE
    strip = TILE // len(pieces)
    blocks = below(tiles)
    whole = tiles * tiles // 2
    for flip, parts in enumerate(pieces):
        other = jnp.bitwise_xor(me, flip)
        each = whole // len(parts)
        for k in range(whole):
            value = parts[k // each][pl.ds(k % each * strip, strip), :]
            if k < len(blocks):
                i, j = blocks[k]
                root[pl.ds(pl.multiple_of(i * TILE + other * strip, strip), strip), block(j)] = value
            else:
                at = (k - len(blocks)) * TILE + other * strip
                folded[pl.ds(pl.multiple_of(at, strip), strip), :] = value
    row = lax.broadcasted_iota(jnp.int32, (TILE, TILE), 0)
    column = lax.broadcasted_iota(jnp.int32, (TILE, TILE), 1)
    lines = pieces[0][0][pl.ds(whole * strip, EXTRA), :].astype(F32)
    for i in range(tiles):
        value = folded[block(i // 2), :].astype(F32)
        value = jnp.where(row >= column if i % 2 == 0 else row < column, value, value.T)
        if i % 2:
            line = jnp.broadcast_to(lines[i // 2 : i // 2 + 1, :], (TILE, TILE))
            value = jnp.where(row == column, line, value)
        root[block(i), block(i)] = value.astype(BF16)
        for j in range(i):
            root[block(j), block(i)] = root[block(i), block(j)].T


def dealt(refs, counts):
    lists = []
    for count in counts:
        lists.append(refs[:count])
        refs = refs[count:]
    return lists, refs


def columns_kernel(groups, held, split, me_ref, rows_ref, cols_ref, *refs):
    pieces, refs = dealt(refs, held)
    terms, refs = dealt(refs, split)
    outs, (left, folded, masked, mixed) = refs[:groups], refs[groups:]
    me = me_ref[0]
    width, strip = masked.shape
    unfold(pieces, me, left, folded)
    part = width // len(terms)
    column = lax.broadcasted_iota(jnp.int32, (part, strip), 1) + me * strip
    row = lax.broadcasted_iota(jnp.int32, (part, strip), 0)
    for index, used in enumerate(terms):
        total = functools.reduce(lambda a, b: a + b, [term[pl.ds(0, part), :].astype(F32) for term in used])
        keep = (row + index * part < rows_ref[0]) & (column < cols_ref[0])
        masked[pl.ds(index * part, part), :] = jnp.where(keep, total, 0.0).astype(BF16)
    mixed[...] = jnp.dot(left[...], masked[...], preferred_element_type=F32).astype(BF16)
    for flip, out in enumerate(outs):
        out[...] = mixed[strip_of(jnp.bitwise_xor(me, flip), strip), :]


def left_columns(me, rows_valid, cols_valid, pieces, terms, width):
    groups = len(pieces)
    strip = width // groups
    flat = [array for part in (*pieces, *terms) for array in part]
    return pl.pallas_call(
        functools.partial(columns_kernel, groups, [len(part) for part in pieces], [len(part) for part in terms]),
        in_specs=[SMEM_SPEC] * 3 + [VMEM_SPEC] * len(flat),
        out_specs=[VMEM_SPEC] * groups,
        out_shape=[pltpu.VMEM((strip, strip), BF16)] * groups,
        scratch_shapes=[
            pltpu.VMEM((width, width), BF16),
            pltpu.VMEM((width // 2, TILE), BF16),
            pltpu.VMEM((width, strip), BF16),
            pltpu.VMEM((width, strip), BF16),
        ],
        compiler_params=pltpu.CompilerParams(vmem_limit_bytes=VMEM),
        cost_estimate=cost(2 * strip * width**2, 4 * width**2),
        name="left_columns",
    )(me, rows_valid, cols_valid, *flat)


def rows_kernel(groups, held, me_ref, rows_ref, cols_ref, *refs):
    pieces, refs = dealt(refs, held)
    strips, (out, right, folded, mixed) = refs[:groups], refs[groups:]
    me = me_ref[0]
    width = right.shape[0]
    strip = width // groups
    unfold(pieces, me, right, folded)
    if strip % 128 == 0:
        for flip, part in enumerate(strips):
            mixed[:, strip_of(jnp.bitwise_xor(me, flip), strip)] = part[...]
        value = jnp.dot(mixed[...], right[...], preferred_element_type=F32)
    else:
        value = 0.0
        for flip, part in enumerate(strips):
            rows = right[strip_of(jnp.bitwise_xor(me, flip), strip), :]
            value += jnp.dot(part[...], rows, preferred_element_type=F32)
    column = lax.broadcasted_iota(jnp.int32, (strip, width), 1)
    row = lax.broadcasted_iota(jnp.int32, (strip, width), 0) + me * strip
    out[0] = jnp.where((row < rows_ref[0]) & (column < cols_ref[0]), value, 0.0).astype(BF16)


def update_rows(me, rows_valid, cols_valid, pieces, strips, width):
    groups = len(pieces)
    strip = width // groups
    flat = [array for part in pieces for array in part]
    return pl.pallas_call(
        functools.partial(rows_kernel, groups, [len(part) for part in pieces]),
        in_specs=[SMEM_SPEC] * 3 + [VMEM_SPEC] * (len(flat) + groups),
        out_specs=VMEM_SPEC,
        out_shape=jax.ShapeDtypeStruct((1, strip, width), BF16),
        scratch_shapes=[
            pltpu.VMEM((width, width), BF16),
            pltpu.VMEM((width // 2, TILE), BF16),
            pltpu.VMEM((strip, width), BF16),
        ],
        compiler_params=pltpu.CompilerParams(vmem_limit_bytes=VMEM),
        cost_estimate=cost(2 * strip * width**2, 4 * width**2),
        name="update_rows",
    )(me, rows_valid, cols_valid, *flat, *strips)


def added(*terms):
    return functools.reduce(lambda a, b: a + b, [term.astype(F32) for term in terms])


def on_device(grads, left_roots, right_roots, rows_valid, cols_valid):
    groups = lax.axis_size("dp")
    me = lax.axis_index("dp").astype(jnp.int32).reshape(1)
    width = grads.shape[-1]
    half, strip = width // 2, width // groups
    plain = grads
    grads, left_roots, right_roots = (
        pltpu.with_memory_space_constraint(array, pltpu.HBM) for array in (grads, left_roots, right_roots)
    )

    if groups == 4:
        far_0, far_1, near_0, near_1, left, right = messages(
            me, grads, left_roots, right_roots, groups, [[(3, 0)], [(3, 1)], [(1, 0)], [(2, 1)]]
        )
        far_0, far_1 = swapped(far_0, 1, "far_0"), swapped(far_1, 2, "far_1")
        near_0, near_1 = swapped(near_0, 1, "near_0"), swapped(near_1, 2, "near_1")
        left, right = shifted(left, "left"), shifted(right, "right")
        kept = pick(me, grads, groups, [[(2, 0)], [(1, 1)], [(0, 0)], [(0, 1)]])
        via_0, via_1 = added(kept[0], far_0).astype(BF16), added(kept[1], far_1).astype(BF16)
        left = after(left, via_0, via_1, near_0, near_1)
        via_0, via_1 = swapped(via_0, 2, "via_0"), swapped(via_1, 1, "via_1")
        left_1, left_2 = swapped(left, 1, "left_1"), swapped(left, 2, "left_2")
        cut = (left.shape[0] - EXTRA) // 2
        left_3 = [
            swapped(left_1[:cut], 2, "left_3a"),
            swapped(left_2[cut : 2 * cut], 1, "left_3b"),
        ]
        strips = left_columns(
            me,
            rows_valid,
            cols_valid,
            [[left], [left_1], [left_2], left_3],
            [[kept[2], near_0, via_0], [kept[3], near_1, via_1]],
            width,
        )
        right = after(right, via_0, via_1)
        right_1, right_2 = swapped(right, 1, "right_1"), swapped(right, 2, "right_2")
        right_3 = [
            swapped(after(right_1[:cut], strips[0]), 2, "right_3a"),
            swapped(after(right_2[cut : 2 * cut], strips[0]), 1, "right_3b"),
        ]
        rights = [[right], [right_1], [right_2], right_3]
    else:
        left, right = messages(me, grads, left_roots, right_roots, groups, [])
        left, right = shifted(left, "left"), shifted(right, "right")
        parts = [
            lax.dynamic_slice_in_dim(plain[0, 0], jnp.bitwise_xor(me[0], flip) * strip, strip, 1)
            for flip in range(groups)
        ]
        terms = [parts[:1] + [swapped(parts[flip], flip, "grad") for flip in range(1, groups)]]
        lefts = [[left]] + [[swapped(left, flip, "left")] for flip in range(1, groups)]
        strips = left_columns(me, rows_valid, cols_valid, lefts, terms, width)
        rights = [[right]] + [[swapped(right, flip, "right")] for flip in range(1, groups)]
    strips = [strips[0]] + [swapped(strips[flip], flip, "strip_%d" % flip) for flip in range(1, groups)]
    return update_rows(me, rows_valid, cols_valid, rights, strips, width)


def solution(mesh):
    placed = (
        P("dp", "shard", None, None),
        P("shard", None, None),
        P("shard", None, None),
        P("shard"),
        P("shard"),
    )
    return jax.shard_map(
        on_device, mesh=mesh, in_specs=placed, out_specs=P("shard", "dp", None), check_vma=False
    )
```

```python
import functools

import jax
import jax.numpy as jnp
from jax import lax
from jax.experimental import pallas as pl
from jax.experimental.pallas import tpu as pltpu
from jax.sharding import PartitionSpec as P

TILE = 256
EXTRA = 16
VMEM = 24 * 1024 * 1024
SMEM_SPEC = pl.BlockSpec(memory_space=pltpu.SMEM)
VMEM_SPEC = pl.BlockSpec(memory_space=pltpu.VMEM)
HBM_SPEC = pl.BlockSpec(memory_space=pltpu.HBM)
BF16 = jnp.bfloat16
F32 = jnp.float32


def shifted(value, name):
    count = lax.axis_size("shard")
    with jax.named_scope(name):
        return lax.ppermute(value, "shard", [(source, (source + count // 2) % count) for source in range(count)])


def swapped(value, flip, name):
    count = lax.axis_size("dp")
    with jax.named_scope(name):
        return lax.ppermute(value, "dp", [(source, source ^ flip) for source in range(count)])


def after(value, *earlier):
    return lax.optimization_barrier((value, *earlier))[0]


def block(index):
    return pl.ds(index * TILE, TILE)


def strip_of(index, size):
    return pl.ds(pl.multiple_of(index * size, size), size)


def cost(flops, bytes_accessed):
    return pl.CostEstimate(flops=flops, bytes_accessed=bytes_accessed, transcendentals=0)


def below(tiles):
    return [(i, j) for j in range(tiles) for i in range(j + 1, tiles)]


def pick_copies(wanted, me, grad_ref, outs, sems):
    copies = []
    for parts, out in zip(wanted, outs):
        half, strip = out.shape[0] // len(parts), out.shape[1]
        for part, (flip, h) in enumerate(parts):
            source = grad_ref.at[0, 0, pl.ds(h * half, half), strip_of(jnp.bitwise_xor(me, flip), strip)]
            copies.append(
                pltpu.make_async_copy(source, out.at[pl.ds(part * half, half), :], sems.at[len(copies)])
            )
    return copies


def picked_shapes(wanted, width, groups):
    return [pltpu.VMEM((len(parts) * (width // 2), width // groups), BF16) for parts in wanted]


def pick_kernel(wanted, me_ref, grad_ref, *refs):
    copies = pick_copies(wanted, me_ref[0], grad_ref, refs[:-1], refs[-1])
    for copy in copies:
        copy.start()
    for copy in copies:
        copy.wait()


def pick(me, grads, groups, wanted):
    return pl.pallas_call(
        functools.partial(pick_kernel, wanted),
        in_specs=[SMEM_SPEC, HBM_SPEC],
        out_specs=[VMEM_SPEC] * len(wanted),
        out_shape=picked_shapes(wanted, grads.shape[-1], groups),
        scratch_shapes=[pltpu.SemaphoreType.DMA((sum(len(parts) for parts in wanted),))],
        compiler_params=pltpu.CompilerParams(vmem_limit_bytes=VMEM),
        name="pick_kept",
    )(me, grads)


def strip_copies(me, root_ref, strips, sems):
    tiles, strip, _ = strips.shape
    return [
        pltpu.make_async_copy(
            root_ref.at[0, pl.ds(pl.multiple_of(i * TILE + me * strip, strip), strip), :], strips.at[i], sems.at[i]
        )
        for i in range(tiles)
    ]


def corner_copies(root_ref, corners, sems):
    return [
        pltpu.make_async_copy(root_ref.at[0, block(i), block(i)], corners.at[i], sems.at[i])
        for i in range(corners.shape[0])
    ]


def fold_below(strips, out):
    tiles, strip, _ = strips.shape
    for k, (i, j) in enumerate(below(tiles)):
        out[pl.ds(k * strip, strip), :] = strips[i, :, block(j)]


def fold_corners(corners, start, strip, out, base):
    tiles = corners.shape[0]
    row = lax.broadcasted_iota(jnp.int32, (strip, TILE), 0) + start
    column = lax.broadcasted_iota(jnp.int32, (strip, TILE), 1)
    on_diag = lax.broadcasted_iota(jnp.int32, (TILE, TILE), 0) == lax.broadcasted_iota(jnp.int32, (TILE, TILE), 1)
    rows = pl.ds(pl.multiple_of(start, strip), strip) if strip < TILE else pl.ds(0, TILE)
    lines = []
    for pair in range(tiles // 2):
        even, odd = 2 * pair, 2 * pair + 1
        out[pl.ds(base + pair * strip, strip), :] = jnp.where(
            row >= column, corners[even, rows, :], corners[odd, rows, :]
        )
        lines.append(jnp.sum(jnp.where(on_diag, corners[odd].astype(F32), 0.0), axis=0, keepdims=True))
    lines.append(jnp.zeros((EXTRA - len(lines), TILE), F32))
    out[pl.ds(base + tiles // 2 * strip, EXTRA), :] = jnp.concatenate(lines, axis=0).astype(BF16)


def messages_kernel(wanted, me_ref, grad_ref, left_ref, right_ref, *refs):
    outs, (left, right, right_corners, strips, corners, pick_sems, strip_sems, corner_sems) = (
        refs[: len(wanted)],
        refs[len(wanted) :],
    )
    me = me_ref[0]
    tiles, strip = strips.shape[1:3]
    copies = pick_copies(wanted, me, grad_ref, outs, pick_sems)
    rooted = [
        strip_copies(me, root, strips.at[index], strip_sems.at[index])
        + corner_copies(root, corners.at[index], corner_sems.at[index])
        for index, root in enumerate((left_ref, right_ref))
    ]
    for copy in copies + rooted[0] + rooted[1]:
        copy.start()
    for copy in rooted[0] + rooted[1]:
        copy.wait()
    fold_below(strips.at[0], left)
    fold_corners(corners.at[0], me * strip, strip, left, len(below(tiles)) * strip)
    fold_below(strips.at[1], right)
    fold_corners(corners.at[1], 0, TILE, right_corners, 0)
    for copy in copies:
        copy.wait()


def messages(me, grads, left, right, groups, wanted):
    width = grads.shape[-1]
    strip, tiles = TILE // groups, width // TILE
    count = sum(len(parts) for parts in wanted)
    low = len(below(tiles)) * strip
    return pl.pallas_call(
        functools.partial(messages_kernel, wanted),
        in_specs=[SMEM_SPEC] + [HBM_SPEC] * 3,
        out_specs=[VMEM_SPEC] * (len(wanted) + 3),
        out_shape=picked_shapes(wanted, width, groups)
        + [
            pltpu.VMEM((low + tiles // 2 * strip + EXTRA, TILE), BF16),
            pltpu.VMEM((low, TILE), BF16),
            pltpu.VMEM((tiles // 2 * TILE + EXTRA, TILE), BF16),
        ],
        scratch_shapes=[
            pltpu.VMEM((2, tiles, strip, width), BF16),
            pltpu.VMEM((2, tiles, TILE, TILE), BF16),
            pltpu.SemaphoreType.DMA((max(count, 1),)),
            pltpu.SemaphoreType.DMA((2, tiles)),
            pltpu.SemaphoreType.DMA((2, tiles)),
        ],
        compiler_params=pltpu.CompilerParams(vmem_limit_bytes=VMEM),
        name="messages",
    )(me, grads, left, right)


def unfold_below(pieces, me, root):
    tiles = root.shape[0] // TILE
    strip = TILE // len(pieces)
    blocks = below(tiles)
    for flip, parts in enumerate(pieces):
        other = jnp.bitwise_xor(me, flip)
        for k, (i, j) in enumerate(blocks):
            part, row = 0, k * strip
            while row >= parts[part].shape[0]:
                row -= parts[part].shape[0]
                part += 1
            at = pl.ds(pl.multiple_of(i * TILE + other * strip, strip), strip)
            root[at, block(j)] = parts[part][pl.ds(row, strip), :]
    for i, j in blocks:
        root[block(j), block(i)] = root[block(i), block(j)].T


def unfold_corners(folded, lines, root):
    row = lax.broadcasted_iota(jnp.int32, (TILE, TILE), 0)
    column = lax.broadcasted_iota(jnp.int32, (TILE, TILE), 1)
    lines = lines.astype(F32)
    for i in range(root.shape[0] // TILE):
        value = folded[block(i // 2), :].astype(F32)
        value = jnp.where(row >= column if i % 2 == 0 else row < column, value, value.T)
        if i % 2:
            line = jnp.broadcast_to(lines[i // 2 : i // 2 + 1, :], (TILE, TILE))
            value = jnp.where(row == column, line, value)
        root[block(i), block(i)] = value.astype(BF16)


def unfold(pieces, me, root, folded):
    tiles = root.shape[0] // TILE
    strip = TILE // len(pieces)
    unfold_below(pieces, me, root)
    base = len(below(tiles)) * strip
    for flip, parts in enumerate(pieces):
        other = jnp.bitwise_xor(me, flip)
        for pair in range(tiles // 2):
            part, row = 0, base + pair * strip
            while row >= parts[part].shape[0]:
                row -= parts[part].shape[0]
                part += 1
            at = pl.ds(pl.multiple_of(pair * TILE + other * strip, strip), strip)
            folded[at, :] = parts[part][pl.ds(row, strip), :]
    unfold_corners(folded, pieces[0][0][pl.ds(base + tiles // 2 * strip, EXTRA), :], root)


def dealt(refs, counts):
    lists = []
    for count in counts:
        lists.append(refs[:count])
        refs = refs[count:]
    return lists, refs


def columns_kernel(groups, held, split, me_ref, rows_ref, cols_ref, *refs):
    pieces, refs = dealt(refs, held)
    terms, refs = dealt(refs, split)
    outs, (left, folded, masked, mixed) = refs[:groups], refs[groups:]
    me = me_ref[0]
    width, strip = masked.shape
    unfold(pieces, me, left, folded)
    part = width // len(terms)
    column = lax.broadcasted_iota(jnp.int32, (part, strip), 1) + me * strip
    row = lax.broadcasted_iota(jnp.int32, (part, strip), 0)
    for index, used in enumerate(terms):
        total = functools.reduce(lambda a, b: a + b, [term[pl.ds(0, part), :].astype(F32) for term in used])
        keep = (row + index * part < rows_ref[0]) & (column < cols_ref[0])
        masked[pl.ds(index * part, part), :] = jnp.where(keep, total, 0.0).astype(BF16)
    mixed[...] = jnp.dot(left[...], masked[...], preferred_element_type=F32).astype(BF16)
    for flip, out in enumerate(outs):
        out[...] = mixed[strip_of(jnp.bitwise_xor(me, flip), strip), :]


def left_columns(me, rows_valid, cols_valid, pieces, terms, width):
    groups = len(pieces)
    strip = width // groups
    flat = [array for part in (*pieces, *terms) for array in part]
    return pl.pallas_call(
        functools.partial(columns_kernel, groups, [len(part) for part in pieces], [len(part) for part in terms]),
        in_specs=[SMEM_SPEC] * 3 + [VMEM_SPEC] * len(flat),
        out_specs=[VMEM_SPEC] * groups,
        out_shape=[pltpu.VMEM((strip, strip), BF16)] * groups,
        scratch_shapes=[
            pltpu.VMEM((width, width), BF16),
            pltpu.VMEM((width // 2, TILE), BF16),
            pltpu.VMEM((width, strip), BF16),
            pltpu.VMEM((width, strip), BF16),
        ],
        compiler_params=pltpu.CompilerParams(vmem_limit_bytes=VMEM),
        cost_estimate=cost(2 * strip * width**2, 4 * width**2),
        name="left_columns",
    )(me, rows_valid, cols_valid, *flat)


def rows_kernel(groups, held, me_ref, rows_ref, cols_ref, corners_ref, *refs):
    pieces, refs = dealt(refs, held)
    strips, (out, right, mixed) = refs[:groups], refs[groups:]
    me = me_ref[0]
    width = right.shape[0]
    strip = width // groups
    unfold_below(pieces, me, right)
    unfold_corners(corners_ref, corners_ref[pl.ds(width // 2, EXTRA), :], right)
    if strip % 128 == 0:
        for flip, part in enumerate(strips):
            mixed[:, strip_of(jnp.bitwise_xor(me, flip), strip)] = part[...]
        value = jnp.dot(mixed[...], right[...], preferred_element_type=F32)
    else:
        value = 0.0
        for flip, part in enumerate(strips):
            rows = right[strip_of(jnp.bitwise_xor(me, flip), strip), :]
            value += jnp.dot(part[...], rows, preferred_element_type=F32)
    column = lax.broadcasted_iota(jnp.int32, (strip, width), 1)
    row = lax.broadcasted_iota(jnp.int32, (strip, width), 0) + me * strip
    out[0] = jnp.where((row < rows_ref[0]) & (column < cols_ref[0]), value, 0.0).astype(BF16)


def update_rows(me, rows_valid, cols_valid, corners, pieces, strips, width):
    groups = len(pieces)
    strip = width // groups
    flat = [array for part in pieces for array in part]
    return pl.pallas_call(
        functools.partial(rows_kernel, groups, [len(part) for part in pieces]),
        in_specs=[SMEM_SPEC] * 3 + [VMEM_SPEC] * (1 + len(flat) + groups),
        out_specs=VMEM_SPEC,
        out_shape=jax.ShapeDtypeStruct((1, strip, width), BF16),
        scratch_shapes=[
            pltpu.VMEM((width, width), BF16),
            pltpu.VMEM((strip, width), BF16),
        ],
        compiler_params=pltpu.CompilerParams(vmem_limit_bytes=VMEM),
        cost_estimate=cost(2 * strip * width**2, 4 * width**2),
        name="update_rows",
    )(me, rows_valid, cols_valid, corners, *flat, *strips)


def added(*terms):
    return functools.reduce(lambda a, b: a + b, [term.astype(F32) for term in terms])


def on_device(grads, left_roots, right_roots, rows_valid, cols_valid):
    groups = lax.axis_size("dp")
    me = lax.axis_index("dp").astype(jnp.int32).reshape(1)
    width = grads.shape[-1]
    half, strip = width // 2, width // groups
    plain = grads
    grads, left_roots, right_roots = (
        pltpu.with_memory_space_constraint(array, pltpu.HBM) for array in (grads, left_roots, right_roots)
    )

    if groups == 4:
        far_0, far_1, near_0, near_1, left, right, corners = messages(
            me, grads, left_roots, right_roots, groups, [[(3, 0)], [(3, 1)], [(1, 0)], [(2, 1)]]
        )
        far_0, far_1 = swapped(far_0, 1, "far_0"), swapped(far_1, 2, "far_1")
        near_0, near_1 = swapped(near_0, 1, "near_0"), swapped(near_1, 2, "near_1")
        left = shifted(left, "left")
        kept = pick(me, grads, groups, [[(2, 0)], [(1, 1)], [(0, 0)], [(0, 1)]])
        via_0, via_1 = added(kept[0], far_0).astype(BF16), added(kept[1], far_1).astype(BF16)
        right = shifted(after(right, left), "right")
        left = after(left, via_0, via_1, near_0, near_1)
        via_0, via_1 = swapped(via_0, 2, "via_0"), swapped(via_1, 1, "via_1")
        left_1, left_2 = swapped(after(left, via_1), 1, "left_1"), swapped(after(left, via_0), 2, "left_2")
        cut = (left.shape[0] - EXTRA) // 2
        left_3a, left_3b = left_1[:cut], left_2[cut : 2 * cut]
        tie_0, tie_1 = left_3a, left_3b = after(left_3a, via_0, via_1), after(left_3b, via_0, via_1)
        corners = shifted(after(corners, right, tie_0, tie_1), "corners")
        left_3 = [swapped(left_3a, 2, "left_3a"), swapped(left_3b, 1, "left_3b")]
        strips = left_columns(
            me,
            rows_valid,
            cols_valid,
            [[left], [left_1], [left_2], left_3],
            [[kept[2], near_0, via_0], [kept[3], near_1, via_1]],
            width,
        )
        right = after(right, via_0, via_1)
        right_1, right_2 = swapped(right, 1, "right_1"), swapped(right, 2, "right_2")
        cut = right.shape[0] // 2
        right_3 = [
            swapped(after(right_1[:cut], left), 2, "right_3a"),
            swapped(after(right_2[cut:], left), 1, "right_3b"),
        ]
        rights = [[right], [right_1], [right_2], right_3]
    else:
        left, right, corners = messages(me, grads, left_roots, right_roots, groups, [])
        left, right, corners = shifted(left, "left"), shifted(right, "right"), shifted(corners, "corners")
        parts = [
            lax.dynamic_slice_in_dim(plain[0, 0], jnp.bitwise_xor(me[0], flip) * strip, strip, 1)
            for flip in range(groups)
        ]
        terms = [parts[:1] + [swapped(parts[flip], flip, "grad") for flip in range(1, groups)]]
        lefts = [[left]] + [[swapped(left, flip, "left")] for flip in range(1, groups)]
        strips = left_columns(me, rows_valid, cols_valid, lefts, terms, width)
        rights = [[right]] + [[swapped(right, flip, "right")] for flip in range(1, groups)]
    strips = [strips[0]] + [swapped(strips[flip], flip, "strip_%d" % flip) for flip in range(1, groups)]
    return update_rows(me, rows_valid, cols_valid, corners, rights, strips, width)


def solution(mesh):
    placed = (
        P("dp", "shard", None, None),
        P("shard", None, None),
        P("shard", None, None),
        P("shard"),
        P("shard"),
    )
    return jax.shard_map(
        on_device, mesh=mesh, in_specs=placed, out_specs=P("shard", "dp", None), check_vma=False
    )
```

```python
import functools

import jax
import jax.numpy as jnp
from jax import lax
from jax.experimental import pallas as pl
from jax.experimental.pallas import tpu as pltpu
from jax.sharding import PartitionSpec as P

TILE = 256
EXTRA = 16
VMEM = 24 * 1024 * 1024
SMEM_SPEC = pl.BlockSpec(memory_space=pltpu.SMEM)
VMEM_SPEC = pl.BlockSpec(memory_space=pltpu.VMEM)
HBM_SPEC = pl.BlockSpec(memory_space=pltpu.HBM)
BF16 = jnp.bfloat16
F32 = jnp.float32


def shifted(value, name):
    count = lax.axis_size("shard")
    with jax.named_scope(name):
        return lax.ppermute(value, "shard", [(source, (source + count // 2) % count) for source in range(count)])


def swapped(value, flip, name):
    count = lax.axis_size("dp")
    with jax.named_scope(name):
        return lax.ppermute(value, "dp", [(source, source ^ flip) for source in range(count)])


def after(value, *earlier):
    return lax.optimization_barrier((value, *earlier))[0]


def block(index):
    return pl.ds(index * TILE, TILE)


def strip_of(index, size):
    return pl.ds(pl.multiple_of(index * size, size), size)


def cost(flops, bytes_accessed):
    return pl.CostEstimate(flops=flops, bytes_accessed=bytes_accessed, transcendentals=0)


def below(tiles):
    return [(i, j) for j in range(tiles) for i in range(j + 1, tiles)]


def pick_copies(wanted, me, grad_ref, outs, sems):
    copies = []
    for parts, out in zip(wanted, outs):
        half, strip = out.shape[0] // len(parts), out.shape[1]
        for part, (flip, h) in enumerate(parts):
            source = grad_ref.at[0, 0, pl.ds(h * half, half), strip_of(jnp.bitwise_xor(me, flip), strip)]
            copies.append(
                pltpu.make_async_copy(source, out.at[pl.ds(part * half, half), :], sems.at[len(copies)])
            )
    return copies


def picked_shapes(wanted, width, groups):
    return [pltpu.VMEM((len(parts) * (width // 2), width // groups), BF16) for parts in wanted]


def strip_copies(me, root_ref, strip, out, sems):
    return [
        pltpu.make_async_copy(
            root_ref.at[0, pl.ds(pl.multiple_of(i * TILE + me * strip, strip), strip), block(j)],
            out.at[pl.ds(k * strip, strip), :],
            sems.at[k],
        )
        for k, (i, j) in enumerate(below(root_ref.shape[1] // TILE))
    ]


def corner_copies(root_ref, corners, sems):
    return [
        pltpu.make_async_copy(root_ref.at[0, block(i), block(i)], corners.at[i], sems.at[i])
        for i in range(corners.shape[0])
    ]


def fold_corners(corners, start, strip, out, base):
    tiles = corners.shape[0]
    row = lax.broadcasted_iota(jnp.int32, (strip, TILE), 0) + start
    column = lax.broadcasted_iota(jnp.int32, (strip, TILE), 1)
    on_diag = lax.broadcasted_iota(jnp.int32, (TILE, TILE), 0) == lax.broadcasted_iota(jnp.int32, (TILE, TILE), 1)
    rows = pl.ds(pl.multiple_of(start, strip), strip) if strip < TILE else pl.ds(0, TILE)
    lines = []
    for pair in range(tiles // 2):
        even, odd = 2 * pair, 2 * pair + 1
        out[pl.ds(base + pair * strip, strip), :] = jnp.where(
            row >= column, corners[even, rows, :], corners[odd, rows, :]
        )
        lines.append(jnp.sum(jnp.where(on_diag, corners[odd].astype(F32), 0.0), axis=0, keepdims=True))
    lines.append(jnp.zeros((EXTRA - len(lines), TILE), F32))
    out[pl.ds(base + tiles // 2 * strip, EXTRA), :] = jnp.concatenate(lines, axis=0).astype(BF16)


def messages_kernel(wanted, quarter, me_ref, grad_ref, root_ref, *refs):
    outs, (*folded, corners, pick_sems, strip_sems, corner_sems) = refs[: len(wanted)], refs[len(wanted) :]
    me = me_ref[0]
    tiles = corners.shape[0]
    low = len(below(tiles))
    strip = quarter
    strips = strip_copies(me, root_ref, strip, folded[0], strip_sems)
    cornered = corner_copies(root_ref, corners, corner_sems)
    copies = pick_copies(wanted, me, grad_ref, outs, pick_sems)
    for copy in cornered + strips + copies:
        copy.start()
    for copy in cornered:
        copy.wait()
    if len(folded) == 1:
        fold_corners(corners, me * strip, strip, folded[0], low * strip)
    else:
        fold_corners(corners, 0, TILE, folded[1], 0)
    for copy in strips + copies:
        copy.wait()


def messages(me, grads, root, groups, wanted, apart, name):
    width = grads.shape[-1]
    strip, tiles = TILE // groups, width // TILE
    count = sum(len(parts) for parts in wanted)
    low = len(below(tiles)) * strip
    if apart:
        rows = [low, tiles // 2 * TILE + EXTRA]
    else:
        rows = [low + tiles // 2 * strip + EXTRA]
    return pl.pallas_call(
        functools.partial(messages_kernel, wanted, strip),
        in_specs=[SMEM_SPEC] + [HBM_SPEC] * 2,
        out_specs=[VMEM_SPEC] * (len(wanted) + len(rows)),
        out_shape=picked_shapes(wanted, width, groups) + [pltpu.VMEM((number, TILE), BF16) for number in rows],
        scratch_shapes=[
            pltpu.VMEM((tiles, TILE, TILE), BF16),
            pltpu.SemaphoreType.DMA((max(count, 1),)),
            pltpu.SemaphoreType.DMA((len(below(tiles)),)),
            pltpu.SemaphoreType.DMA((tiles,)),
        ],
        compiler_params=pltpu.CompilerParams(vmem_limit_bytes=VMEM),
        name=name,
    )(me, grads, root)


def unfold_below(pieces, me, root):
    tiles = root.shape[0] // TILE
    strip = TILE // len(pieces)
    blocks = below(tiles)
    for flip, parts in enumerate(pieces):
        other = jnp.bitwise_xor(me, flip)
        for k, (i, j) in enumerate(blocks):
            part, row = 0, k * strip
            while row >= parts[part].shape[0]:
                row -= parts[part].shape[0]
                part += 1
            at = pl.ds(pl.multiple_of(i * TILE + other * strip, strip), strip)
            root[at, block(j)] = parts[part][pl.ds(row, strip), :]
    for i, j in blocks:
        root[block(j), block(i)] = root[block(i), block(j)].T


def unfold_corners(folded, lines, root):
    row = lax.broadcasted_iota(jnp.int32, (TILE, TILE), 0)
    column = lax.broadcasted_iota(jnp.int32, (TILE, TILE), 1)
    lines = lines.astype(F32)
    for i in range(root.shape[0] // TILE):
        value = folded[block(i // 2), :].astype(F32)
        value = jnp.where(row >= column if i % 2 == 0 else row < column, value, value.T)
        if i % 2:
            line = jnp.broadcast_to(lines[i // 2 : i // 2 + 1, :], (TILE, TILE))
            value = jnp.where(row == column, line, value)
        root[block(i), block(i)] = value.astype(BF16)


def unfold(pieces, me, root, folded):
    tiles = root.shape[0] // TILE
    strip = TILE // len(pieces)
    unfold_below(pieces, me, root)
    base = len(below(tiles)) * strip
    for flip, parts in enumerate(pieces):
        other = jnp.bitwise_xor(me, flip)
        for pair in range(tiles // 2):
            part, row = 0, base + pair * strip
            while row >= parts[part].shape[0]:
                row -= parts[part].shape[0]
                part += 1
            at = pl.ds(pl.multiple_of(pair * TILE + other * strip, strip), strip)
            folded[at, :] = parts[part][pl.ds(row, strip), :]
    unfold_corners(folded, pieces[0][0][pl.ds(base + tiles // 2 * strip, EXTRA), :], root)


def dealt(refs, counts):
    lists = []
    for count in counts:
        lists.append(refs[:count])
        refs = refs[count:]
    return lists, refs


def columns_kernel(groups, held, split, me_ref, rows_ref, cols_ref, *refs):
    pieces, refs = dealt(refs, held)
    terms, refs = dealt(refs, split)
    out, left, folded, masked = refs
    me = me_ref[0]
    width, strip = masked.shape
    unfold(pieces, me, left, folded)
    part = width // len(terms)
    column = lax.broadcasted_iota(jnp.int32, (part, strip), 1) + me * strip
    row = lax.broadcasted_iota(jnp.int32, (part, strip), 0)
    for index, used in enumerate(terms):
        total = functools.reduce(lambda a, b: a + b, [term[pl.ds(0, part), :].astype(F32) for term in used])
        keep = (row + index * part < rows_ref[0]) & (column < cols_ref[0])
        masked[pl.ds(index * part, part), :] = jnp.where(keep, total, 0.0).astype(BF16)
    out[...] = jnp.dot(left[...], masked[...], preferred_element_type=F32).astype(BF16)


def left_columns(me, rows_valid, cols_valid, pieces, terms, width):
    groups = len(pieces)
    strip = width // groups
    flat = [array for part in (*pieces, *terms) for array in part]
    return pl.pallas_call(
        functools.partial(columns_kernel, groups, [len(part) for part in pieces], [len(part) for part in terms]),
        in_specs=[SMEM_SPEC] * 3 + [VMEM_SPEC] * len(flat),
        out_specs=VMEM_SPEC,
        out_shape=pltpu.VMEM((width, strip), BF16),
        scratch_shapes=[
            pltpu.VMEM((width, width), BF16),
            pltpu.VMEM((width // 2, TILE), BF16),
            pltpu.VMEM((width, strip), BF16),
        ],
        compiler_params=pltpu.CompilerParams(vmem_limit_bytes=VMEM),
        cost_estimate=cost(2 * strip * width**2, 4 * width**2),
        name="left_columns",
    )(me, rows_valid, cols_valid, *flat)


def whole_right_kernel(held, me_ref, corners_ref, *refs):
    pieces, (right,) = dealt(refs, held)
    unfold_below(pieces, me_ref[0], right)
    unfold_corners(corners_ref, corners_ref[pl.ds(right.shape[0] // 2, EXTRA), :], right)


def whole_right(me, corners, pieces, width):
    flat = [array for part in pieces for array in part]
    return pl.pallas_call(
        functools.partial(whole_right_kernel, [len(part) for part in pieces]),
        in_specs=[SMEM_SPEC] + [VMEM_SPEC] * (1 + len(flat)),
        out_specs=VMEM_SPEC,
        out_shape=pltpu.VMEM((width, width), BF16),
        compiler_params=pltpu.CompilerParams(vmem_limit_bytes=VMEM),
        cost_estimate=cost(width**2, 4 * width**2),
        name="whole_right",
    )(me, corners, *flat)


def rows_kernel(me_ref, rows_ref, cols_ref, strips_ref, right, out, mixed):
    groups, strip, _ = strips_ref.shape
    width = right.shape[0]
    for k in range(groups):
        mixed[:, pl.ds(k * strip, strip)] = strips_ref[k]
    value = jnp.dot(mixed[...], right[...], preferred_element_type=F32)
    column = lax.broadcasted_iota(jnp.int32, (strip, width), 1)
    row = lax.broadcasted_iota(jnp.int32, (strip, width), 0) + me_ref[0] * strip
    out[0] = jnp.where((row < rows_ref[0]) & (column < cols_ref[0]), value, 0.0).astype(BF16)


def update_rows(me, rows_valid, cols_valid, strips, right):
    width = right.shape[0]
    strip = strips.shape[1]
    return pl.pallas_call(
        rows_kernel,
        in_specs=[SMEM_SPEC] * 3 + [VMEM_SPEC] * 2,
        out_specs=VMEM_SPEC,
        out_shape=jax.ShapeDtypeStruct((1, strip, width), BF16),
        scratch_shapes=[pltpu.VMEM((strip, width), BF16)],
        compiler_params=pltpu.CompilerParams(vmem_limit_bytes=VMEM),
        cost_estimate=cost(2 * strip * width**2, 4 * width**2),
        name="update_rows",
    )(me, rows_valid, cols_valid, strips, right)


def added(*terms):
    return functools.reduce(lambda a, b: a + b, [term.astype(F32) for term in terms])


def on_device(grads, left_roots, right_roots, rows_valid, cols_valid):
    groups = lax.axis_size("dp")
    me = lax.axis_index("dp").astype(jnp.int32).reshape(1)
    width = grads.shape[-1]
    half, strip = width // 2, width // groups
    plain = grads
    grads, left_roots, right_roots = (
        pltpu.with_memory_space_constraint(array, pltpu.HBM) for array in (grads, left_roots, right_roots)
    )

    if groups == 4:
        far_0, far_1, near_0, near_1, left = messages(
            me, grads, left_roots, groups, [[(3, 0)], [(3, 1)], [(1, 0)], [(2, 1)]], False, "sent_first"
        )
        far_0, far_1 = swapped(far_0, 1, "far_0"), swapped(far_1, 2, "far_1")
        near_0, near_1 = swapped(near_0, 1, "near_0"), swapped(near_1, 2, "near_1")
        left = shifted(left, "left")
        *kept, right, corners = messages(
            me, grads, right_roots, groups, [[(2, 0)], [(1, 1)], [(0, 0)], [(0, 1)]], True, "sent_later"
        )
        via_0, via_1 = added(kept[0], far_0).astype(BF16), added(kept[1], far_1).astype(BF16)
        right = shifted(after(right, left), "right")
        left = after(left, via_0, via_1, near_0, near_1)
        via_0, via_1 = swapped(via_0, 2, "via_0"), swapped(via_1, 1, "via_1")
        left_1, left_2 = swapped(left, 1, "left_1"), swapped(left, 2, "left_2")
        cut = (left.shape[0] - EXTRA) // 2
        left_3a, left_3b = left_1[:cut], left_2[cut : 2 * cut]
        corners = shifted(after(corners, right, left_3a, left_3b), "corners")
        left_3 = [swapped(left_3a, 2, "left_3a"), swapped(left_3b, 1, "left_3b")]
        mixed = left_columns(
            me,
            rows_valid,
            cols_valid,
            [[left], [left_1], [left_2], left_3],
            [[kept[2], near_0, via_0], [kept[3], near_1, via_1]],
            width,
        )
        right = after(right, via_0, via_1)
        right_1, right_2 = swapped(right, 1, "right_1"), swapped(right, 2, "right_2")
        cut = right.shape[0] // 2
        right_3 = [swapped(right_1[:cut], 2, "right_3a"), swapped(right_2[cut:], 1, "right_3b")]
        rights = [[right], [right_1], [right_2], right_3]
    else:
        (left,) = messages(me, grads, left_roots, groups, [], False, "sent_first")
        right, corners = messages(me, grads, right_roots, groups, [], True, "sent_later")
        left, right, corners = shifted(left, "left"), shifted(right, "right"), shifted(corners, "corners")
        parts = [
            lax.dynamic_slice_in_dim(plain[0, 0], jnp.bitwise_xor(me[0], flip) * strip, strip, 1)
            for flip in range(groups)
        ]
        terms = [parts[:1] + [swapped(parts[flip], flip, "grad") for flip in range(1, groups)]]
        lefts = [[left]] + [[swapped(left, flip, "left")] for flip in range(1, groups)]
        mixed = left_columns(me, rows_valid, cols_valid, lefts, terms, width)
        rights = [[right]] + [[swapped(right, flip, "right")] for flip in range(1, groups)]
    whole = whole_right(me, corners, rights, width)
    with jax.named_scope("strips"):
        strips = lax.all_to_all(mixed.reshape(groups, strip, strip), "dp", 0, 0)
    return update_rows(me, rows_valid, cols_valid, strips, whole)


def solution(mesh):
    placed = (
        P("dp", "shard", None, None),
        P("shard", None, None),
        P("shard", None, None),
        P("shard"),
        P("shard"),
    )
    return jax.shard_map(
        on_device, mesh=mesh, in_specs=placed, out_specs=P("shard", "dp", None), check_vma=False
    )
```

```python
import functools

import jax
import jax.numpy as jnp
from jax import lax
from jax.experimental import pallas as pl
from jax.experimental.pallas import tpu as pltpu
from jax.sharding import PartitionSpec as P

TILE = 256
EXTRA = 16
VMEM = 24 * 1024 * 1024
SMEM_SPEC = pl.BlockSpec(memory_space=pltpu.SMEM)
VMEM_SPEC = pl.BlockSpec(memory_space=pltpu.VMEM)
HBM_SPEC = pl.BlockSpec(memory_space=pltpu.HBM)
BF16 = jnp.bfloat16
F32 = jnp.float32


def shifted(value, name):
    count = lax.axis_size("shard")
    with jax.named_scope(name):
        return lax.ppermute(value, "shard", [(source, (source + count // 2) % count) for source in range(count)])


def swapped(value, flip, name):
    count = lax.axis_size("dp")
    with jax.named_scope(name):
        return lax.ppermute(value, "dp", [(source, source ^ flip) for source in range(count)])


def after(value, *earlier):
    return lax.optimization_barrier((value, *earlier))[0]


def block(index):
    return pl.ds(index * TILE, TILE)


def strip_of(index, size):
    return pl.ds(pl.multiple_of(index * size, size), size)


def cost(flops, bytes_accessed):
    return pl.CostEstimate(flops=flops, bytes_accessed=bytes_accessed, transcendentals=0)


def below(tiles):
    return [(i, j) for j in range(tiles) for i in range(j + 1, tiles)]


def pick_copies(wanted, me, grad_ref, outs, sems):
    copies = []
    for parts, out in zip(wanted, outs):
        half, strip = out.shape[0] // len(parts), out.shape[1]
        for part, (flip, h) in enumerate(parts):
            source = grad_ref.at[0, 0, pl.ds(h * half, half), strip_of(jnp.bitwise_xor(me, flip), strip)]
            copies.append(
                pltpu.make_async_copy(source, out.at[pl.ds(part * half, half), :], sems.at[len(copies)])
            )
    return copies


def picked_shapes(wanted, width, groups):
    return [pltpu.VMEM((len(parts) * (width // 2), width // groups), BF16) for parts in wanted]


def strip_copies(me, root_ref, strip, out, sems):
    return [
        pltpu.make_async_copy(
            root_ref.at[0, pl.ds(pl.multiple_of(i * TILE + me * strip, strip), strip), block(j)],
            out.at[pl.ds(k * strip, strip), :],
            sems.at[k],
        )
        for k, (i, j) in enumerate(below(root_ref.shape[1] // TILE))
    ]


def corner_copies(root_ref, corners, sems):
    return [
        pltpu.make_async_copy(root_ref.at[0, block(i), block(i)], corners.at[i], sems.at[i])
        for i in range(corners.shape[0])
    ]


def fold_corners(corners, start, strip, out, base):
    tiles = corners.shape[0]
    row = lax.broadcasted_iota(jnp.int32, (strip, TILE), 0) + start
    column = lax.broadcasted_iota(jnp.int32, (strip, TILE), 1)
    on_diag = lax.broadcasted_iota(jnp.int32, (TILE, TILE), 0) == lax.broadcasted_iota(jnp.int32, (TILE, TILE), 1)
    rows = pl.ds(pl.multiple_of(start, strip), strip) if strip < TILE else pl.ds(0, TILE)
    lines = []
    for pair in range(tiles // 2):
        even, odd = 2 * pair, 2 * pair + 1
        out[pl.ds(base + pair * strip, strip), :] = jnp.where(
            row >= column, corners[even, rows, :], corners[odd, rows, :]
        )
        lines.append(jnp.sum(jnp.where(on_diag, corners[odd].astype(F32), 0.0), axis=0, keepdims=True))
    lines.append(jnp.zeros((EXTRA - len(lines), TILE), F32))
    out[pl.ds(base + tiles // 2 * strip, EXTRA), :] = jnp.concatenate(lines, axis=0).astype(BF16)


def messages_kernel(wanted, quarter, me_ref, grad_ref, root_ref, *refs):
    outs, (*folded, corners, pick_sems, strip_sems, corner_sems) = refs[: len(wanted)], refs[len(wanted) :]
    me = me_ref[0]
    tiles = corners.shape[0]
    low = len(below(tiles))
    strip = quarter
    strips = strip_copies(me, root_ref, strip, folded[0], strip_sems)
    cornered = corner_copies(root_ref, corners, corner_sems)
    copies = pick_copies(wanted, me, grad_ref, outs, pick_sems)
    for copy in cornered + strips + copies:
        copy.start()
    for copy in cornered:
        copy.wait()
    if len(folded) == 1:
        fold_corners(corners, me * strip, strip, folded[0], low * strip)
    else:
        fold_corners(corners, 0, TILE, folded[1], 0)
    for copy in strips + copies:
        copy.wait()


def messages(me, grads, root, groups, wanted, apart, name):
    width = grads.shape[-1]
    strip, tiles = TILE // groups, width // TILE
    count = sum(len(parts) for parts in wanted)
    low = len(below(tiles)) * strip
    if apart:
        rows = [low, tiles // 2 * TILE + EXTRA]
    else:
        rows = [low + tiles // 2 * strip + EXTRA]
    return pl.pallas_call(
        functools.partial(messages_kernel, wanted, strip),
        in_specs=[SMEM_SPEC] + [HBM_SPEC] * 2,
        out_specs=[VMEM_SPEC] * (len(wanted) + len(rows)),
        out_shape=picked_shapes(wanted, width, groups) + [pltpu.VMEM((number, TILE), BF16) for number in rows],
        scratch_shapes=[
            pltpu.VMEM((tiles, TILE, TILE), BF16),
            pltpu.SemaphoreType.DMA((max(count, 1),)),
            pltpu.SemaphoreType.DMA((len(below(tiles)),)),
            pltpu.SemaphoreType.DMA((tiles,)),
        ],
        compiler_params=pltpu.CompilerParams(vmem_limit_bytes=VMEM),
        name=name,
    )(me, grads, root)


def unfold_below(pieces, me, root):
    tiles = root.shape[0] // TILE
    strip = TILE // len(pieces)
    blocks = below(tiles)
    for flip, parts in enumerate(pieces):
        other = jnp.bitwise_xor(me, flip)
        for k, (i, j) in enumerate(blocks):
            part, row = 0, k * strip
            while row >= parts[part].shape[0]:
                row -= parts[part].shape[0]
                part += 1
            at = pl.ds(pl.multiple_of(i * TILE + other * strip, strip), strip)
            root[at, block(j)] = parts[part][pl.ds(row, strip), :]
    for i, j in blocks:
        root[block(j), block(i)] = root[block(i), block(j)].T


def unfold_corners(folded, lines, root):
    row = lax.broadcasted_iota(jnp.int32, (TILE, TILE), 0)
    column = lax.broadcasted_iota(jnp.int32, (TILE, TILE), 1)
    lines = lines.astype(F32)
    for i in range(root.shape[0] // TILE):
        value = folded[block(i // 2), :].astype(F32)
        value = jnp.where(row >= column if i % 2 == 0 else row < column, value, value.T)
        if i % 2:
            line = jnp.broadcast_to(lines[i // 2 : i // 2 + 1, :], (TILE, TILE))
            value = jnp.where(row == column, line, value)
        root[block(i), block(i)] = value.astype(BF16)


def unfold(pieces, me, root, folded):
    tiles = root.shape[0] // TILE
    strip = TILE // len(pieces)
    unfold_below(pieces, me, root)
    base = len(below(tiles)) * strip
    for flip, parts in enumerate(pieces):
        other = jnp.bitwise_xor(me, flip)
        for pair in range(tiles // 2):
            part, row = 0, base + pair * strip
            while row >= parts[part].shape[0]:
                row -= parts[part].shape[0]
                part += 1
            at = pl.ds(pl.multiple_of(pair * TILE + other * strip, strip), strip)
            folded[at, :] = parts[part][pl.ds(row, strip), :]
    unfold_corners(folded, pieces[0][0][pl.ds(base + tiles // 2 * strip, EXTRA), :], root)


def dealt(refs, counts):
    lists = []
    for count in counts:
        lists.append(refs[:count])
        refs = refs[count:]
    return lists, refs


def columns_kernel(groups, held, split, me_ref, rows_ref, cols_ref, *refs):
    pieces, refs = dealt(refs, held)
    terms, refs = dealt(refs, split)
    outs, (left, folded, masked, mixed) = refs[:groups], refs[groups:]
    me = me_ref[0]
    width, strip = masked.shape
    unfold(pieces, me, left, folded)
    part = width // len(terms)
    column = lax.broadcasted_iota(jnp.int32, (part, strip), 1) + me * strip
    row = lax.broadcasted_iota(jnp.int32, (part, strip), 0)
    for index, used in enumerate(terms):
        total = functools.reduce(lambda a, b: a + b, [term[pl.ds(0, part), :].astype(F32) for term in used])
        keep = (row + index * part < rows_ref[0]) & (column < cols_ref[0])
        masked[pl.ds(index * part, part), :] = jnp.where(keep, total, 0.0).astype(BF16)
    mixed[...] = jnp.dot(left[...], masked[...], preferred_element_type=F32).astype(BF16)
    for flip, out in enumerate(outs):
        out[...] = mixed[strip_of(jnp.bitwise_xor(me, flip), strip), :]


def left_columns(me, rows_valid, cols_valid, pieces, terms, width):
    groups = len(pieces)
    strip = width // groups
    flat = [array for part in (*pieces, *terms) for array in part]
    return pl.pallas_call(
        functools.partial(columns_kernel, groups, [len(part) for part in pieces], [len(part) for part in terms]),
        in_specs=[SMEM_SPEC] * 3 + [VMEM_SPEC] * len(flat),
        out_specs=[VMEM_SPEC] * groups,
        out_shape=[pltpu.VMEM((strip, strip), BF16)] * groups,
        scratch_shapes=[
            pltpu.VMEM((width, width), BF16),
            pltpu.VMEM((width // 2, TILE), BF16),
            pltpu.VMEM((width, strip), BF16),
            pltpu.VMEM((width, strip), BF16),
        ],
        compiler_params=pltpu.CompilerParams(vmem_limit_bytes=VMEM),
        cost_estimate=cost(2 * strip * width**2, 4 * width**2),
        name="left_columns",
    )(me, rows_valid, cols_valid, *flat)


def whole_right_kernel(held, me_ref, corners_ref, *refs):
    pieces, (right,) = dealt(refs, held)
    unfold_below(pieces, me_ref[0], right)
    unfold_corners(corners_ref, corners_ref[pl.ds(right.shape[0] // 2, EXTRA), :], right)


def whole_right(me, corners, pieces, width):
    flat = [array for part in pieces for array in part]
    return pl.pallas_call(
        functools.partial(whole_right_kernel, [len(part) for part in pieces]),
        in_specs=[SMEM_SPEC] + [VMEM_SPEC] * (1 + len(flat)),
        out_specs=VMEM_SPEC,
        out_shape=pltpu.VMEM((width, width), BF16),
        compiler_params=pltpu.CompilerParams(vmem_limit_bytes=VMEM),
        cost_estimate=cost(width**2, 4 * width**2),
        name="whole_right",
    )(me, corners, *flat)


def rows_kernel(groups, me_ref, rows_ref, cols_ref, *refs):
    strips, (right, out, mixed) = refs[:groups], refs[groups:]
    me = me_ref[0]
    strip, width = mixed.shape
    if strip % 128 == 0:
        for flip, part in enumerate(strips):
            mixed[:, strip_of(jnp.bitwise_xor(me, flip), strip)] = part[...]
        value = jnp.dot(mixed[...], right[...], preferred_element_type=F32)
    else:
        value = 0.0
        for flip, part in enumerate(strips):
            rows = right[strip_of(jnp.bitwise_xor(me, flip), strip), :]
            value += jnp.dot(part[...], rows, preferred_element_type=F32)
    column = lax.broadcasted_iota(jnp.int32, (strip, width), 1)
    row = lax.broadcasted_iota(jnp.int32, (strip, width), 0) + me * strip
    out[0] = jnp.where((row < rows_ref[0]) & (column < cols_ref[0]), value, 0.0).astype(BF16)


def update_rows(me, rows_valid, cols_valid, strips, right):
    width = right.shape[0]
    groups, strip = len(strips), strips[0].shape[0]
    return pl.pallas_call(
        functools.partial(rows_kernel, groups),
        in_specs=[SMEM_SPEC] * 3 + [VMEM_SPEC] * (groups + 1),
        out_specs=VMEM_SPEC,
        out_shape=jax.ShapeDtypeStruct((1, strip, width), BF16),
        scratch_shapes=[pltpu.VMEM((strip, width), BF16)],
        compiler_params=pltpu.CompilerParams(vmem_limit_bytes=VMEM),
        cost_estimate=cost(2 * strip * width**2, 4 * width**2),
        name="update_rows",
    )(me, rows_valid, cols_valid, *strips, right)


def added(*terms):
    return functools.reduce(lambda a, b: a + b, [term.astype(F32) for term in terms])


def on_device(grads, left_roots, right_roots, rows_valid, cols_valid):
    groups = lax.axis_size("dp")
    me = lax.axis_index("dp").astype(jnp.int32).reshape(1)
    width = grads.shape[-1]
    half, strip = width // 2, width // groups
    plain = grads
    grads, left_roots, right_roots = (
        pltpu.with_memory_space_constraint(array, pltpu.HBM) for array in (grads, left_roots, right_roots)
    )

    if groups == 4:
        far_0, far_1, near_0, near_1, left = messages(
            me, grads, left_roots, groups, [[(3, 0)], [(3, 1)], [(1, 0)], [(2, 1)]], False, "sent_first"
        )
        far_0, far_1 = swapped(far_0, 1, "far_0"), swapped(far_1, 2, "far_1")
        near_0, near_1 = swapped(near_0, 1, "near_0"), swapped(near_1, 2, "near_1")
        left = shifted(left, "left")
        *kept, right, corners = messages(
            me, grads, right_roots, groups, [[(2, 0)], [(1, 1)], [(0, 0)], [(0, 1)]], True, "sent_later"
        )
        via_0, via_1 = added(kept[0], far_0).astype(BF16), added(kept[1], far_1).astype(BF16)
        right = shifted(after(right, left), "right")
        left = after(left, via_0, via_1, near_0, near_1)
        via_0, via_1 = swapped(via_0, 2, "via_0"), swapped(via_1, 1, "via_1")
        left_1, left_2 = swapped(left, 1, "left_1"), swapped(after(left, via_0), 2, "left_2")
        cut = (left.shape[0] - EXTRA) // 2
        left_3a, left_3b = left_1[:cut], left_2[cut : 2 * cut]
        corners = shifted(after(corners, right, left_3a, left_3b), "corners")
        left_3 = [swapped(left_3a, 2, "left_3a"), swapped(left_3b, 1, "left_3b")]
        mixed = left_columns(
            me,
            rows_valid,
            cols_valid,
            [[left], [left_1], [left_2], left_3],
            [[kept[2], near_0, via_0], [kept[3], near_1, via_1]],
            width,
        )
        right = after(right, via_0, via_1)
        right_1, right_2 = swapped(right, 1, "right_1"), swapped(right, 2, "right_2")
        cut = right.shape[0] // 2
        right_3 = [swapped(right_1[:cut], 2, "right_3a"), swapped(right_2[cut:], 1, "right_3b")]
        rights = [[right], [right_1], [right_2], right_3]
    else:
        (left,) = messages(me, grads, left_roots, groups, [], False, "sent_first")
        right, corners = messages(me, grads, right_roots, groups, [], True, "sent_later")
        left, right, corners = shifted(left, "left"), shifted(right, "right"), shifted(corners, "corners")
        parts = [
            lax.dynamic_slice_in_dim(plain[0, 0], jnp.bitwise_xor(me[0], flip) * strip, strip, 1)
            for flip in range(groups)
        ]
        terms = [parts[:1] + [swapped(parts[flip], flip, "grad") for flip in range(1, groups)]]
        lefts = [[left]] + [[swapped(left, flip, "left")] for flip in range(1, groups)]
        mixed = left_columns(me, rows_valid, cols_valid, lefts, terms, width)
        rights = [[right]] + [[swapped(right, flip, "right")] for flip in range(1, groups)]
    whole = whole_right(me, corners, rights, width)
    strips = [mixed[0]] + [swapped(mixed[flip], flip, "strip_%d" % flip) for flip in range(1, groups)]
    return update_rows(me, rows_valid, cols_valid, strips, whole)


def solution(mesh):
    placed = (
        P("dp", "shard", None, None),
        P("shard", None, None),
        P("shard", None, None),
        P("shard"),
        P("shard"),
    )
    return jax.shard_map(
        on_device, mesh=mesh, in_specs=placed, out_specs=P("shard", "dp", None), check_vma=False
    )
```

```python
import functools

import jax
import jax.numpy as jnp
from jax import lax
from jax.experimental import pallas as pl
from jax.experimental.pallas import tpu as pltpu
from jax.sharding import PartitionSpec as P

TILE = 256
EXTRA = 16
VMEM = 24 * 1024 * 1024
SMEM_SPEC = pl.BlockSpec(memory_space=pltpu.SMEM)
VMEM_SPEC = pl.BlockSpec(memory_space=pltpu.VMEM)
HBM_SPEC = pl.BlockSpec(memory_space=pltpu.HBM)
BF16 = jnp.bfloat16
F32 = jnp.float32


def shifted(value, name):
    count = lax.axis_size("shard")
    with jax.named_scope(name):
        return lax.ppermute(value, "shard", [(source, (source + count // 2) % count) for source in range(count)])


def swapped(value, flip, name):
    count = lax.axis_size("dp")
    with jax.named_scope(name):
        return lax.ppermute(value, "dp", [(source, source ^ flip) for source in range(count)])


def after(value, *earlier):
    return lax.optimization_barrier((value, *earlier))[0]


def block(index):
    return pl.ds(index * TILE, TILE)


def strip_of(index, size):
    return pl.ds(pl.multiple_of(index * size, size), size)


def cost(flops, bytes_accessed):
    return pl.CostEstimate(flops=flops, bytes_accessed=bytes_accessed, transcendentals=0)


def below(tiles):
    return [(i, j) for j in range(tiles) for i in range(j + 1, tiles)]


def pick_copies(wanted, me, grad_ref, outs, sems):
    copies = []
    for parts, out in zip(wanted, outs):
        half, strip = out.shape[0] // len(parts), out.shape[1]
        for part, (flip, h) in enumerate(parts):
            source = grad_ref.at[0, 0, pl.ds(h * half, half), strip_of(jnp.bitwise_xor(me, flip), strip)]
            copies.append(
                pltpu.make_async_copy(source, out.at[pl.ds(part * half, half), :], sems.at[len(copies)])
            )
    return copies


def picked_shapes(wanted, width, groups):
    return [pltpu.VMEM((len(parts) * (width // 2), width // groups), BF16) for parts in wanted]


def strip_copies(me, root_ref, strip, out, sems):
    return [
        pltpu.make_async_copy(
            root_ref.at[0, pl.ds(pl.multiple_of(i * TILE + me * strip, strip), strip), block(j)],
            out.at[pl.ds(k * strip, strip), :],
            sems.at[k],
        )
        for k, (i, j) in enumerate(below(root_ref.shape[1] // TILE))
    ]


def corner_copies(root_ref, corners, sems):
    return [
        pltpu.make_async_copy(root_ref.at[0, block(i), block(i)], corners.at[i], sems.at[i])
        for i in range(corners.shape[0])
    ]


def fold_corners(corners, start, strip, out, base):
    tiles = corners.shape[0]
    row = lax.broadcasted_iota(jnp.int32, (strip, TILE), 0) + start
    column = lax.broadcasted_iota(jnp.int32, (strip, TILE), 1)
    on_diag = lax.broadcasted_iota(jnp.int32, (TILE, TILE), 0) == lax.broadcasted_iota(jnp.int32, (TILE, TILE), 1)
    rows = pl.ds(pl.multiple_of(start, strip), strip) if strip < TILE else pl.ds(0, TILE)
    lines = []
    for pair in range(tiles // 2):
        even, odd = 2 * pair, 2 * pair + 1
        out[pl.ds(base + pair * strip, strip), :] = jnp.where(
            row >= column, corners[even, rows, :], corners[odd, rows, :]
        )
        lines.append(jnp.sum(jnp.where(on_diag, corners[odd].astype(F32), 0.0), axis=0, keepdims=True))
    lines.append(jnp.zeros((EXTRA - len(lines), TILE), F32))
    out[pl.ds(base + tiles // 2 * strip, EXTRA), :] = jnp.concatenate(lines, axis=0).astype(BF16)


def messages_kernel(wanted, quarter, me_ref, grad_ref, root_ref, *refs):
    outs, (*folded, corners, pick_sems, strip_sems, corner_sems) = refs[: len(wanted)], refs[len(wanted) :]
    me = me_ref[0]
    tiles = corners.shape[0]
    low = len(below(tiles))
    strip = quarter
    strips = strip_copies(me, root_ref, strip, folded[0], strip_sems)
    cornered = corner_copies(root_ref, corners, corner_sems)
    copies = pick_copies(wanted, me, grad_ref, outs, pick_sems)
    for copy in cornered + strips + copies:
        copy.start()
    for copy in cornered:
        copy.wait()
    if len(folded) == 1:
        fold_corners(corners, me * strip, strip, folded[0], low * strip)
    else:
        fold_corners(corners, 0, TILE, folded[1], 0)
    for copy in strips + copies:
        copy.wait()


def messages(me, grads, root, groups, wanted, apart, name):
    width = grads.shape[-1]
    strip, tiles = TILE // groups, width // TILE
    count = sum(len(parts) for parts in wanted)
    low = len(below(tiles)) * strip
    if apart:
        rows = [low, tiles // 2 * TILE + EXTRA]
    else:
        rows = [low + tiles // 2 * strip + EXTRA]
    return pl.pallas_call(
        functools.partial(messages_kernel, wanted, strip),
        in_specs=[SMEM_SPEC] + [HBM_SPEC] * 2,
        out_specs=[VMEM_SPEC] * (len(wanted) + len(rows)),
        out_shape=picked_shapes(wanted, width, groups) + [pltpu.VMEM((number, TILE), BF16) for number in rows],
        scratch_shapes=[
            pltpu.VMEM((tiles, TILE, TILE), BF16),
            pltpu.SemaphoreType.DMA((max(count, 1),)),
            pltpu.SemaphoreType.DMA((len(below(tiles)),)),
            pltpu.SemaphoreType.DMA((tiles,)),
        ],
        compiler_params=pltpu.CompilerParams(vmem_limit_bytes=VMEM),
        name=name,
    )(me, grads, root)


def unfold_below(pieces, me, root):
    tiles = root.shape[0] // TILE
    strip = TILE // len(pieces)
    blocks = below(tiles)
    for flip, parts in enumerate(pieces):
        other = jnp.bitwise_xor(me, flip)
        for k, (i, j) in enumerate(blocks):
            part, row = 0, k * strip
            while row >= parts[part].shape[0]:
                row -= parts[part].shape[0]
                part += 1
            at = pl.ds(pl.multiple_of(i * TILE + other * strip, strip), strip)
            root[at, block(j)] = parts[part][pl.ds(row, strip), :]
    for i, j in blocks:
        root[block(j), block(i)] = root[block(i), block(j)].T


def unfold_corners(folded, lines, root):
    row = lax.broadcasted_iota(jnp.int32, (TILE, TILE), 0)
    column = lax.broadcasted_iota(jnp.int32, (TILE, TILE), 1)
    lines = lines.astype(F32)
    for i in range(root.shape[0] // TILE):
        value = folded[block(i // 2), :].astype(F32)
        value = jnp.where(row >= column if i % 2 == 0 else row < column, value, value.T)
        if i % 2:
            line = jnp.broadcast_to(lines[i // 2 : i // 2 + 1, :], (TILE, TILE))
            value = jnp.where(row == column, line, value)
        root[block(i), block(i)] = value.astype(BF16)


def unfold(pieces, me, root, folded):
    tiles = root.shape[0] // TILE
    strip = TILE // len(pieces)
    unfold_below(pieces, me, root)
    base = len(below(tiles)) * strip
    for flip, parts in enumerate(pieces):
        other = jnp.bitwise_xor(me, flip)
        for pair in range(tiles // 2):
            part, row = 0, base + pair * strip
            while row >= parts[part].shape[0]:
                row -= parts[part].shape[0]
                part += 1
            at = pl.ds(pl.multiple_of(pair * TILE + other * strip, strip), strip)
            folded[at, :] = parts[part][pl.ds(row, strip), :]
    unfold_corners(folded, pieces[0][0][pl.ds(base + tiles // 2 * strip, EXTRA), :], root)


def dealt(refs, counts):
    lists = []
    for count in counts:
        lists.append(refs[:count])
        refs = refs[count:]
    return lists, refs


def columns_kernel(groups, held, split, me_ref, rows_ref, cols_ref, *refs):
    pieces, refs = dealt(refs, held)
    terms, refs = dealt(refs, split)
    outs, (left, folded, masked, mixed) = refs[:groups], refs[groups:]
    me = me_ref[0]
    width, strip = masked.shape
    unfold(pieces, me, left, folded)
    part = width // len(terms)
    column = lax.broadcasted_iota(jnp.int32, (part, strip), 1) + me * strip
    row = lax.broadcasted_iota(jnp.int32, (part, strip), 0)
    for index, used in enumerate(terms):
        total = functools.reduce(lambda a, b: a + b, [term[pl.ds(0, part), :].astype(F32) for term in used])
        keep = (row + index * part < rows_ref[0]) & (column < cols_ref[0])
        masked[pl.ds(index * part, part), :] = jnp.where(keep, total, 0.0).astype(BF16)
    mixed[...] = jnp.dot(left[...], masked[...], preferred_element_type=F32).astype(BF16)
    for flip, out in enumerate(outs):
        out[...] = mixed[strip_of(jnp.bitwise_xor(me, flip), strip), :]


def left_columns(me, rows_valid, cols_valid, pieces, terms, width):
    groups = len(pieces)
    strip = width // groups
    flat = [array for part in (*pieces, *terms) for array in part]
    return pl.pallas_call(
        functools.partial(columns_kernel, groups, [len(part) for part in pieces], [len(part) for part in terms]),
        in_specs=[SMEM_SPEC] * 3 + [VMEM_SPEC] * len(flat),
        out_specs=[VMEM_SPEC] * groups,
        out_shape=[pltpu.VMEM((strip, strip), BF16)] * groups,
        scratch_shapes=[
            pltpu.VMEM((width, width), BF16),
            pltpu.VMEM((width // 2, TILE), BF16),
            pltpu.VMEM((width, strip), BF16),
            pltpu.VMEM((width, strip), BF16),
        ],
        compiler_params=pltpu.CompilerParams(vmem_limit_bytes=VMEM),
        cost_estimate=cost(2 * strip * width**2, 4 * width**2),
        name="left_columns",
    )(me, rows_valid, cols_valid, *flat)


def whole_right_kernel(held, me_ref, corners_ref, *refs):
    pieces, (right,) = dealt(refs, held)
    unfold_below(pieces, me_ref[0], right)
    unfold_corners(corners_ref, corners_ref[pl.ds(right.shape[0] // 2, EXTRA), :], right)


def whole_right(me, corners, pieces, width):
    flat = [array for part in pieces for array in part]
    return pl.pallas_call(
        functools.partial(whole_right_kernel, [len(part) for part in pieces]),
        in_specs=[SMEM_SPEC] + [VMEM_SPEC] * (1 + len(flat)),
        out_specs=VMEM_SPEC,
        out_shape=pltpu.VMEM((width, width), BF16),
        compiler_params=pltpu.CompilerParams(vmem_limit_bytes=VMEM),
        cost_estimate=cost(width**2, 4 * width**2),
        name="whole_right",
    )(me, corners, *flat)


def rows_kernel(groups, me_ref, rows_ref, cols_ref, *refs):
    strips, (right, out, mixed) = refs[:groups], refs[groups:]
    me = me_ref[0]
    strip, width = mixed.shape
    if strip % 128 == 0:
        for flip, part in enumerate(strips):
            mixed[:, strip_of(jnp.bitwise_xor(me, flip), strip)] = part[...]
        value = jnp.dot(mixed[...], right[...], preferred_element_type=F32)
    else:
        value = 0.0
        for flip, part in enumerate(strips):
            rows = right[strip_of(jnp.bitwise_xor(me, flip), strip), :]
            value += jnp.dot(part[...], rows, preferred_element_type=F32)
    column = lax.broadcasted_iota(jnp.int32, (strip, width), 1)
    row = lax.broadcasted_iota(jnp.int32, (strip, width), 0) + me * strip
    out[0] = jnp.where((row < rows_ref[0]) & (column < cols_ref[0]), value, 0.0).astype(BF16)


def update_rows(me, rows_valid, cols_valid, strips, right):
    width = right.shape[0]
    groups, strip = len(strips), strips[0].shape[0]
    return pl.pallas_call(
        functools.partial(rows_kernel, groups),
        in_specs=[SMEM_SPEC] * 3 + [VMEM_SPEC] * (groups + 1),
        out_specs=VMEM_SPEC,
        out_shape=jax.ShapeDtypeStruct((1, strip, width), BF16),
        scratch_shapes=[pltpu.VMEM((strip, width), BF16)],
        compiler_params=pltpu.CompilerParams(vmem_limit_bytes=VMEM),
        cost_estimate=cost(2 * strip * width**2, 4 * width**2),
        name="update_rows",
    )(me, rows_valid, cols_valid, *strips, right)


def added(*terms):
    return functools.reduce(lambda a, b: a + b, [term.astype(F32) for term in terms])


def on_device(grads, left_roots, right_roots, rows_valid, cols_valid):
    groups = lax.axis_size("dp")
    me = lax.axis_index("dp").astype(jnp.int32).reshape(1)
    width = grads.shape[-1]
    half, strip = width // 2, width // groups
    plain = grads
    grads, left_roots, right_roots = (
        pltpu.with_memory_space_constraint(array, pltpu.HBM) for array in (grads, left_roots, right_roots)
    )

    if groups == 4:
        far_0, far_1, near_0, near_1, left = messages(
            me, grads, left_roots, groups, [[(3, 0)], [(3, 1)], [(1, 0)], [(2, 1)]], False, "sent_first"
        )
        far_0, far_1 = swapped(far_0, 1, "far_0"), swapped(far_1, 2, "far_1")
        near_0, near_1 = swapped(near_0, 1, "near_0"), swapped(near_1, 2, "near_1")
        left = shifted(left, "left")
        *kept, right, corners = messages(
            me, grads, right_roots, groups, [[(2, 0)], [(1, 1)], [(0, 0)], [(0, 1)]], True, "sent_later"
        )
        via_0, via_1 = added(kept[0], far_0).astype(BF16), added(kept[1], far_1).astype(BF16)
        right = shifted(after(right, left), "right")
        left = after(left, via_0, via_1, near_0, near_1)
        via_0, via_1 = swapped(via_0, 2, "via_0"), swapped(via_1, 1, "via_1")
        left_1, left_2, left_3 = [swapped(left if flip < 3 else after(left, via_0), flip, "left_%d" % flip) for flip in (1, 2, 3)]
        corners = shifted(after(corners, right, left_1, left_2), "corners")
        mixed = left_columns(
            me,
            rows_valid,
            cols_valid,
            [[left], [left_1], [left_2], [left_3]],
            [[kept[2], near_0, via_0], [kept[3], near_1, via_1]],
            width,
        )
        right = after(right, via_0, via_1)
        right_1, right_2, right_3 = [swapped(right, flip, "right_%d" % flip) for flip in (1, 2, 3)]
        rights = [[right], [right_1], [right_2], [right_3]]
    else:
        (left,) = messages(me, grads, left_roots, groups, [], False, "sent_first")
        right, corners = messages(me, grads, right_roots, groups, [], True, "sent_later")
        left, right, corners = shifted(left, "left"), shifted(right, "right"), shifted(corners, "corners")
        parts = [
            lax.dynamic_slice_in_dim(plain[0, 0], jnp.bitwise_xor(me[0], flip) * strip, strip, 1)
            for flip in range(groups)
        ]
        terms = [parts[:1] + [swapped(parts[flip], flip, "grad") for flip in range(1, groups)]]
        lefts = [[left]] + [[swapped(left, flip, "left")] for flip in range(1, groups)]
        mixed = left_columns(me, rows_valid, cols_valid, lefts, terms, width)
        rights = [[right]] + [[swapped(right, flip, "right")] for flip in range(1, groups)]
    whole = whole_right(me, corners, rights, width)
    strips = [mixed[0]] + [swapped(mixed[flip], flip, "strip_%d" % flip) for flip in range(1, groups)]
    return update_rows(me, rows_valid, cols_valid, strips, whole)


def solution(mesh):
    placed = (
        P("dp", "shard", None, None),
        P("shard", None, None),
        P("shard", None, None),
        P("shard"),
        P("shard"),
    )
    return jax.shard_map(
        on_device, mesh=mesh, in_specs=placed, out_specs=P("shard", "dp", None), check_vma=False
    )
```

```python
import functools

import jax
import jax.numpy as jnp
from jax import lax
from jax.experimental import pallas as pl
from jax.experimental.pallas import tpu as pltpu
from jax.sharding import PartitionSpec as P

TILE = 256
EXTRA = 16
VMEM = 24 * 1024 * 1024
SMEM_SPEC = pl.BlockSpec(memory_space=pltpu.SMEM)
VMEM_SPEC = pl.BlockSpec(memory_space=pltpu.VMEM)
HBM_SPEC = pl.BlockSpec(memory_space=pltpu.HBM)
BF16 = jnp.bfloat16
F32 = jnp.float32


def shifted(value, name):
    count = lax.axis_size("shard")
    with jax.named_scope(name):
        return lax.ppermute(value, "shard", [(source, (source + count // 2) % count) for source in range(count)])


def swapped(value, flip, name):
    count = lax.axis_size("dp")
    with jax.named_scope(name):
        return lax.ppermute(value, "dp", [(source, source ^ flip) for source in range(count)])


def after(value, *earlier):
    return lax.optimization_barrier((value, *earlier))[0]


def block(index):
    return pl.ds(index * TILE, TILE)


def strip_of(index, size):
    return pl.ds(pl.multiple_of(index * size, size), size)


def cost(flops, bytes_accessed):
    return pl.CostEstimate(flops=flops, bytes_accessed=bytes_accessed, transcendentals=0)


def below(tiles):
    return [(i, j) for j in range(tiles) for i in range(j + 1, tiles)]


def pick_copies(wanted, me, grad_ref, outs, sems):
    copies = []
    for parts, out in zip(wanted, outs):
        half, strip = out.shape[0] // len(parts), out.shape[1]
        for part, (flip, h) in enumerate(parts):
            source = grad_ref.at[0, 0, pl.ds(h * half, half), strip_of(jnp.bitwise_xor(me, flip), strip)]
            copies.append(
                pltpu.make_async_copy(source, out.at[pl.ds(part * half, half), :], sems.at[len(copies)])
            )
    return copies


def picked_shapes(wanted, width, groups):
    return [pltpu.VMEM((len(parts) * (width // 2), width // groups), BF16) for parts in wanted]


def strip_copies(me, root_ref, strip, out, sems):
    return [
        pltpu.make_async_copy(
            root_ref.at[0, pl.ds(pl.multiple_of(i * TILE + me * strip, strip), strip), block(j)],
            out.at[pl.ds(k * strip, strip), :],
            sems.at[k],
        )
        for k, (i, j) in enumerate(below(root_ref.shape[1] // TILE))
    ]


def corner_copies(root_ref, corners, sems):
    return [
        pltpu.make_async_copy(root_ref.at[0, block(i), block(i)], corners.at[i], sems.at[i])
        for i in range(corners.shape[0])
    ]


def fold_corners(corners, start, strip, out, base):
    tiles = corners.shape[0]
    row = lax.broadcasted_iota(jnp.int32, (strip, TILE), 0) + start
    column = lax.broadcasted_iota(jnp.int32, (strip, TILE), 1)
    on_diag = lax.broadcasted_iota(jnp.int32, (TILE, TILE), 0) == lax.broadcasted_iota(jnp.int32, (TILE, TILE), 1)
    rows = pl.ds(pl.multiple_of(start, strip), strip) if strip < TILE else pl.ds(0, TILE)
    lines = []
    for pair in range(tiles // 2):
        even, odd = 2 * pair, 2 * pair + 1
        out[pl.ds(base + pair * strip, strip), :] = jnp.where(
            row >= column, corners[even, rows, :], corners[odd, rows, :]
        )
        lines.append(jnp.sum(jnp.where(on_diag, corners[odd].astype(F32), 0.0), axis=0, keepdims=True))
    lines.append(jnp.zeros((EXTRA - len(lines), TILE), F32))
    out[pl.ds(base + tiles // 2 * strip, EXTRA), :] = jnp.concatenate(lines, axis=0).astype(BF16)


def messages_kernel(wanted, quarter, me_ref, grad_ref, root_ref, *refs):
    outs, (*folded, corners, pick_sems, strip_sems, corner_sems) = refs[: len(wanted)], refs[len(wanted) :]
    me = me_ref[0]
    tiles = corners.shape[0]
    low = len(below(tiles))
    strip = quarter
    strips = strip_copies(me, root_ref, strip, folded[0], strip_sems)
    cornered = corner_copies(root_ref, corners, corner_sems)
    copies = pick_copies(wanted, me, grad_ref, outs, pick_sems)
    for copy in cornered + strips + copies:
        copy.start()
    for copy in cornered:
        copy.wait()
    if len(folded) == 1:
        fold_corners(corners, me * strip, strip, folded[0], low * strip)
    else:
        fold_corners(corners, 0, TILE, folded[1], 0)
    for copy in strips + copies:
        copy.wait()


def messages(me, grads, root, groups, wanted, apart, name):
    width = grads.shape[-1]
    strip, tiles = TILE // groups, width // TILE
    count = sum(len(parts) for parts in wanted)
    low = len(below(tiles)) * strip
    if apart:
        rows = [low, tiles // 2 * TILE + EXTRA]
    else:
        rows = [low + tiles // 2 * strip + EXTRA]
    return pl.pallas_call(
        functools.partial(messages_kernel, wanted, strip),
        in_specs=[SMEM_SPEC] + [HBM_SPEC] * 2,
        out_specs=[VMEM_SPEC] * (len(wanted) + len(rows)),
        out_shape=picked_shapes(wanted, width, groups) + [pltpu.VMEM((number, TILE), BF16) for number in rows],
        scratch_shapes=[
            pltpu.VMEM((tiles, TILE, TILE), BF16),
            pltpu.SemaphoreType.DMA((max(count, 1),)),
            pltpu.SemaphoreType.DMA((len(below(tiles)),)),
            pltpu.SemaphoreType.DMA((tiles,)),
        ],
        compiler_params=pltpu.CompilerParams(vmem_limit_bytes=VMEM),
        name=name,
    )(me, grads, root)


def unfold_below(pieces, me, root):
    tiles = root.shape[0] // TILE
    strip = TILE // len(pieces)
    blocks = below(tiles)
    for flip, parts in enumerate(pieces):
        other = jnp.bitwise_xor(me, flip)
        for k, (i, j) in enumerate(blocks):
            part, row = 0, k * strip
            while row >= parts[part].shape[0]:
                row -= parts[part].shape[0]
                part += 1
            at = pl.ds(pl.multiple_of(i * TILE + other * strip, strip), strip)
            root[at, block(j)] = parts[part][pl.ds(row, strip), :]
    for i, j in blocks:
        root[block(j), block(i)] = root[block(i), block(j)].T


def unfold_corners(folded, lines, root):
    row = lax.broadcasted_iota(jnp.int32, (TILE, TILE), 0)
    column = lax.broadcasted_iota(jnp.int32, (TILE, TILE), 1)
    lines = lines.astype(F32)
    for i in range(root.shape[0] // TILE):
        value = folded[block(i // 2), :].astype(F32)
        value = jnp.where(row >= column if i % 2 == 0 else row < column, value, value.T)
        if i % 2:
            line = jnp.broadcast_to(lines[i // 2 : i // 2 + 1, :], (TILE, TILE))
            value = jnp.where(row == column, line, value)
        root[block(i), block(i)] = value.astype(BF16)


def unfold(pieces, me, root, folded):
    tiles = root.shape[0] // TILE
    strip = TILE // len(pieces)
    unfold_below(pieces, me, root)
    base = len(below(tiles)) * strip
    for flip, parts in enumerate(pieces):
        other = jnp.bitwise_xor(me, flip)
        for pair in range(tiles // 2):
            part, row = 0, base + pair * strip
            while row >= parts[part].shape[0]:
                row -= parts[part].shape[0]
                part += 1
            at = pl.ds(pl.multiple_of(pair * TILE + other * strip, strip), strip)
            folded[at, :] = parts[part][pl.ds(row, strip), :]
    unfold_corners(folded, pieces[0][0][pl.ds(base + tiles // 2 * strip, EXTRA), :], root)


def dealt(refs, counts):
    lists = []
    for count in counts:
        lists.append(refs[:count])
        refs = refs[count:]
    return lists, refs


def columns_kernel(groups, held, split, me_ref, rows_ref, cols_ref, *refs):
    pieces, refs = dealt(refs, held)
    terms, refs = dealt(refs, split)
    outs, (left, folded, masked) = refs[:groups], refs[groups:]
    me = me_ref[0]
    width, strip = masked.shape
    unfold(pieces, me, left, folded)
    part = width // len(terms)
    column = lax.broadcasted_iota(jnp.int32, (part, strip), 1) + me * strip
    row = lax.broadcasted_iota(jnp.int32, (part, strip), 0)
    for index, used in enumerate(terms):
        total = functools.reduce(lambda a, b: a + b, [term[pl.ds(0, part), :].astype(F32) for term in used])
        keep = (row + index * part < rows_ref[0]) & (column < cols_ref[0])
        masked[pl.ds(index * part, part), :] = jnp.where(keep, total, 0.0).astype(BF16)
    for flip, out in enumerate(outs):
        rows = left[strip_of(jnp.bitwise_xor(me, flip), strip), :]
        out[...] = jnp.dot(rows, masked[...], preferred_element_type=F32).astype(BF16)


def left_columns(me, rows_valid, cols_valid, pieces, terms, width):
    groups = len(pieces)
    strip = width // groups
    flat = [array for part in (*pieces, *terms) for array in part]
    return pl.pallas_call(
        functools.partial(columns_kernel, groups, [len(part) for part in pieces], [len(part) for part in terms]),
        in_specs=[SMEM_SPEC] * 3 + [VMEM_SPEC] * len(flat),
        out_specs=[VMEM_SPEC] * groups,
        out_shape=[pltpu.VMEM((strip, strip), BF16)] * groups,
        scratch_shapes=[
            pltpu.VMEM((width, width), BF16),
            pltpu.VMEM((width // 2, TILE), BF16),
            pltpu.VMEM((width, strip), BF16),
        ],
        compiler_params=pltpu.CompilerParams(vmem_limit_bytes=VMEM),
        cost_estimate=cost(2 * strip * width**2, 4 * width**2),
        name="left_columns",
    )(me, rows_valid, cols_valid, *flat)


def whole_right_kernel(held, me_ref, corners_ref, *refs):
    pieces, (right,) = dealt(refs, held)
    unfold_below(pieces, me_ref[0], right)
    unfold_corners(corners_ref, corners_ref[pl.ds(right.shape[0] // 2, EXTRA), :], right)


def whole_right(me, corners, pieces, width):
    flat = [array for part in pieces for array in part]
    return pl.pallas_call(
        functools.partial(whole_right_kernel, [len(part) for part in pieces]),
        in_specs=[SMEM_SPEC] + [VMEM_SPEC] * (1 + len(flat)),
        out_specs=VMEM_SPEC,
        out_shape=pltpu.VMEM((width, width), BF16),
        compiler_params=pltpu.CompilerParams(vmem_limit_bytes=VMEM),
        cost_estimate=cost(width**2, 4 * width**2),
        name="whole_right",
    )(me, corners, *flat)


def rows_kernel(groups, me_ref, rows_ref, cols_ref, *refs):
    strips, (right, out, mixed, staged, sems) = refs[:groups], refs[groups:]
    me = me_ref[0]
    strip, width = mixed.shape
    joined = strip % 128 == 0
    if joined:
        for flip, part in enumerate(strips):
            mixed[:, strip_of(jnp.bitwise_xor(me, flip), strip)] = part[...]
    row = lax.broadcasted_iota(jnp.int32, (strip, TILE), 0) + me * strip
    copies = []
    for tile in range(width // TILE):
        if joined:
            value = jnp.dot(mixed[...], right[:, block(tile)], preferred_element_type=F32)
        else:
            value = 0.0
            for flip, part in enumerate(strips):
                rows = right[strip_of(jnp.bitwise_xor(me, flip), strip), block(tile)]
                value += jnp.dot(part[...], rows, preferred_element_type=F32)
        column = lax.broadcasted_iota(jnp.int32, (strip, TILE), 1) + tile * TILE
        keep = (row < rows_ref[0]) & (column < cols_ref[0])
        staged[:, block(tile)] = jnp.where(keep, value, 0.0).astype(BF16)
        copies.append(pltpu.make_async_copy(staged.at[:, block(tile)], out.at[0, :, block(tile)], sems.at[tile]))
        copies[-1].start()
    for copy in copies:
        copy.wait()


def update_rows(me, rows_valid, cols_valid, strips, right):
    width = right.shape[0]
    groups, strip = len(strips), strips[0].shape[0]
    return pl.pallas_call(
        functools.partial(rows_kernel, groups),
        in_specs=[SMEM_SPEC] * 3 + [VMEM_SPEC] * (groups + 1),
        out_specs=HBM_SPEC,
        out_shape=jax.ShapeDtypeStruct((1, strip, width), BF16),
        scratch_shapes=[
            pltpu.VMEM((strip, width), BF16),
            pltpu.VMEM((strip, width), BF16),
            pltpu.SemaphoreType.DMA((width // TILE,)),
        ],
        compiler_params=pltpu.CompilerParams(vmem_limit_bytes=VMEM),
        cost_estimate=cost(2 * strip * width**2, 4 * width**2),
        name="update_rows",
    )(me, rows_valid, cols_valid, *strips, right)


def added(*terms):
    return functools.reduce(lambda a, b: a + b, [term.astype(F32) for term in terms])


def on_device(grads, left_roots, right_roots, rows_valid, cols_valid):
    groups = lax.axis_size("dp")
    me = lax.axis_index("dp").astype(jnp.int32).reshape(1)
    width = grads.shape[-1]
    half, strip = width // 2, width // groups
    plain = grads
    grads, left_roots, right_roots = (
        pltpu.with_memory_space_constraint(array, pltpu.HBM) for array in (grads, left_roots, right_roots)
    )

    if groups == 4:
        far_0, far_1, near_0, near_1, left = messages(
            me, grads, left_roots, groups, [[(3, 0)], [(3, 1)], [(1, 0)], [(2, 1)]], False, "sent_first"
        )
        far_0, far_1 = swapped(far_0, 1, "far_0"), swapped(far_1, 2, "far_1")
        near_0, near_1 = swapped(near_0, 1, "near_0"), swapped(near_1, 2, "near_1")
        left = shifted(left, "left")
        *kept, right, corners = messages(
            me, grads, right_roots, groups, [[(2, 0)], [(1, 1)], [(0, 0)], [(0, 1)]], True, "sent_later"
        )
        via_0, via_1 = added(kept[0], far_0).astype(BF16), added(kept[1], far_1).astype(BF16)
        right = shifted(after(right, left), "right")
        left = after(left, via_0, via_1, near_0, near_1)
        via_0, via_1 = swapped(via_0, 2, "via_0"), swapped(via_1, 1, "via_1")
        left_1, left_2, left_3 = [swapped(left if flip < 3 else after(left, via_0), flip, "left_%d" % flip) for flip in (1, 2, 3)]
        corners = shifted(after(corners, right, left_1, left_2), "corners")
        mixed = left_columns(
            me,
            rows_valid,
            cols_valid,
            [[left], [left_1], [left_2], [left_3]],
            [[kept[2], near_0, via_0], [kept[3], near_1, via_1]],
            width,
        )
        right = after(right, via_0, via_1)
        right_1, right_2, right_3 = [swapped(right, flip, "right_%d" % flip) for flip in (1, 2, 3)]
        rights = [[right], [right_1], [right_2], [right_3]]
    else:
        (left,) = messages(me, grads, left_roots, groups, [], False, "sent_first")
        right, corners = messages(me, grads, right_roots, groups, [], True, "sent_later")
        left, right, corners = shifted(left, "left"), shifted(right, "right"), shifted(corners, "corners")
        parts = [
            lax.dynamic_slice_in_dim(plain[0, 0], jnp.bitwise_xor(me[0], flip) * strip, strip, 1)
            for flip in range(groups)
        ]
        terms = [parts[:1] + [swapped(parts[flip], flip, "grad") for flip in range(1, groups)]]
        lefts = [[left]] + [[swapped(left, flip, "left")] for flip in range(1, groups)]
        mixed = left_columns(me, rows_valid, cols_valid, lefts, terms, width)
        rights = [[right]] + [[swapped(right, flip, "right")] for flip in range(1, groups)]
    whole = whole_right(me, corners, rights, width)
    strips = [mixed[0]] + [swapped(mixed[flip], flip, "strip_%d" % flip) for flip in range(1, groups)]
    return update_rows(me, rows_valid, cols_valid, strips, whole)


def solution(mesh):
    placed = (
        P("dp", "shard", None, None),
        P("shard", None, None),
        P("shard", None, None),
        P("shard"),
        P("shard"),
    )
    return jax.shard_map(
        on_device, mesh=mesh, in_specs=placed, out_specs=P("shard", "dp", None), check_vma=False
    )
```

```python
import functools

import jax
import jax.numpy as jnp
from jax import lax
from jax.experimental import pallas as pl
from jax.experimental.pallas import tpu as pltpu
from jax.sharding import PartitionSpec as P

TILE = 256
EXTRA = 16
VMEM = 24 * 1024 * 1024
SMEM_SPEC = pl.BlockSpec(memory_space=pltpu.SMEM)
VMEM_SPEC = pl.BlockSpec(memory_space=pltpu.VMEM)
HBM_SPEC = pl.BlockSpec(memory_space=pltpu.HBM)
BF16 = jnp.bfloat16
F32 = jnp.float32


def shifted(value, name):
    count = lax.axis_size("shard")
    with jax.named_scope(name):
        return lax.ppermute(value, "shard", [(source, (source + count // 2) % count) for source in range(count)])


def swapped(value, flip, name):
    count = lax.axis_size("dp")
    with jax.named_scope(name):
        return lax.ppermute(value, "dp", [(source, source ^ flip) for source in range(count)])


def after(value, *earlier):
    return lax.optimization_barrier((value, *earlier))[0]


def block(index):
    return pl.ds(index * TILE, TILE)


def strip_of(index, size):
    return pl.ds(pl.multiple_of(index * size, size), size)


def cost(flops, bytes_accessed):
    return pl.CostEstimate(flops=flops, bytes_accessed=bytes_accessed, transcendentals=0)


def below(tiles):
    return [(i, j) for j in range(tiles) for i in range(j + 1, tiles)]


def pick_copies(wanted, me, grad_ref, outs, sems):
    copies = []
    for parts, out in zip(wanted, outs):
        half, strip = out.shape[0] // len(parts), out.shape[1]
        for part, (flip, h) in enumerate(parts):
            source = grad_ref.at[0, 0, pl.ds(h * half, half), strip_of(jnp.bitwise_xor(me, flip), strip)]
            copies.append(
                pltpu.make_async_copy(source, out.at[pl.ds(part * half, half), :], sems.at[len(copies)])
            )
    return copies


def picked_shapes(wanted, width, groups):
    return [pltpu.VMEM((len(parts) * (width // 2), width // groups), BF16) for parts in wanted]


def strip_copies(me, root_ref, strip, out, sems):
    return [
        pltpu.make_async_copy(
            root_ref.at[0, pl.ds(pl.multiple_of(i * TILE + me * strip, strip), strip), block(j)],
            out.at[pl.ds(k * strip, strip), :],
            sems.at[k],
        )
        for k, (i, j) in enumerate(below(root_ref.shape[1] // TILE))
    ]


def corner_copies(root_ref, corners, sems):
    return [
        pltpu.make_async_copy(root_ref.at[0, block(i), block(i)], corners.at[i], sems.at[i])
        for i in range(corners.shape[0])
    ]


def fold_corners(corners, start, strip, out, base):
    tiles = corners.shape[0]
    row = lax.broadcasted_iota(jnp.int32, (strip, TILE), 0) + start
    column = lax.broadcasted_iota(jnp.int32, (strip, TILE), 1)
    on_diag = lax.broadcasted_iota(jnp.int32, (TILE, TILE), 0) == lax.broadcasted_iota(jnp.int32, (TILE, TILE), 1)
    rows = pl.ds(pl.multiple_of(start, strip), strip) if strip < TILE else pl.ds(0, TILE)
    lines = []
    for pair in range(tiles // 2):
        even, odd = 2 * pair, 2 * pair + 1
        out[pl.ds(base + pair * strip, strip), :] = jnp.where(
            row >= column, corners[even, rows, :], corners[odd, rows, :]
        )
        lines.append(jnp.sum(jnp.where(on_diag, corners[odd].astype(F32), 0.0), axis=0, keepdims=True))
    lines.append(jnp.zeros((EXTRA - len(lines), TILE), F32))
    out[pl.ds(base + tiles // 2 * strip, EXTRA), :] = jnp.concatenate(lines, axis=0).astype(BF16)


def messages_kernel(wanted, quarter, me_ref, grad_ref, root_ref, *refs):
    outs, (*folded, corners, pick_sems, strip_sems, corner_sems) = refs[: len(wanted)], refs[len(wanted) :]
    me = me_ref[0]
    tiles = corners.shape[0]
    low = len(below(tiles))
    strip = quarter
    strips = strip_copies(me, root_ref, strip, folded[0], strip_sems)
    cornered = corner_copies(root_ref, corners, corner_sems)
    copies = pick_copies(wanted, me, grad_ref, outs, pick_sems)
    for copy in cornered + strips + copies:
        copy.start()
    for copy in cornered:
        copy.wait()
    if len(folded) == 1:
        fold_corners(corners, me * strip, strip, folded[0], low * strip)
    else:
        fold_corners(corners, 0, TILE, folded[1], 0)
    for copy in strips + copies:
        copy.wait()


def messages(me, grads, root, groups, wanted, apart, name):
    width = grads.shape[-1]
    strip, tiles = TILE // groups, width // TILE
    count = sum(len(parts) for parts in wanted)
    low = len(below(tiles)) * strip
    if apart:
        rows = [low, tiles // 2 * TILE + EXTRA]
    else:
        rows = [low + tiles // 2 * strip + EXTRA]
    return pl.pallas_call(
        functools.partial(messages_kernel, wanted, strip),
        in_specs=[SMEM_SPEC] + [HBM_SPEC] * 2,
        out_specs=[VMEM_SPEC] * (len(wanted) + len(rows)),
        out_shape=picked_shapes(wanted, width, groups) + [pltpu.VMEM((number, TILE), BF16) for number in rows],
        scratch_shapes=[
            pltpu.VMEM((tiles, TILE, TILE), BF16),
            pltpu.SemaphoreType.DMA((max(count, 1),)),
            pltpu.SemaphoreType.DMA((len(below(tiles)),)),
            pltpu.SemaphoreType.DMA((tiles,)),
        ],
        compiler_params=pltpu.CompilerParams(vmem_limit_bytes=VMEM),
        name=name,
    )(me, grads, root)


def unfold_below(pieces, me, root):
    tiles = root.shape[0] // TILE
    strip = TILE // len(pieces)
    blocks = below(tiles)
    for flip, parts in enumerate(pieces):
        other = jnp.bitwise_xor(me, flip)
        for k, (i, j) in enumerate(blocks):
            part, row = 0, k * strip
            while row >= parts[part].shape[0]:
                row -= parts[part].shape[0]
                part += 1
            at = pl.ds(pl.multiple_of(i * TILE + other * strip, strip), strip)
            root[at, block(j)] = parts[part][pl.ds(row, strip), :]
    for i, j in blocks:
        root[block(j), block(i)] = root[block(i), block(j)].T


def unfold_corners(folded, lines, root):
    row = lax.broadcasted_iota(jnp.int32, (TILE, TILE), 0)
    column = lax.broadcasted_iota(jnp.int32, (TILE, TILE), 1)
    lines = lines.astype(F32)
    for i in range(root.shape[0] // TILE):
        value = folded[block(i // 2), :].astype(F32)
        value = jnp.where(row >= column if i % 2 == 0 else row < column, value, value.T)
        if i % 2:
            line = jnp.broadcast_to(lines[i // 2 : i // 2 + 1, :], (TILE, TILE))
            value = jnp.where(row == column, line, value)
        root[block(i), block(i)] = value.astype(BF16)


def unfold(pieces, me, root, folded):
    tiles = root.shape[0] // TILE
    strip = TILE // len(pieces)
    unfold_below(pieces, me, root)
    base = len(below(tiles)) * strip
    for flip, parts in enumerate(pieces):
        other = jnp.bitwise_xor(me, flip)
        for pair in range(tiles // 2):
            part, row = 0, base + pair * strip
            while row >= parts[part].shape[0]:
                row -= parts[part].shape[0]
                part += 1
            at = pl.ds(pl.multiple_of(pair * TILE + other * strip, strip), strip)
            folded[at, :] = parts[part][pl.ds(row, strip), :]
    unfold_corners(folded, pieces[0][0][pl.ds(base + tiles // 2 * strip, EXTRA), :], root)


def dealt(refs, counts):
    lists = []
    for count in counts:
        lists.append(refs[:count])
        refs = refs[count:]
    return lists, refs


def columns_kernel(groups, held, split, me_ref, rows_ref, cols_ref, *refs):
    pieces, refs = dealt(refs, held)
    terms, refs = dealt(refs, split)
    outs, (left, folded, masked, mixed) = refs[:groups], refs[groups:]
    me = me_ref[0]
    width, strip = masked.shape
    unfold(pieces, me, left, folded)
    part = width // len(terms)
    column = lax.broadcasted_iota(jnp.int32, (part, strip), 1) + me * strip
    row = lax.broadcasted_iota(jnp.int32, (part, strip), 0)
    for index, used in enumerate(terms):
        total = functools.reduce(lambda a, b: a + b, [term[pl.ds(0, part), :].astype(F32) for term in used])
        keep = (row + index * part < rows_ref[0]) & (column < cols_ref[0])
        masked[pl.ds(index * part, part), :] = jnp.where(keep, total, 0.0).astype(BF16)
    mixed[...] = jnp.dot(left[...], masked[...], preferred_element_type=F32).astype(BF16)
    for flip, out in enumerate(outs):
        out[...] = mixed[strip_of(jnp.bitwise_xor(me, flip), strip), :]


def left_columns(me, rows_valid, cols_valid, pieces, terms, width):
    groups = len(pieces)
    strip = width // groups
    flat = [array for part in (*pieces, *terms) for array in part]
    return pl.pallas_call(
        functools.partial(columns_kernel, groups, [len(part) for part in pieces], [len(part) for part in terms]),
        in_specs=[SMEM_SPEC] * 3 + [VMEM_SPEC] * len(flat),
        out_specs=[VMEM_SPEC] * groups,
        out_shape=[pltpu.VMEM((strip, strip), BF16)] * groups,
        scratch_shapes=[
            pltpu.VMEM((width, width), BF16),
            pltpu.VMEM((width // 2, TILE), BF16),
            pltpu.VMEM((width, strip), BF16),
            pltpu.VMEM((width, strip), BF16),
        ],
        compiler_params=pltpu.CompilerParams(vmem_limit_bytes=VMEM),
        cost_estimate=cost(2 * strip * width**2, 4 * width**2),
        name="left_columns",
    )(me, rows_valid, cols_valid, *flat)


def whole_right_kernel(held, me_ref, corners_ref, *refs):
    pieces, (right,) = dealt(refs, held)
    unfold_below(pieces, me_ref[0], right)
    unfold_corners(corners_ref, corners_ref[pl.ds(right.shape[0] // 2, EXTRA), :], right)


def whole_right(me, corners, pieces, width):
    flat = [array for part in pieces for array in part]
    return pl.pallas_call(
        functools.partial(whole_right_kernel, [len(part) for part in pieces]),
        in_specs=[SMEM_SPEC] + [VMEM_SPEC] * (1 + len(flat)),
        out_specs=VMEM_SPEC,
        out_shape=pltpu.VMEM((width, width), BF16),
        compiler_params=pltpu.CompilerParams(vmem_limit_bytes=VMEM),
        cost_estimate=cost(width**2, 4 * width**2),
        name="whole_right",
    )(me, corners, *flat)


def rows_kernel(groups, me_ref, rows_ref, cols_ref, *refs):
    strips, (right, out, mixed) = refs[:groups], refs[groups:]
    me = me_ref[0]
    strip, width = mixed.shape
    if strip % 128 == 0:
        for flip, part in enumerate(strips):
            mixed[:, strip_of(jnp.bitwise_xor(me, flip), strip)] = part[...]
        value = jnp.dot(mixed[...], right[...], preferred_element_type=F32)
    else:
        value = 0.0
        for flip, part in enumerate(strips):
            rows = right[strip_of(jnp.bitwise_xor(me, flip), strip), :]
            value += jnp.dot(part[...], rows, preferred_element_type=F32)
    column = lax.broadcasted_iota(jnp.int32, (strip, width), 1)
    row = lax.broadcasted_iota(jnp.int32, (strip, width), 0) + me * strip
    out[0] = jnp.where((row < rows_ref[0]) & (column < cols_ref[0]), value, 0.0).astype(BF16)


def update_rows(me, rows_valid, cols_valid, strips, right):
    width = right.shape[0]
    groups, strip = len(strips), strips[0].shape[0]
    return pl.pallas_call(
        functools.partial(rows_kernel, groups),
        in_specs=[SMEM_SPEC] * 3 + [VMEM_SPEC] * (groups + 1),
        out_specs=VMEM_SPEC,
        out_shape=jax.ShapeDtypeStruct((1, strip, width), BF16),
        scratch_shapes=[pltpu.VMEM((strip, width), BF16)],
        compiler_params=pltpu.CompilerParams(vmem_limit_bytes=VMEM),
        cost_estimate=cost(2 * strip * width**2, 4 * width**2),
        name="update_rows",
    )(me, rows_valid, cols_valid, *strips, right)


def added(*terms):
    return functools.reduce(lambda a, b: a + b, [term.astype(F32) for term in terms])


def on_device(grads, left_roots, right_roots, rows_valid, cols_valid):
    groups = lax.axis_size("dp")
    me = lax.axis_index("dp").astype(jnp.int32).reshape(1)
    width = grads.shape[-1]
    half, strip = width // 2, width // groups
    plain = grads
    grads, left_roots, right_roots = (
        pltpu.with_memory_space_constraint(array, pltpu.HBM) for array in (grads, left_roots, right_roots)
    )

    if groups == 4:
        far_0, far_1, left = messages(
            me, grads, left_roots, groups, [[(3, 0)], [(3, 1)]], False, "sent_first"
        )
        far_0, far_1 = swapped(far_0, 1, "far_0"), swapped(far_1, 2, "far_1")
        left = shifted(left, "left")
        near_0, near_1, *kept, right, corners = messages(
            me,
            grads,
            right_roots,
            groups,
            [[(1, 0)], [(2, 1)], [(2, 0)], [(1, 1)], [(0, 0)], [(0, 1)]],
            True,
            "sent_later",
        )
        near_0, near_1 = swapped(near_0, 1, "near_0"), swapped(near_1, 2, "near_1")
        via_0, via_1 = added(kept[0], far_0).astype(BF16), added(kept[1], far_1).astype(BF16)
        right = shifted(after(right, left), "right")
        left = after(left, via_0, via_1, near_0, near_1)
        via_0, via_1 = swapped(via_0, 2, "via_0"), swapped(via_1, 1, "via_1")
        left_1, left_2 = swapped(left, 1, "left_1"), swapped(after(left, via_0), 2, "left_2")
        cut = (left.shape[0] - EXTRA) // 2
        left_3a, left_3b = left_1[:cut], left_2[cut : 2 * cut]
        corners = shifted(after(corners, right, left_3a, left_3b), "corners")
        left_3 = [swapped(left_3a, 2, "left_3a"), swapped(left_3b, 1, "left_3b")]
        mixed = left_columns(
            me,
            rows_valid,
            cols_valid,
            [[left], [left_1], [left_2], left_3],
            [[kept[2], near_0, via_0], [kept[3], near_1, via_1]],
            width,
        )
        right = after(right, via_0, via_1)
        right_1, right_2 = swapped(right, 1, "right_1"), swapped(right, 2, "right_2")
        cut = right.shape[0] // 2
        right_3 = [swapped(right_1[:cut], 2, "right_3a"), swapped(right_2[cut:], 1, "right_3b")]
        rights = [[right], [right_1], [right_2], right_3]
    else:
        (left,) = messages(me, grads, left_roots, groups, [], False, "sent_first")
        right, corners = messages(me, grads, right_roots, groups, [], True, "sent_later")
        left, right, corners = shifted(left, "left"), shifted(right, "right"), shifted(corners, "corners")
        parts = [
            lax.dynamic_slice_in_dim(plain[0, 0], jnp.bitwise_xor(me[0], flip) * strip, strip, 1)
            for flip in range(groups)
        ]
        terms = [parts[:1] + [swapped(parts[flip], flip, "grad") for flip in range(1, groups)]]
        lefts = [[left]] + [[swapped(left, flip, "left")] for flip in range(1, groups)]
        mixed = left_columns(me, rows_valid, cols_valid, lefts, terms, width)
        rights = [[right]] + [[swapped(right, flip, "right")] for flip in range(1, groups)]
    whole = whole_right(me, corners, rights, width)
    strips = [mixed[0]] + [swapped(mixed[flip], flip, "strip_%d" % flip) for flip in range(1, groups)]
    return update_rows(me, rows_valid, cols_valid, strips, whole)


def solution(mesh):
    placed = (
        P("dp", "shard", None, None),
        P("shard", None, None),
        P("shard", None, None),
        P("shard"),
        P("shard"),
    )
    return jax.shard_map(
        on_device, mesh=mesh, in_specs=placed, out_specs=P("shard", "dp", None), check_vma=False
    )
```

```python
import functools

import jax
import jax.numpy as jnp
from jax import lax
from jax.experimental import pallas as pl
from jax.experimental.pallas import tpu as pltpu
from jax.sharding import PartitionSpec as P

TILE = 256
EXTRA = 16
VMEM = 24 * 1024 * 1024
SMEM_SPEC = pl.BlockSpec(memory_space=pltpu.SMEM)
VMEM_SPEC = pl.BlockSpec(memory_space=pltpu.VMEM)
HBM_SPEC = pl.BlockSpec(memory_space=pltpu.HBM)
BF16 = jnp.bfloat16
F32 = jnp.float32


def shifted(value, name):
    count = lax.axis_size("shard")
    with jax.named_scope(name):
        return lax.ppermute(value, "shard", [(source, (source + count // 2) % count) for source in range(count)])


def swapped(value, flip, name):
    count = lax.axis_size("dp")
    with jax.named_scope(name):
        return lax.ppermute(value, "dp", [(source, source ^ flip) for source in range(count)])


def after(value, *earlier):
    return lax.optimization_barrier((value, *earlier))[0]


def block(index):
    return pl.ds(index * TILE, TILE)


def strip_of(index, size):
    return pl.ds(pl.multiple_of(index * size, size), size)


def cost(flops, bytes_accessed):
    return pl.CostEstimate(flops=flops, bytes_accessed=bytes_accessed, transcendentals=0)


def below(tiles):
    return [(i, j) for j in range(tiles) for i in range(j + 1, tiles)]


def pick_copies(wanted, me, grad_ref, outs, sems):
    copies = []
    for parts, out in zip(wanted, outs):
        half, strip = out.shape[0] // len(parts), out.shape[1]
        for part, (flip, h) in enumerate(parts):
            source = grad_ref.at[0, 0, pl.ds(h * half, half), strip_of(jnp.bitwise_xor(me, flip), strip)]
            copies.append(
                pltpu.make_async_copy(source, out.at[pl.ds(part * half, half), :], sems.at[len(copies)])
            )
    return copies


def picked_shapes(wanted, width, groups):
    return [pltpu.VMEM((len(parts) * (width // 2), width // groups), BF16) for parts in wanted]


def strip_copies(me, root_ref, strip, out, sems):
    return [
        pltpu.make_async_copy(
            root_ref.at[0, pl.ds(pl.multiple_of(i * TILE + me * strip, strip), strip), block(j)],
            out.at[pl.ds(k * strip, strip), :],
            sems.at[k],
        )
        for k, (i, j) in enumerate(below(root_ref.shape[1] // TILE))
    ]


def corner_copies(root_ref, corners, sems):
    return [
        pltpu.make_async_copy(root_ref.at[0, block(i), block(i)], corners.at[i], sems.at[i])
        for i in range(corners.shape[0])
    ]


def fold_corners(corners, start, strip, out, base):
    tiles = corners.shape[0]
    row = lax.broadcasted_iota(jnp.int32, (strip, TILE), 0) + start
    column = lax.broadcasted_iota(jnp.int32, (strip, TILE), 1)
    on_diag = lax.broadcasted_iota(jnp.int32, (TILE, TILE), 0) == lax.broadcasted_iota(jnp.int32, (TILE, TILE), 1)
    rows = pl.ds(pl.multiple_of(start, strip), strip) if strip < TILE else pl.ds(0, TILE)
    lines = []
    for pair in range(tiles // 2):
        even, odd = 2 * pair, 2 * pair + 1
        out[pl.ds(base + pair * strip, strip), :] = jnp.where(
            row >= column, corners[even, rows, :], corners[odd, rows, :]
        )
        lines.append(jnp.sum(jnp.where(on_diag, corners[odd].astype(F32), 0.0), axis=0, keepdims=True))
    lines.append(jnp.zeros((EXTRA - len(lines), TILE), F32))
    out[pl.ds(base + tiles // 2 * strip, EXTRA), :] = jnp.concatenate(lines, axis=0).astype(BF16)


def messages_kernel(wanted, quarter, me_ref, grad_ref, root_ref, *refs):
    outs, (*folded, corners, pick_sems, strip_sems, corner_sems) = refs[: len(wanted)], refs[len(wanted) :]
    me = me_ref[0]
    tiles = corners.shape[0]
    low = len(below(tiles))
    strip = quarter
    strips = strip_copies(me, root_ref, strip, folded[0], strip_sems)
    cornered = corner_copies(root_ref, corners, corner_sems)
    copies = pick_copies(wanted, me, grad_ref, outs, pick_sems)
    for copy in cornered + strips + copies:
        copy.start()
    for copy in cornered:
        copy.wait()
    if len(folded) == 1:
        fold_corners(corners, me * strip, strip, folded[0], low * strip)
    else:
        fold_corners(corners, 0, TILE, folded[1], 0)
    for copy in strips + copies:
        copy.wait()


def messages(me, grads, root, groups, wanted, apart, name):
    width = grads.shape[-1]
    strip, tiles = TILE // groups, width // TILE
    count = sum(len(parts) for parts in wanted)
    low = len(below(tiles)) * strip
    if apart:
        rows = [low, tiles // 2 * TILE + EXTRA]
    else:
        rows = [low + tiles // 2 * strip + EXTRA]
    return pl.pallas_call(
        functools.partial(messages_kernel, wanted, strip),
        in_specs=[SMEM_SPEC] + [HBM_SPEC] * 2,
        out_specs=[VMEM_SPEC] * (len(wanted) + len(rows)),
        out_shape=picked_shapes(wanted, width, groups) + [pltpu.VMEM((number, TILE), BF16) for number in rows],
        scratch_shapes=[
            pltpu.VMEM((tiles, TILE, TILE), BF16),
            pltpu.SemaphoreType.DMA((max(count, 1),)),
            pltpu.SemaphoreType.DMA((len(below(tiles)),)),
            pltpu.SemaphoreType.DMA((tiles,)),
        ],
        compiler_params=pltpu.CompilerParams(vmem_limit_bytes=VMEM),
        name=name,
    )(me, grads, root)


def unfold_below(pieces, me, root):
    tiles = root.shape[0] // TILE
    strip = TILE // len(pieces)
    blocks = below(tiles)
    for flip, parts in enumerate(pieces):
        other = jnp.bitwise_xor(me, flip)
        for k, (i, j) in enumerate(blocks):
            part, row = 0, k * strip
            while row >= parts[part].shape[0]:
                row -= parts[part].shape[0]
                part += 1
            at = pl.ds(pl.multiple_of(i * TILE + other * strip, strip), strip)
            root[at, block(j)] = parts[part][pl.ds(row, strip), :]
    for i, j in blocks:
        root[block(j), block(i)] = root[block(i), block(j)].T


def unfold_corners(folded, lines, root):
    row = lax.broadcasted_iota(jnp.int32, (TILE, TILE), 0)
    column = lax.broadcasted_iota(jnp.int32, (TILE, TILE), 1)
    lines = lines.astype(F32)
    for i in range(root.shape[0] // TILE):
        value = folded[block(i // 2), :].astype(F32)
        value = jnp.where(row >= column if i % 2 == 0 else row < column, value, value.T)
        if i % 2:
            line = jnp.broadcast_to(lines[i // 2 : i // 2 + 1, :], (TILE, TILE))
            value = jnp.where(row == column, line, value)
        root[block(i), block(i)] = value.astype(BF16)


def unfold(pieces, me, root, folded):
    tiles = root.shape[0] // TILE
    strip = TILE // len(pieces)
    unfold_below(pieces, me, root)
    base = len(below(tiles)) * strip
    for flip, parts in enumerate(pieces):
        other = jnp.bitwise_xor(me, flip)
        for pair in range(tiles // 2):
            part, row = 0, base + pair * strip
            while row >= parts[part].shape[0]:
                row -= parts[part].shape[0]
                part += 1
            at = pl.ds(pl.multiple_of(pair * TILE + other * strip, strip), strip)
            folded[at, :] = parts[part][pl.ds(row, strip), :]
    unfold_corners(folded, pieces[0][0][pl.ds(base + tiles // 2 * strip, EXTRA), :], root)


def dealt(refs, counts):
    lists = []
    for count in counts:
        lists.append(refs[:count])
        refs = refs[count:]
    return lists, refs


def columns_kernel(groups, held, split, me_ref, rows_ref, cols_ref, *refs):
    pieces, refs = dealt(refs, held)
    terms, refs = dealt(refs, split)
    outs, (left, folded, masked, mixed) = refs[:groups], refs[groups:]
    me = me_ref[0]
    width, strip = masked.shape
    unfold(pieces, me, left, folded)
    part = width // len(terms)
    column = lax.broadcasted_iota(jnp.int32, (part, strip), 1) + me * strip
    row = lax.broadcasted_iota(jnp.int32, (part, strip), 0)
    for index, used in enumerate(terms):
        total = functools.reduce(lambda a, b: a + b, [term[pl.ds(0, part), :].astype(F32) for term in used])
        keep = (row + index * part < rows_ref[0]) & (column < cols_ref[0])
        masked[pl.ds(index * part, part), :] = jnp.where(keep, total, 0.0).astype(BF16)
    mixed[...] = jnp.dot(left[...], masked[...], preferred_element_type=F32).astype(BF16)
    for flip, out in enumerate(outs):
        out[...] = mixed[strip_of(jnp.bitwise_xor(me, flip), strip), :]


def left_columns(me, rows_valid, cols_valid, pieces, terms, width):
    groups = len(pieces)
    strip = width // groups
    flat = [array for part in (*pieces, *terms) for array in part]
    return pl.pallas_call(
        functools.partial(columns_kernel, groups, [len(part) for part in pieces], [len(part) for part in terms]),
        in_specs=[SMEM_SPEC] * 3 + [VMEM_SPEC] * len(flat),
        out_specs=[VMEM_SPEC] * groups,
        out_shape=[pltpu.VMEM((strip, strip), BF16)] * groups,
        scratch_shapes=[
            pltpu.VMEM((width, width), BF16),
            pltpu.VMEM((width // 2, TILE), BF16),
            pltpu.VMEM((width, strip), BF16),
            pltpu.VMEM((width, strip), BF16),
        ],
        compiler_params=pltpu.CompilerParams(vmem_limit_bytes=VMEM),
        cost_estimate=cost(2 * strip * width**2, 4 * width**2),
        name="left_columns",
    )(me, rows_valid, cols_valid, *flat)


def whole_right_kernel(held, me_ref, corners_ref, *refs):
    pieces, (right,) = dealt(refs, held)
    unfold_below(pieces, me_ref[0], right)
    unfold_corners(corners_ref, corners_ref[pl.ds(right.shape[0] // 2, EXTRA), :], right)


def whole_right(me, corners, pieces, width):
    flat = [array for part in pieces for array in part]
    return pl.pallas_call(
        functools.partial(whole_right_kernel, [len(part) for part in pieces]),
        in_specs=[SMEM_SPEC] + [VMEM_SPEC] * (1 + len(flat)),
        out_specs=VMEM_SPEC,
        out_shape=pltpu.VMEM((width, width), BF16),
        compiler_params=pltpu.CompilerParams(vmem_limit_bytes=VMEM),
        cost_estimate=cost(width**2, 4 * width**2),
        name="whole_right",
    )(me, corners, *flat)


def rows_kernel(groups, me_ref, rows_ref, cols_ref, *refs):
    strips, (right, out, mixed) = refs[:groups], refs[groups:]
    me = me_ref[0]
    strip, width = mixed.shape
    if strip % 128 == 0:
        for flip, part in enumerate(strips):
            mixed[:, strip_of(jnp.bitwise_xor(me, flip), strip)] = part[...]
        value = jnp.dot(mixed[...], right[...], preferred_element_type=F32)
    else:
        value = 0.0
        for flip, part in enumerate(strips):
            rows = right[strip_of(jnp.bitwise_xor(me, flip), strip), :]
            value += jnp.dot(part[...], rows, preferred_element_type=F32)
    column = lax.broadcasted_iota(jnp.int32, (strip, width), 1)
    row = lax.broadcasted_iota(jnp.int32, (strip, width), 0) + me * strip
    out[0] = jnp.where((row < rows_ref[0]) & (column < cols_ref[0]), value, 0.0).astype(BF16)


def update_rows(me, rows_valid, cols_valid, strips, right):
    width = right.shape[0]
    groups, strip = len(strips), strips[0].shape[0]
    return pl.pallas_call(
        functools.partial(rows_kernel, groups),
        in_specs=[SMEM_SPEC] * 3 + [VMEM_SPEC] * (groups + 1),
        out_specs=VMEM_SPEC,
        out_shape=jax.ShapeDtypeStruct((1, strip, width), BF16),
        scratch_shapes=[pltpu.VMEM((strip, width), BF16)],
        compiler_params=pltpu.CompilerParams(vmem_limit_bytes=VMEM),
        cost_estimate=cost(2 * strip * width**2, 4 * width**2),
        name="update_rows",
    )(me, rows_valid, cols_valid, *strips, right)


def added(*terms):
    return functools.reduce(lambda a, b: a + b, [term.astype(F32) for term in terms])


def on_device(grads, left_roots, right_roots, rows_valid, cols_valid):
    groups = lax.axis_size("dp")
    me = lax.axis_index("dp").astype(jnp.int32).reshape(1)
    width = grads.shape[-1]
    half, strip = width // 2, width // groups
    plain = grads
    grads, left_roots, right_roots = (
        pltpu.with_memory_space_constraint(array, pltpu.HBM) for array in (grads, left_roots, right_roots)
    )

    if groups == 4:
        far_0, far_1, left = messages(
            me, grads, left_roots, groups, [[(3, 0)], [(3, 1)]], False, "sent_first"
        )
        far_0, far_1 = swapped(far_0, 1, "far_0"), swapped(far_1, 2, "far_1")
        left = shifted(left, "left")
        near_0, near_1, *kept, right, corners = messages(
            me,
            grads,
            right_roots,
            groups,
            [[(1, 0)], [(2, 1)], [(2, 0)], [(1, 1)], [(0, 0)], [(0, 1)]],
            True,
            "sent_later",
        )
        near_0, near_1 = swapped(near_0, 1, "near_0"), swapped(near_1, 2, "near_1")
        via_0, via_1 = added(kept[0], far_0).astype(BF16), added(kept[1], far_1).astype(BF16)
        right = shifted(after(right, left), "right")
        left = after(left, via_0, via_1, near_0, near_1)
        via_0, via_1 = swapped(via_0, 2, "via_0"), swapped(via_1, 1, "via_1")
        left_1, left_2 = swapped(left, 1, "left_1"), swapped(after(left, via_0), 2, "left_2")
        cut = (left.shape[0] - EXTRA) // 2
        left_3a, left_3b = left_1[:cut], left_2[cut : 2 * cut]
        corners = shifted(after(corners, right, left_3a, left_3b), "corners")
        left_3 = [swapped(left_3a, 2, "left_3a"), swapped(left_3b, 1, "left_3b")]
        mixed = left_columns(
            me,
            rows_valid,
            cols_valid,
            [[left], [left_1], [left_2], left_3],
            [[kept[2], near_0, via_0], [kept[3], near_1, via_1]],
            width,
        )
        right = after(right, via_0, via_1)
        right_1, right_2 = swapped(right, 1, "right_1"), swapped(right, 2, "right_2")
        right_3 = [swapped(right_1, 2, "right_3")]
        rights = [[right], [right_1], [right_2], right_3]
    else:
        (left,) = messages(me, grads, left_roots, groups, [], False, "sent_first")
        right, corners = messages(me, grads, right_roots, groups, [], True, "sent_later")
        left, right, corners = shifted(left, "left"), shifted(right, "right"), shifted(corners, "corners")
        parts = [
            lax.dynamic_slice_in_dim(plain[0, 0], jnp.bitwise_xor(me[0], flip) * strip, strip, 1)
            for flip in range(groups)
        ]
        terms = [parts[:1] + [swapped(parts[flip], flip, "grad") for flip in range(1, groups)]]
        lefts = [[left]] + [[swapped(left, flip, "left")] for flip in range(1, groups)]
        mixed = left_columns(me, rows_valid, cols_valid, lefts, terms, width)
        rights = [[right]] + [[swapped(right, flip, "right")] for flip in range(1, groups)]
    whole = whole_right(me, corners, rights, width)
    strips = [mixed[0]] + [swapped(mixed[flip], flip, "strip_%d" % flip) for flip in range(1, groups)]
    return update_rows(me, rows_valid, cols_valid, strips, whole)


def solution(mesh):
    placed = (
        P("dp", "shard", None, None),
        P("shard", None, None),
        P("shard", None, None),
        P("shard"),
        P("shard"),
    )
    return jax.shard_map(
        on_device, mesh=mesh, in_specs=placed, out_specs=P("shard", "dp", None), check_vma=False
    )
```

```python
import functools

import jax
import jax.numpy as jnp
from jax import lax
from jax.experimental import pallas as pl
from jax.experimental.pallas import tpu as pltpu
from jax.sharding import PartitionSpec as P

TILE = 256
EXTRA = 16
VMEM = 24 * 1024 * 1024
SMEM_SPEC = pl.BlockSpec(memory_space=pltpu.SMEM)
VMEM_SPEC = pl.BlockSpec(memory_space=pltpu.VMEM)
HBM_SPEC = pl.BlockSpec(memory_space=pltpu.HBM)
BF16 = jnp.bfloat16
F32 = jnp.float32


def shifted(value, name):
    count = lax.axis_size("shard")
    with jax.named_scope(name):
        return lax.ppermute(value, "shard", [(source, (source + count // 2) % count) for source in range(count)])


def swapped(value, flip, name):
    count = lax.axis_size("dp")
    with jax.named_scope(name):
        return lax.ppermute(value, "dp", [(source, source ^ flip) for source in range(count)])


def after(value, *earlier):
    return lax.optimization_barrier((value, *earlier))[0]


def block(index):
    return pl.ds(index * TILE, TILE)


def strip_of(index, size):
    return pl.ds(pl.multiple_of(index * size, size), size)


def cost(flops, bytes_accessed):
    return pl.CostEstimate(flops=flops, bytes_accessed=bytes_accessed, transcendentals=0)


def below(tiles):
    return [(i, j) for j in range(tiles) for i in range(j + 1, tiles)]


def pick_copies(wanted, me, grad_ref, outs, sems):
    copies = []
    for parts, out in zip(wanted, outs):
        half, strip = out.shape[0] // len(parts), out.shape[1]
        for part, (flip, h) in enumerate(parts):
            source = grad_ref.at[0, 0, pl.ds(h * half, half), strip_of(jnp.bitwise_xor(me, flip), strip)]
            copies.append(
                pltpu.make_async_copy(source, out.at[pl.ds(part * half, half), :], sems.at[len(copies)])
            )
    return copies


def picked_shapes(wanted, width, groups):
    return [pltpu.VMEM((len(parts) * (width // 2), width // groups), BF16) for parts in wanted]


def strip_copies(me, root_ref, strip, out, sems):
    return [
        pltpu.make_async_copy(
            root_ref.at[0, pl.ds(pl.multiple_of(i * TILE + me * strip, strip), strip), block(j)],
            out.at[pl.ds(k * strip, strip), :],
            sems.at[k],
        )
        for k, (i, j) in enumerate(below(root_ref.shape[1] // TILE))
    ]


def corner_copies(root_ref, corners, sems):
    return [
        pltpu.make_async_copy(root_ref.at[0, block(i), block(i)], corners.at[i], sems.at[i])
        for i in range(corners.shape[0])
    ]


def fold_corners(corners, start, strip, out, base):
    tiles = corners.shape[0]
    row = lax.broadcasted_iota(jnp.int32, (strip, TILE), 0) + start
    column = lax.broadcasted_iota(jnp.int32, (strip, TILE), 1)
    on_diag = lax.broadcasted_iota(jnp.int32, (TILE, TILE), 0) == lax.broadcasted_iota(jnp.int32, (TILE, TILE), 1)
    rows = pl.ds(pl.multiple_of(start, strip), strip) if strip < TILE else pl.ds(0, TILE)
    lines = []
    for pair in range(tiles // 2):
        even, odd = 2 * pair, 2 * pair + 1
        out[pl.ds(base + pair * strip, strip), :] = jnp.where(
            row >= column, corners[even, rows, :], corners[odd, rows, :]
        )
        lines.append(jnp.sum(jnp.where(on_diag, corners[odd].astype(F32), 0.0), axis=0, keepdims=True))
    lines.append(jnp.zeros((EXTRA - len(lines), TILE), F32))
    out[pl.ds(base + tiles // 2 * strip, EXTRA), :] = jnp.concatenate(lines, axis=0).astype(BF16)


def messages_kernel(wanted, quarter, me_ref, grad_ref, root_ref, *refs):
    outs, (*folded, corners, pick_sems, strip_sems, corner_sems) = refs[: len(wanted)], refs[len(wanted) :]
    me = me_ref[0]
    tiles = corners.shape[0]
    low = len(below(tiles))
    strip = quarter
    strips = strip_copies(me, root_ref, strip, folded[0], strip_sems)
    cornered = corner_copies(root_ref, corners, corner_sems)
    copies = pick_copies(wanted, me, grad_ref, outs, pick_sems)
    for copy in cornered + strips + copies:
        copy.start()
    for copy in cornered:
        copy.wait()
    if len(folded) == 1:
        fold_corners(corners, me * strip, strip, folded[0], low * strip)
    else:
        fold_corners(corners, 0, TILE, folded[1], 0)
    for copy in strips + copies:
        copy.wait()


def messages(me, grads, root, groups, wanted, apart, name):
    width = grads.shape[-1]
    strip, tiles = TILE // groups, width // TILE
    count = sum(len(parts) for parts in wanted)
    low = len(below(tiles)) * strip
    if apart:
        rows = [low, tiles // 2 * TILE + EXTRA]
    else:
        rows = [low + tiles // 2 * strip + EXTRA]
    return pl.pallas_call(
        functools.partial(messages_kernel, wanted, strip),
        in_specs=[SMEM_SPEC] + [HBM_SPEC] * 2,
        out_specs=[VMEM_SPEC] * (len(wanted) + len(rows)),
        out_shape=picked_shapes(wanted, width, groups) + [pltpu.VMEM((number, TILE), BF16) for number in rows],
        scratch_shapes=[
            pltpu.VMEM((tiles, TILE, TILE), BF16),
            pltpu.SemaphoreType.DMA((max(count, 1),)),
            pltpu.SemaphoreType.DMA((len(below(tiles)),)),
            pltpu.SemaphoreType.DMA((tiles,)),
        ],
        compiler_params=pltpu.CompilerParams(vmem_limit_bytes=VMEM),
        name=name,
    )(me, grads, root)


def unfold_below(pieces, me, root):
    tiles = root.shape[0] // TILE
    strip = TILE // len(pieces)
    blocks = below(tiles)
    for flip, parts in enumerate(pieces):
        other = jnp.bitwise_xor(me, flip)
        for k, (i, j) in enumerate(blocks):
            part, row = 0, k * strip
            while row >= parts[part].shape[0]:
                row -= parts[part].shape[0]
                part += 1
            at = pl.ds(pl.multiple_of(i * TILE + other * strip, strip), strip)
            root[at, block(j)] = parts[part][pl.ds(row, strip), :]
    for i, j in blocks:
        root[block(j), block(i)] = root[block(i), block(j)].T


def unfold_corners(folded, lines, root):
    row = lax.broadcasted_iota(jnp.int32, (TILE, TILE), 0)
    column = lax.broadcasted_iota(jnp.int32, (TILE, TILE), 1)
    lines = lines.astype(F32)
    for i in range(root.shape[0] // TILE):
        value = folded[block(i // 2), :].astype(F32)
        value = jnp.where(row >= column if i % 2 == 0 else row < column, value, value.T)
        if i % 2:
            line = jnp.broadcast_to(lines[i // 2 : i // 2 + 1, :], (TILE, TILE))
            value = jnp.where(row == column, line, value)
        root[block(i), block(i)] = value.astype(BF16)


def unfold(pieces, me, root, folded):
    tiles = root.shape[0] // TILE
    strip = TILE // len(pieces)
    unfold_below(pieces, me, root)
    base = len(below(tiles)) * strip
    for flip, parts in enumerate(pieces):
        other = jnp.bitwise_xor(me, flip)
        for pair in range(tiles // 2):
            part, row = 0, base + pair * strip
            while row >= parts[part].shape[0]:
                row -= parts[part].shape[0]
                part += 1
            at = pl.ds(pl.multiple_of(pair * TILE + other * strip, strip), strip)
            folded[at, :] = parts[part][pl.ds(row, strip), :]
    unfold_corners(folded, pieces[0][0][pl.ds(base + tiles // 2 * strip, EXTRA), :], root)


def dealt(refs, counts):
    lists = []
    for count in counts:
        lists.append(refs[:count])
        refs = refs[count:]
    return lists, refs


def columns_kernel(groups, held, split, me_ref, rows_ref, cols_ref, *refs):
    pieces, refs = dealt(refs, held)
    terms, refs = dealt(refs, split)
    outs, (left, folded, masked, mixed) = refs[:groups], refs[groups:]
    me = me_ref[0]
    width, strip = masked.shape
    unfold(pieces, me, left, folded)
    part = width // len(terms)
    column = lax.broadcasted_iota(jnp.int32, (part, strip), 1) + me * strip
    row = lax.broadcasted_iota(jnp.int32, (part, strip), 0)
    for index, used in enumerate(terms):
        total = functools.reduce(lambda a, b: a + b, [term[pl.ds(0, part), :].astype(F32) for term in used])
        keep = (row + index * part < rows_ref[0]) & (column < cols_ref[0])
        masked[pl.ds(index * part, part), :] = jnp.where(keep, total, 0.0).astype(BF16)
    mixed[...] = jnp.dot(left[...], masked[...], preferred_element_type=F32).astype(BF16)
    for flip, out in enumerate(outs):
        out[...] = mixed[strip_of(jnp.bitwise_xor(me, flip), strip), :]


def left_columns(me, rows_valid, cols_valid, pieces, terms, width):
    groups = len(pieces)
    strip = width // groups
    flat = [array for part in (*pieces, *terms) for array in part]
    return pl.pallas_call(
        functools.partial(columns_kernel, groups, [len(part) for part in pieces], [len(part) for part in terms]),
        in_specs=[SMEM_SPEC] * 3 + [VMEM_SPEC] * len(flat),
        out_specs=[VMEM_SPEC] * groups,
        out_shape=[pltpu.VMEM((strip, strip), BF16)] * groups,
        scratch_shapes=[
            pltpu.VMEM((width, width), BF16),
            pltpu.VMEM((width // 2, TILE), BF16),
            pltpu.VMEM((width, strip), BF16),
            pltpu.VMEM((width, strip), BF16),
        ],
        compiler_params=pltpu.CompilerParams(vmem_limit_bytes=VMEM),
        cost_estimate=cost(2 * strip * width**2, 4 * width**2),
        name="left_columns",
    )(me, rows_valid, cols_valid, *flat)


def whole_right_kernel(held, me_ref, corners_ref, *refs):
    pieces, (right,) = dealt(refs, held)
    unfold_below(pieces, me_ref[0], right)
    unfold_corners(corners_ref, corners_ref[pl.ds(right.shape[0] // 2, EXTRA), :], right)


def whole_right(me, corners, pieces, width):
    flat = [array for part in pieces for array in part]
    return pl.pallas_call(
        functools.partial(whole_right_kernel, [len(part) for part in pieces]),
        in_specs=[SMEM_SPEC] + [VMEM_SPEC] * (1 + len(flat)),
        out_specs=VMEM_SPEC,
        out_shape=pltpu.VMEM((width, width), BF16),
        compiler_params=pltpu.CompilerParams(vmem_limit_bytes=VMEM),
        cost_estimate=cost(width**2, 4 * width**2),
        name="whole_right",
    )(me, corners, *flat)


def rows_kernel(groups, me_ref, rows_ref, cols_ref, *refs):
    strips, (right, out, mixed) = refs[:groups], refs[groups:]
    me = me_ref[0]
    strip, width = mixed.shape
    if strip % 128 == 0:
        for flip, part in enumerate(strips):
            mixed[:, strip_of(jnp.bitwise_xor(me, flip), strip)] = part[...]
        value = jnp.dot(mixed[...], right[...], preferred_element_type=F32)
    else:
        value = 0.0
        for flip, part in enumerate(strips):
            rows = right[strip_of(jnp.bitwise_xor(me, flip), strip), :]
            value += jnp.dot(part[...], rows, preferred_element_type=F32)
    column = lax.broadcasted_iota(jnp.int32, (strip, width), 1)
    row = lax.broadcasted_iota(jnp.int32, (strip, width), 0) + me * strip
    out[0] = jnp.where((row < rows_ref[0]) & (column < cols_ref[0]), value, 0.0).astype(BF16)


def update_rows(me, rows_valid, cols_valid, strips, right):
    width = right.shape[0]
    groups, strip = len(strips), strips[0].shape[0]
    return pl.pallas_call(
        functools.partial(rows_kernel, groups),
        in_specs=[SMEM_SPEC] * 3 + [VMEM_SPEC] * (groups + 1),
        out_specs=VMEM_SPEC,
        out_shape=jax.ShapeDtypeStruct((1, strip, width), BF16),
        scratch_shapes=[pltpu.VMEM((strip, width), BF16)],
        compiler_params=pltpu.CompilerParams(vmem_limit_bytes=VMEM),
        cost_estimate=cost(2 * strip * width**2, 4 * width**2),
        name="update_rows",
    )(me, rows_valid, cols_valid, *strips, right)


def added(*terms):
    return functools.reduce(lambda a, b: a + b, [term.astype(F32) for term in terms])


def on_device(grads, left_roots, right_roots, rows_valid, cols_valid):
    groups = lax.axis_size("dp")
    me = lax.axis_index("dp").astype(jnp.int32).reshape(1)
    width = grads.shape[-1]
    half, strip = width // 2, width // groups
    plain = grads
    grads, left_roots, right_roots = (
        pltpu.with_memory_space_constraint(array, pltpu.HBM) for array in (grads, left_roots, right_roots)
    )

    if groups == 4:
        far_0, far_1, left = messages(
            me, grads, left_roots, groups, [[(3, 0)], [(3, 1)]], False, "sent_first"
        )
        far_0, far_1 = swapped(far_0, 1, "far_0"), swapped(far_1, 2, "far_1")
        left = shifted(left, "left")
        near_0, near_1, *kept, right, corners = messages(
            me,
            grads,
            right_roots,
            groups,
            [[(1, 0)], [(2, 1)], [(2, 0)], [(1, 1)], [(0, 0)], [(0, 1)]],
            True,
            "sent_later",
        )
        near_0, near_1 = swapped(near_0, 1, "near_0"), swapped(near_1, 2, "near_1")
        via_0, via_1 = added(kept[0], far_0).astype(BF16), added(kept[1], far_1).astype(BF16)
        right = shifted(after(right, left), "right")
        left = after(left, via_0, via_1, near_0, near_1)
        via_0, via_1 = swapped(via_0, 2, "via_0"), swapped(via_1, 1, "via_1")
        left_1, left_2 = swapped(left, 1, "left_1"), swapped(after(left, via_0), 2, "left_2")
        cut = (left.shape[0] - EXTRA) // 2
        left_3a, left_3b = left_1[:cut], left_2[cut : 2 * cut]
        corners = shifted(after(corners, right, left_3a, left_3b), "corners")
        left_3 = [swapped(left_3a, 2, "left_3a"), swapped(left_3b, 1, "left_3b")]
        mixed = left_columns(
            me,
            rows_valid,
            cols_valid,
            [[left], [left_1], [left_2], left_3],
            [[kept[2], near_0, via_0], [kept[3], near_1, via_1]],
            width,
        )
        right = after(right, via_0, via_1)
        right_1, right_2 = swapped(right, 1, "right_1"), swapped(right, 2, "right_2")
        cut = TILE
        right_3 = [swapped(right_1[:cut], 2, "right_3a"), swapped(right_2[cut:], 1, "right_3b")]
        rights = [[right], [right_1], [right_2], right_3]
    else:
        (left,) = messages(me, grads, left_roots, groups, [], False, "sent_first")
        right, corners = messages(me, grads, right_roots, groups, [], True, "sent_later")
        left, right, corners = shifted(left, "left"), shifted(right, "right"), shifted(corners, "corners")
        parts = [
            lax.dynamic_slice_in_dim(plain[0, 0], jnp.bitwise_xor(me[0], flip) * strip, strip, 1)
            for flip in range(groups)
        ]
        terms = [parts[:1] + [swapped(parts[flip], flip, "grad") for flip in range(1, groups)]]
        lefts = [[left]] + [[swapped(left, flip, "left")] for flip in range(1, groups)]
        mixed = left_columns(me, rows_valid, cols_valid, lefts, terms, width)
        rights = [[right]] + [[swapped(right, flip, "right")] for flip in range(1, groups)]
    whole = whole_right(me, corners, rights, width)
    strips = [mixed[0]] + [swapped(mixed[flip], flip, "strip_%d" % flip) for flip in range(1, groups)]
    return update_rows(me, rows_valid, cols_valid, strips, whole)


def solution(mesh):
    placed = (
        P("dp", "shard", None, None),
        P("shard", None, None),
        P("shard", None, None),
        P("shard"),
        P("shard"),
    )
    return jax.shard_map(
        on_device, mesh=mesh, in_specs=placed, out_specs=P("shard", "dp", None), check_vma=False
    )
```

```python
import functools

import jax
import jax.numpy as jnp
from jax import lax
from jax.experimental import pallas as pl
from jax.experimental.pallas import tpu as pltpu
from jax.sharding import PartitionSpec as P

TILE = 256
EXTRA = 16
VMEM = 24 * 1024 * 1024
SMEM_SPEC = pl.BlockSpec(memory_space=pltpu.SMEM)
VMEM_SPEC = pl.BlockSpec(memory_space=pltpu.VMEM)
HBM_SPEC = pl.BlockSpec(memory_space=pltpu.HBM)
BF16 = jnp.bfloat16
F32 = jnp.float32


def shifted(value, name):
    count = lax.axis_size("shard")
    with jax.named_scope(name):
        return lax.ppermute(value, "shard", [(source, (source + count // 2) % count) for source in range(count)])


def swapped(value, flip, name):
    count = lax.axis_size("dp")
    with jax.named_scope(name):
        return lax.ppermute(value, "dp", [(source, source ^ flip) for source in range(count)])


def after(value, *earlier):
    return lax.optimization_barrier((value, *earlier))[0]


def block(index):
    return pl.ds(index * TILE, TILE)


def strip_of(index, size):
    return pl.ds(pl.multiple_of(index * size, size), size)


def cost(flops, bytes_accessed):
    return pl.CostEstimate(flops=flops, bytes_accessed=bytes_accessed, transcendentals=0)


def below(tiles):
    return [(i, j) for j in range(tiles) for i in range(j + 1, tiles)]


def pick_copies(wanted, me, grad_ref, outs, sems):
    copies = []
    for parts, out in zip(wanted, outs):
        half, strip = out.shape[0] // len(parts), out.shape[1]
        for part, (flip, h) in enumerate(parts):
            source = grad_ref.at[0, 0, pl.ds(h * half, half), strip_of(jnp.bitwise_xor(me, flip), strip)]
            copies.append(
                pltpu.make_async_copy(source, out.at[pl.ds(part * half, half), :], sems.at[len(copies)])
            )
    return copies


def picked_shapes(wanted, width, groups):
    return [pltpu.VMEM((len(parts) * (width // 2), width // groups), BF16) for parts in wanted]


def strip_copies(me, root_ref, strip, out, sems):
    return [
        pltpu.make_async_copy(
            root_ref.at[0, pl.ds(pl.multiple_of(i * TILE + me * strip, strip), strip), block(j)],
            out.at[pl.ds(k * strip, strip), :],
            sems.at[k],
        )
        for k, (i, j) in enumerate(below(root_ref.shape[1] // TILE))
    ]


def corner_copies(me, strip, root_ref, corners, sems):
    copies = []
    for i in range(corners.shape[0]):
        rows, size = (me * strip, strip) if i % 2 == 0 else (0, TILE)
        if size < TILE:
            source = root_ref.at[0, pl.ds(pl.multiple_of(i * TILE + rows, size), size), block(i)]
            target = corners.at[i, pl.ds(pl.multiple_of(rows, size), size), :]
        else:
            source, target = root_ref.at[0, block(i), block(i)], corners.at[i]
        copies.append(pltpu.make_async_copy(source, target, sems.at[i]))
    return copies


def fold_corners(corners, start, strip, out, base):
    tiles = corners.shape[0]
    row = lax.broadcasted_iota(jnp.int32, (strip, TILE), 0) + start
    column = lax.broadcasted_iota(jnp.int32, (strip, TILE), 1)
    on_diag = lax.broadcasted_iota(jnp.int32, (TILE, TILE), 0) == lax.broadcasted_iota(jnp.int32, (TILE, TILE), 1)
    rows = pl.ds(pl.multiple_of(start, strip), strip) if strip < TILE else pl.ds(0, TILE)
    lines = []
    for pair in range(tiles // 2):
        even, odd = 2 * pair, 2 * pair + 1
        out[pl.ds(base + pair * strip, strip), :] = jnp.where(
            row >= column, corners[even, rows, :], corners[odd, rows, :]
        )
        lines.append(jnp.sum(jnp.where(on_diag, corners[odd].astype(F32), 0.0), axis=0, keepdims=True))
    lines.append(jnp.zeros((EXTRA - len(lines), TILE), F32))
    out[pl.ds(base + tiles // 2 * strip, EXTRA), :] = jnp.concatenate(lines, axis=0).astype(BF16)


def messages_kernel(wanted, quarter, me_ref, grad_ref, root_ref, *refs):
    outs, (*folded, corners, pick_sems, strip_sems, corner_sems) = refs[: len(wanted)], refs[len(wanted) :]
    me = me_ref[0]
    tiles = corners.shape[0]
    low = len(below(tiles))
    strip = quarter
    strips = strip_copies(me, root_ref, strip, folded[0], strip_sems)
    cornered = corner_copies(me, strip if len(folded) == 1 else TILE, root_ref, corners, corner_sems)
    copies = pick_copies(wanted, me, grad_ref, outs, pick_sems)
    for copy in cornered + strips + copies:
        copy.start()
    for copy in cornered:
        copy.wait()
    if len(folded) == 1:
        fold_corners(corners, me * strip, strip, folded[0], low * strip)
    else:
        fold_corners(corners, 0, TILE, folded[1], 0)
    for copy in strips + copies:
        copy.wait()


def messages(me, grads, root, groups, wanted, apart, name):
    width = grads.shape[-1]
    strip, tiles = TILE // groups, width // TILE
    count = sum(len(parts) for parts in wanted)
    low = len(below(tiles)) * strip
    if apart:
        rows = [low, tiles // 2 * TILE + EXTRA]
    else:
        rows = [low + tiles // 2 * strip + EXTRA]
    return pl.pallas_call(
        functools.partial(messages_kernel, wanted, strip),
        in_specs=[SMEM_SPEC] + [HBM_SPEC] * 2,
        out_specs=[VMEM_SPEC] * (len(wanted) + len(rows)),
        out_shape=picked_shapes(wanted, width, groups) + [pltpu.VMEM((number, TILE), BF16) for number in rows],
        scratch_shapes=[
            pltpu.VMEM((tiles, TILE, TILE), BF16),
            pltpu.SemaphoreType.DMA((max(count, 1),)),
            pltpu.SemaphoreType.DMA((len(below(tiles)),)),
            pltpu.SemaphoreType.DMA((tiles,)),
        ],
        compiler_params=pltpu.CompilerParams(vmem_limit_bytes=VMEM),
        name=name,
    )(me, grads, root)


def unfold_below(pieces, me, root):
    tiles = root.shape[0] // TILE
    strip = TILE // len(pieces)
    blocks = below(tiles)
    for flip, parts in enumerate(pieces):
        other = jnp.bitwise_xor(me, flip)
        for k, (i, j) in enumerate(blocks):
            part, row = 0, k * strip
            while row >= parts[part].shape[0]:
                row -= parts[part].shape[0]
                part += 1
            at = pl.ds(pl.multiple_of(i * TILE + other * strip, strip), strip)
            root[at, block(j)] = parts[part][pl.ds(row, strip), :]
    for i, j in blocks:
        root[block(j), block(i)] = root[block(i), block(j)].T


def unfold_corners(folded, lines, root):
    row = lax.broadcasted_iota(jnp.int32, (TILE, TILE), 0)
    column = lax.broadcasted_iota(jnp.int32, (TILE, TILE), 1)
    lines = lines.astype(F32)
    for i in range(root.shape[0] // TILE):
        value = folded[block(i // 2), :].astype(F32)
        value = jnp.where(row >= column if i % 2 == 0 else row < column, value, value.T)
        if i % 2:
            line = jnp.broadcast_to(lines[i // 2 : i // 2 + 1, :], (TILE, TILE))
            value = jnp.where(row == column, line, value)
        root[block(i), block(i)] = value.astype(BF16)


def unfold(pieces, me, root, folded):
    tiles = root.shape[0] // TILE
    strip = TILE // len(pieces)
    unfold_below(pieces, me, root)
    base = len(below(tiles)) * strip
    for flip, parts in enumerate(pieces):
        other = jnp.bitwise_xor(me, flip)
        for pair in range(tiles // 2):
            part, row = 0, base + pair * strip
            while row >= parts[part].shape[0]:
                row -= parts[part].shape[0]
                part += 1
            at = pl.ds(pl.multiple_of(pair * TILE + other * strip, strip), strip)
            folded[at, :] = parts[part][pl.ds(row, strip), :]
    unfold_corners(folded, pieces[0][0][pl.ds(base + tiles // 2 * strip, EXTRA), :], root)


def dealt(refs, counts):
    lists = []
    for count in counts:
        lists.append(refs[:count])
        refs = refs[count:]
    return lists, refs


def columns_kernel(groups, held, split, me_ref, rows_ref, cols_ref, *refs):
    pieces, refs = dealt(refs, held)
    terms, refs = dealt(refs, split)
    outs, (left, folded, masked, mixed) = refs[:groups], refs[groups:]
    me = me_ref[0]
    width, strip = masked.shape
    unfold(pieces, me, left, folded)
    part = width // len(terms)
    column = lax.broadcasted_iota(jnp.int32, (part, strip), 1) + me * strip
    row = lax.broadcasted_iota(jnp.int32, (part, strip), 0)
    for index, used in enumerate(terms):
        total = functools.reduce(lambda a, b: a + b, [term[pl.ds(0, part), :].astype(F32) for term in used])
        keep = (row + index * part < rows_ref[0]) & (column < cols_ref[0])
        masked[pl.ds(index * part, part), :] = jnp.where(keep, total, 0.0).astype(BF16)
    mixed[...] = jnp.dot(left[...], masked[...], preferred_element_type=F32).astype(BF16)
    for flip, out in enumerate(outs):
        out[...] = mixed[strip_of(jnp.bitwise_xor(me, flip), strip), :]


def left_columns(me, rows_valid, cols_valid, pieces, terms, width):
    groups = len(pieces)
    strip = width // groups
    flat = [array for part in (*pieces, *terms) for array in part]
    return pl.pallas_call(
        functools.partial(columns_kernel, groups, [len(part) for part in pieces], [len(part) for part in terms]),
        in_specs=[SMEM_SPEC] * 3 + [VMEM_SPEC] * len(flat),
        out_specs=[VMEM_SPEC] * groups,
        out_shape=[pltpu.VMEM((strip, strip), BF16)] * groups,
        scratch_shapes=[
            pltpu.VMEM((width, width), BF16),
            pltpu.VMEM((width // 2, TILE), BF16),
            pltpu.VMEM((width, strip), BF16),
            pltpu.VMEM((width, strip), BF16),
        ],
        compiler_params=pltpu.CompilerParams(vmem_limit_bytes=VMEM),
        cost_estimate=cost(2 * strip * width**2, 4 * width**2),
        name="left_columns",
    )(me, rows_valid, cols_valid, *flat)


def whole_right_kernel(held, me_ref, corners_ref, *refs):
    pieces, (right,) = dealt(refs, held)
    unfold_below(pieces, me_ref[0], right)
    unfold_corners(corners_ref, corners_ref[pl.ds(right.shape[0] // 2, EXTRA), :], right)


def whole_right(me, corners, pieces, width):
    flat = [array for part in pieces for array in part]
    return pl.pallas_call(
        functools.partial(whole_right_kernel, [len(part) for part in pieces]),
        in_specs=[SMEM_SPEC] + [VMEM_SPEC] * (1 + len(flat)),
        out_specs=VMEM_SPEC,
        out_shape=pltpu.VMEM((width, width), BF16),
        compiler_params=pltpu.CompilerParams(vmem_limit_bytes=VMEM),
        cost_estimate=cost(width**2, 4 * width**2),
        name="whole_right",
    )(me, corners, *flat)


def rows_kernel(groups, me_ref, rows_ref, cols_ref, *refs):
    strips, (right, out, mixed) = refs[:groups], refs[groups:]
    me = me_ref[0]
    strip, width = mixed.shape
    if strip % 128 == 0:
        for flip, part in enumerate(strips):
            mixed[:, strip_of(jnp.bitwise_xor(me, flip), strip)] = part[...]
        value = jnp.dot(mixed[...], right[...], preferred_element_type=F32)
    else:
        value = 0.0
        for flip, part in enumerate(strips):
            rows = right[strip_of(jnp.bitwise_xor(me, flip), strip), :]
            value += jnp.dot(part[...], rows, preferred_element_type=F32)
    column = lax.broadcasted_iota(jnp.int32, (strip, width), 1)
    row = lax.broadcasted_iota(jnp.int32, (strip, width), 0) + me * strip
    out[0] = jnp.where((row < rows_ref[0]) & (column < cols_ref[0]), value, 0.0).astype(BF16)


def update_rows(me, rows_valid, cols_valid, strips, right):
    width = right.shape[0]
    groups, strip = len(strips), strips[0].shape[0]
    return pl.pallas_call(
        functools.partial(rows_kernel, groups),
        in_specs=[SMEM_SPEC] * 3 + [VMEM_SPEC] * (groups + 1),
        out_specs=VMEM_SPEC,
        out_shape=jax.ShapeDtypeStruct((1, strip, width), BF16),
        scratch_shapes=[pltpu.VMEM((strip, width), BF16)],
        compiler_params=pltpu.CompilerParams(vmem_limit_bytes=VMEM),
        cost_estimate=cost(2 * strip * width**2, 4 * width**2),
        name="update_rows",
    )(me, rows_valid, cols_valid, *strips, right)


def added(*terms):
    return functools.reduce(lambda a, b: a + b, [term.astype(F32) for term in terms])


def on_device(grads, left_roots, right_roots, rows_valid, cols_valid):
    groups = lax.axis_size("dp")
    me = lax.axis_index("dp").astype(jnp.int32).reshape(1)
    width = grads.shape[-1]
    half, strip = width // 2, width // groups
    plain = grads
    grads, left_roots, right_roots = (
        pltpu.with_memory_space_constraint(array, pltpu.HBM) for array in (grads, left_roots, right_roots)
    )

    if groups == 4:
        far_0, far_1, left = messages(
            me, grads, left_roots, groups, [[(3, 0)], [(3, 1)]], False, "sent_first"
        )
        far_0, far_1 = swapped(far_0, 1, "far_0"), swapped(far_1, 2, "far_1")
        left = shifted(left, "left")
        near_0, near_1, *kept, right, corners = messages(
            me,
            grads,
            right_roots,
            groups,
            [[(1, 0)], [(2, 1)], [(2, 0)], [(1, 1)], [(0, 0)], [(0, 1)]],
            True,
            "sent_later",
        )
        near_0, near_1 = swapped(near_0, 1, "near_0"), swapped(near_1, 2, "near_1")
        via_0, via_1 = added(kept[0], far_0).astype(BF16), added(kept[1], far_1).astype(BF16)
        right = shifted(after(right, left), "right")
        left = after(left, via_0, via_1, near_0, near_1)
        via_0, via_1 = swapped(via_0, 2, "via_0"), swapped(via_1, 1, "via_1")
        left_1, left_2 = swapped(left, 1, "left_1"), swapped(after(left, via_0), 2, "left_2")
        cut = (left.shape[0] - EXTRA) // 2
        left_3a, left_3b = left_1[:cut], left_2[cut : 2 * cut]
        corners = shifted(after(corners, right, left_3a, left_3b), "corners")
        left_3 = [swapped(left_3a, 2, "left_3a"), swapped(left_3b, 1, "left_3b")]
        mixed = left_columns(
            me,
            rows_valid,
            cols_valid,
            [[left], [left_1], [left_2], left_3],
            [[kept[2], near_0, via_0], [kept[3], near_1, via_1]],
            width,
        )
        right = after(right, via_0, via_1)
        right_1, right_2 = swapped(right, 1, "right_1"), swapped(right, 2, "right_2")
        cut = TILE
        right_3 = [swapped(right_1[:cut], 2, "right_3a"), swapped(right_2[cut:], 1, "right_3b")]
        rights = [[right], [right_1], [right_2], right_3]
    else:
        (left,) = messages(me, grads, left_roots, groups, [], False, "sent_first")
        right, corners = messages(me, grads, right_roots, groups, [], True, "sent_later")
        left, right, corners = shifted(left, "left"), shifted(right, "right"), shifted(corners, "corners")
        parts = [
            lax.dynamic_slice_in_dim(plain[0, 0], jnp.bitwise_xor(me[0], flip) * strip, strip, 1)
            for flip in range(groups)
        ]
        terms = [parts[:1] + [swapped(parts[flip], flip, "grad") for flip in range(1, groups)]]
        lefts = [[left]] + [[swapped(left, flip, "left")] for flip in range(1, groups)]
        mixed = left_columns(me, rows_valid, cols_valid, lefts, terms, width)
        rights = [[right]] + [[swapped(right, flip, "right")] for flip in range(1, groups)]
    whole = whole_right(me, corners, rights, width)
    strips = [mixed[0]] + [swapped(mixed[flip], flip, "strip_%d" % flip) for flip in range(1, groups)]
    return update_rows(me, rows_valid, cols_valid, strips, whole)


def solution(mesh):
    placed = (
        P("dp", "shard", None, None),
        P("shard", None, None),
        P("shard", None, None),
        P("shard"),
        P("shard"),
    )
    return jax.shard_map(
        on_device, mesh=mesh, in_specs=placed, out_specs=P("shard", "dp", None), check_vma=False
    )
```
